32 devices in a mesh: lat: 4 (over x, core), lon: 8 (over z, y).
Axes of the slice: x: 2, y: 2, z: 4, core: 2. Of those that a mesh axis runs over, the one named last changes fastest.
Arguments:
- fine_query: bfloat16 [96, 256, 512], P('lat', 'lon'), may hold values from -6 to 6
- fine_keyval: bfloat16 [96, 256, 1024], P('lat', 'lon'), may hold values from -6 to 6
- coarse_query: bfloat16 [24, 64, 512], P('lat', 'lon'), may hold values from -6 to 6
- coarse_keyval: bfloat16 [24, 64, 1024], P('lat', 'lon'), may hold values from -6 to 6
- out_weight: bfloat16 [512, 512], replicated, may hold values from -0.25 to 0.25
Outputs:
- output: bfloat16 [96, 256, 512], P('lat', 'lon')
The draws below stay inside these ranges and needn't reach their ends.
All inputs are finite; a program needn't handle non-finite values.
Results may differ from the reference program's by a relative error of at most 0.0061.
Values may be sent and summed in bfloat16 or wider, within the bound.
No kernel may reach another device: no remote copies, remote signals or barrier semaphores. Data moves between devices by JAX's collectives and lax.ppermute only.
A program may use at most 64 MiB of HBM per device.

```python
import math
import jax
import jax.numpy as jnp
from jax import lax

HEADS = 8
D = 512
RADIUS = 6
FH = 24
FW = 32
CH = 6
CW = 8
NLAT = 96
NLON = 256
CLAT = 24
CLON = 64
N_LAT = 4
N_LON = 8


def rough_field(key, shape, spread):
    values = jax.random.normal(key, shape) * spread
    return jnp.clip(values.astype(jnp.float32), -6.0, 6.0)


def draw_fine_query(key, part):
    values = rough_field(jax.random.fold_in(key, 1), (NLAT, NLON, D), 1.4)
    return values.astype(jnp.bfloat16)


def draw_fine_keyval(key, part):
    key_portion = rough_field(jax.random.fold_in(key, 2), (NLAT, NLON, D), 1.4)
    value_portion = rough_field(jax.random.fold_in(key, 3), (NLAT, NLON, D), 1.0)
    return jnp.concatenate([key_portion, value_portion], axis=-1).astype(jnp.bfloat16)


def draw_coarse_query(key, part):
    values = rough_field(jax.random.fold_in(key, 4), (CLAT, CLON, D), 1.4)
    return values.astype(jnp.bfloat16)


def draw_coarse_keyval(key, part):
    key_portion = rough_field(jax.random.fold_in(key, 5), (CLAT, CLON, D), 1.4)
    value_portion = rough_field(jax.random.fold_in(key, 6), (CLAT, CLON, D), 1.0)
    return jnp.concatenate([key_portion, value_portion], axis=-1).astype(jnp.bfloat16)


def centred(own_key, shape, deviation, reach, held_as=jnp.bfloat16):
    drawn = jax.random.normal(own_key, shape, jnp.float32) * deviation
    return jnp.minimum(jnp.maximum(drawn, -reach), reach).astype(held_as)


def setup_inputs(seed: int = 0) -> dict:
    splits = jax.random.split(jax.random.key(seed), 6)
    return {
        "fine_query": draw_fine_query(jax.random.fold_in(splits[5], 71), 0),
        "fine_keyval": draw_fine_keyval(jax.random.fold_in(splits[5], 71), 0),
        "coarse_query": draw_coarse_query(jax.random.fold_in(splits[5], 71), 0),
        "coarse_keyval": draw_coarse_keyval(jax.random.fold_in(splits[5], 71), 0),
        "out_weight": centred(splits[4], (D, D), D ** -0.5, 0.25),
    }


NEGATIVE = -1e+30

def window_allowed(tile_rows, tile_cols, radius, rows_valid):
    ext_rows = tile_rows + 2 * radius
    ext_cols = tile_cols + 2 * radius
    query_pos = jnp.arange(tile_rows * tile_cols, dtype=jnp.int32)
    key_pos = jnp.arange(ext_rows * ext_cols, dtype=jnp.int32)
    lat_gap = (key_pos // ext_cols)[None, :] - radius - (query_pos // tile_cols)[:, None]
    lon_gap = (key_pos % ext_cols)[None, :] - radius - (query_pos % tile_cols)[:, None]
    key_valid = jnp.repeat(rows_valid, ext_cols)
    return (jnp.abs(lat_gap) <= radius) & (jnp.abs(lon_gap) <= radius) & key_valid[None, :]

def rows_inside(tile_index, tile_rows, radius, total_rows):
    global_rows = tile_index * tile_rows - radius + jnp.arange(tile_rows + 2 * radius, dtype=jnp.int32)
    return (global_rows >= 0) & (global_rows < total_rows)

def attend(queries, keyval, allowed, head_count):
    length, channels = queries.shape
    head_dim = channels // head_count
    scaling_factor = 1.0 / math.sqrt(head_dim)
    query_portion = queries.astype(jnp.float32).reshape(length, head_count, head_dim)
    key_portion = keyval[:, :channels].astype(jnp.float32).reshape(-1, head_count, head_dim)
    value_portion = keyval[:, channels:].astype(jnp.float32).reshape(-1, head_count, head_dim)
    logit_scores = jnp.einsum('qkf,okf->kqo', query_portion, key_portion, precision=lax.Precision.HIGHEST) * scaling_factor
    if allowed is not None:
        logit_scores = jnp.where(allowed[None, :, :], logit_scores, NEGATIVE)
    logit_scores = logit_scores - lax.optimization_barrier(jnp.max(logit_scores, axis=-1, keepdims=True))
    raised = jnp.exp(logit_scores)
    softmax_weights = (raised / lax.optimization_barrier(jnp.sum(raised, axis=-1, keepdims=True))).astype(jnp.bfloat16)
    blended_output = jnp.einsum('ekp,peu->keu', softmax_weights.astype(jnp.float32), value_portion, precision=lax.Precision.HIGHEST)
    return blended_output.reshape(length, channels)

def upsample_table(fine_size):
    fine_index = jnp.arange(fine_size, dtype=jnp.int32)
    coarse_index = fine_index // 4
    offset = ((fine_index % 4).astype(jnp.float32) - 1.5) / 4.0
    columns = jnp.arange(fine_size // 4 + 2, dtype=jnp.int32)
    before = jnp.where(offset < 0, -offset, 0.0)
    after = jnp.where(offset > 0, offset, 0.0)
    centre = 1.0 - jnp.abs(offset)
    table = jnp.where(columns[None, :] == coarse_index[:, None], before[:, None], 0.0)
    table = table + jnp.where(columns[None, :] == coarse_index[:, None] + 1, centre[:, None], 0.0)
    table = table + jnp.where(columns[None, :] == coarse_index[:, None] + 2, after[:, None], 0.0)
    return table.astype(jnp.float32)

def upsample(coarse, lat_table, lon_table):
    halfway = jnp.einsum('ia,abc->ibc', lat_table, coarse.astype(jnp.float32), precision=lax.Precision.HIGHEST)
    return jnp.einsum('jb,ibc->ijc', lon_table, halfway, precision=lax.Precision.HIGHEST)

def reference(fine_query, fine_keyval, coarse_query, coarse_keyval, out_weight):
    tiles = N_LAT * N_LON
    tile_ids = jnp.arange(tiles, dtype=jnp.int32)
    zero = jnp.zeros((), jnp.int32)

    def coarse_tile(tile):
        tile_lat = tile // N_LON
        tile_lon = tile % N_LON
        lat_rows = tile_lat * CH - RADIUS + jnp.arange(CH + 2 * RADIUS, dtype=jnp.int32)
        lon_cols = (tile_lon * CW - RADIUS + jnp.arange(CW + 2 * RADIUS, dtype=jnp.int32)) % CLON
        extended = jnp.take(jnp.take(coarse_keyval, lon_cols, axis=1), jnp.clip(lat_rows, 0, CLAT - 1), axis=0)
        queries = lax.dynamic_slice(coarse_query, ((tile_lat * CH).astype(jnp.int32), (tile_lon * CW).astype(jnp.int32), zero), (CH, CW, D))
        allowed = window_allowed(CH, CW, RADIUS, rows_inside(tile_lat, CH, RADIUS, CLAT))
        return attend(queries.reshape(-1, D), extended.reshape(-1, 2 * D), allowed, HEADS).astype(jnp.bfloat16)
    coarse_att = lax.map(coarse_tile, tile_ids)
    coarse_att = coarse_att.reshape(N_LAT, N_LON, CH, CW, D).transpose(0, 2, 1, 3, 4).reshape(CLAT, CLON, D)
    lat_table = upsample_table(FH)
    lon_table = upsample_table(FW)

    def fine_tile(tile):
        tile_lat = tile // N_LON
        tile_lon = tile % N_LON
        lat_rows = tile_lat * FH - RADIUS + jnp.arange(FH + 2 * RADIUS, dtype=jnp.int32)
        lon_cols = (tile_lon * FW - RADIUS + jnp.arange(FW + 2 * RADIUS, dtype=jnp.int32)) % NLON
        extended = jnp.take(jnp.take(fine_keyval, lon_cols, axis=1), jnp.clip(lat_rows, 0, NLAT - 1), axis=0)
        queries = lax.dynamic_slice(fine_query, ((tile_lat * FH).astype(jnp.int32), (tile_lon * FW).astype(jnp.int32), zero), (FH, FW, D)).reshape(-1, D)
        allowed = window_allowed(FH, FW, RADIUS, rows_inside(tile_lat, FH, RADIUS, NLAT))
        fine_att = attend(queries, extended.reshape(-1, 2 * D), allowed, HEADS).astype(jnp.bfloat16)
        cycle_rows = jnp.clip(tile_lat * CH - 1 + jnp.arange(CH + 2, dtype=jnp.int32), 0, CLAT - 1)
        cycle_cols = (tile_lon * CW - 1 + jnp.arange(CW + 2, dtype=jnp.int32)) % CLON
        cycle_keyval = jnp.take(jnp.take(coarse_keyval, cycle_cols, axis=1), cycle_rows, axis=0)
        cycle_att = jnp.take(jnp.take(coarse_att, cycle_cols, axis=1), cycle_rows, axis=0)
        up_keyval = upsample(cycle_keyval, lat_table, lon_table).astype(jnp.bfloat16).reshape(-1, 2 * D)
        up_att = upsample(cycle_att, lat_table, lon_table).reshape(-1, D)
        cross = attend(queries, up_keyval, None, HEADS)
        joined = (fine_att.astype(jnp.float32) + cross + up_att).astype(jnp.bfloat16)
        return jnp.dot(joined, out_weight, preferred_element_type=jnp.float32).astype(jnp.bfloat16)
    output = lax.map(fine_tile, tile_ids)
    return output.reshape(N_LAT, N_LON, FH, FW, D).transpose(0, 2, 1, 3, 4).reshape(NLAT, NLON, D)
```

```python
import math

import jax
import jax.numpy as jnp
import numpy as np
from jax import lax
from jax.experimental import pallas as pl
from jax.experimental.pallas import tpu as pltpu
from jax.sharding import PartitionSpec as P

HEADS = 8
RADIUS = 6
FACTOR = 4
ROWS, COLS = 24, 32
CROWS, CCOLS = 6, 8
LANES = 128
BLOCK_ROWS = 8
BLOCKS = ROWS // BLOCK_ROWS
BLOCK = BLOCK_ROWS * COLS
MASKED = -16384.0
EXPONENT = 0.125 * math.log2(math.e)
F32 = jnp.float32
BF16 = jnp.bfloat16


ROW_ORDER = list(range(2, 22)) + [0, 1, 22, 23]
LEFT_FINE = [(r, c - RADIUS) for r in ROW_ORDER for c in range(RADIUS)]
RIGHT_FINE = [(r, COLS + c) for r in ROW_ORDER for c in range(RADIUS)]
CORNER_TOP = list(range(0, 24)) + list(range(120, 132))
CORNER_BOTTOM = list(range(96, 120)) + list(range(132, 144))
CORNERS = 36
LATE_ROWS = 96


def own_range(block):
    first = max(0, block * BLOCK_ROWS - RADIUS)
    last = min(ROWS, (block + 1) * BLOCK_ROWS + RADIUS)
    return first * COLS, last * COLS


def lon_slices(block):
    return (((0, 80), (112, 144)), ((0, 128),), ((32, 144),))[block]


def corner_keys(top):
    picks = CORNER_BOTTOM if top else CORNER_TOP
    shift = -ROWS if top else ROWS
    keys = [(LEFT_FINE[i][0] + shift, LEFT_FINE[i][1]) for i in picks]
    keys += [(RIGHT_FINE[i][0] + shift, RIGHT_FINE[i][1]) for i in picks]
    return keys + [None] * (LATE_ROWS - len(keys))


def side_keys(block):
    keys = []
    if block == 0:
        keys += [(r - RADIUS, c) for r in range(RADIUS) for c in range(COLS)]
    if block == BLOCKS - 1:
        keys += [(r + ROWS, c) for r in range(RADIUS) for c in range(COLS)]
    for side in (LEFT_FINE, RIGHT_FINE):
        for low, high in lon_slices(block):
            keys += side[low:high]
    return keys


def mask_lanes(keys, rows, cols):
    table = np.zeros((len(keys), LANES), np.float32)
    for n, key in enumerate(keys):
        if key is None:
            table[n, : len(rows) + len(cols)] = MASKED
            continue
        for i, row in enumerate(rows):
            if abs(key[0] - row) > RADIUS:
                table[n, i] = MASKED
        for j, col in enumerate(cols):
            if abs(key[1] - col) > RADIUS:
                table[n, len(rows) + j] = MASKED
    return table


def chosen_lanes(queries, rows, cols):
    table = np.zeros((len(queries), LANES), np.float32)
    for n, query in enumerate(queries):
        if query is None:
            continue
        table[n, rows.index(query[0])] = 1.0
        table[n, len(rows) + cols.index(query[1])] = 1.0
        table[n, LANES - 1] = 1.0
    return table


def block_rows(block):
    return list(range(block * BLOCK_ROWS, (block + 1) * BLOCK_ROWS))


FINE_COLS = list(range(COLS))
FINE_CHOSEN = chosen_lanes(
    [(r, c) for r in range(BLOCK_ROWS) for c in range(COLS)], list(range(BLOCK_ROWS)), FINE_COLS
)
OWN_MASK = np.concatenate(
    [
        mask_lanes(
            [(n // COLS, n % COLS) for n in range(*own_range(b))], block_rows(b), FINE_COLS
        )
        for b in range(BLOCKS)
    ]
)
SIDE_MASK = np.concatenate(
    [mask_lanes(side_keys(b), block_rows(b), FINE_COLS) for b in range(BLOCKS)]
)
SIDE_SIZES = [len(side_keys(b)) for b in range(BLOCKS)]
EDGE = RADIUS * COLS
CORNER_MASK = np.concatenate(
    [
        mask_lanes(corner_keys(True), block_rows(0), FINE_COLS),
        mask_lanes(corner_keys(False), block_rows(BLOCKS - 1), FINE_COLS),
    ]
)

CQ_COLS = list(range(-1, CCOLS + 1))
OWN_COARSE = [(r, c) for r in range(CROWS) for c in range(CCOLS)]
LEFT_COARSE = [(r, c - 7) for r in range(CROWS) for c in range(7)] + [None] * CROWS
RIGHT_COARSE = [(r, c + CCOLS) for r in range(CROWS) for c in range(7)] + [None] * CROWS
BAND = OWN_COARSE + LEFT_COARSE + RIGHT_COARSE


def moved(keys, rows):
    return [None if key is None else (key[0] + rows, key[1]) for key in keys]


COARSE_KEYS = BAND + moved(BAND, -CROWS) + moved(BAND, CROWS)
COARSE_COUNT = 512
COARSE_KEYS = COARSE_KEYS + [None] * (COARSE_COUNT - len(COARSE_KEYS))
COARSE_QUERIES = (
    OWN_COARSE
    + [None] * 10
    + [(r, -1) for r in range(CROWS)]
    + [None] * 10
    + [(r, CCOLS) for r in range(CROWS)]
)
COARSE_CHOSEN = chosen_lanes(COARSE_QUERIES, list(range(CROWS)), CQ_COLS)
COARSE_MASK = mask_lanes(COARSE_KEYS, list(range(CROWS)), CQ_COLS)
LATE_ATT = (
    [None] * 8
    + [(0, c) for c in range(CCOLS)]
    + [(0, -1), (0, CCOLS)]
    + [None] * (LATE_ROWS - 2 * CORNERS - 10)
)
ATT_CELLS = COARSE_QUERIES + moved(LATE_ATT, -1) + moved(LATE_ATT, CROWS)


def coefficient(fine):
    coarse, offset = fine // FACTOR, (fine % FACTOR - 1.5) / FACTOR
    taps = {coarse: 1.0 - abs(offset)}
    taps[coarse + (1 if offset > 0 else -1)] = abs(offset)
    return taps


def up_table(fine_cells, coarse_cells, pole):
    where = {cell: n for n, cell in reversed(list(enumerate(coarse_cells))) if cell is not None}
    table = np.zeros((len(fine_cells), len(coarse_cells)), np.float32)
    for n, (row, col) in enumerate(fine_cells):
        for r, a in coefficient(row).items():
            if pole == "top":
                r = max(r, 0)
            if pole == "bottom":
                r = min(r, CROWS - 1)
            for c, b in coefficient(col).items():
                table[n, where[(r, c)]] += a * b
    return table


def poles(fine_cells, coarse_cells):
    return np.stack([up_table(fine_cells, coarse_cells, p) for p in ("none", "top", "bottom")])


FINE_CELLS = [(r, c) for r in range(ROWS) for c in range(COLS)]
INNER = [(r, c) for r in range(2, ROWS - 2) for c in range(2, COLS - 2)]
EARLY_COUNT = 512
EARLY_CELLS = INNER[:EARLY_COUNT]
LATE_CELLS = [cell for cell in FINE_CELLS if cell not in set(EARLY_CELLS)]
UP_EARLY = up_table(EARLY_CELLS, OWN_COARSE, "none")
UP_LATE = poles(LATE_CELLS, COARSE_KEYS)
UP_ATT = poles(FINE_CELLS, ATT_CELLS)


def picked(indices, count):
    table = np.zeros((len(indices), count), np.float32)
    for n, index in enumerate(indices):
        if index is not None:
            table[n, index] = 1.0
    return table


FINE_EAST = [r * COLS + COLS - RADIUS + c for r in ROW_ORDER for c in range(RADIUS)]
FINE_WEST = [r * COLS + c for r in ROW_ORDER for c in range(RADIUS)]
PICK_FINE = picked(FINE_EAST + FINE_WEST, ROWS * COLS)
PICK_COARSE = picked(
    [r * CCOLS + 1 + c for r in range(CROWS) for c in range(7)]
    + [None] * CROWS
    + [r * CCOLS + c for r in range(CROWS) for c in range(7)]
    + [None] * CROWS,
    CROWS * CCOLS,
)
PICK_QUERY = picked(
    [None] * 42
    + [r * CCOLS + CCOLS - 1 for r in range(CROWS)]
    + [None] * 42
    + [r * CCOLS for r in range(CROWS)],
    CROWS * CCOLS,
)
SIDE = len(ROW_ORDER) * RADIUS


def late_picks(corner, row):
    rest = LATE_ROWS - 2 * CORNERS
    left = picked(list(corner) + [None] * (CORNERS + rest), SIDE)
    right = picked([None] * CORNERS + list(corner) + [None] * rest, SIDE)
    cells = [(row, c) for c in range(CCOLS)] + [(row, -1), (row, CCOLS)]
    att = [None] * (2 * CORNERS) + [COARSE_QUERIES.index(cell) for cell in cells]
    att = picked(att + [None] * (LATE_ROWS - len(att)), len(COARSE_QUERIES))
    return left, right, att


LATE_PICKS = [
    np.concatenate(tables)
    for tables in zip(late_picks(CORNER_BOTTOM, CROWS - 1), late_picks(CORNER_TOP, 0))
]


PAIRS = HEADS // 2
LEAST, MOST = 2.0**-80, 2.0**100


def halves():
    return lax.broadcasted_iota(jnp.int32, (1, LANES), 1) < LANES // 2


def head_of(pair, head):
    return jnp.where(halves() == (head == 0), pair, jnp.zeros((), pair.dtype))


def packed(first, second):
    return jnp.where(halves(), first, second)


def dot(a, b):
    return jnp.dot(a, b, preferred_element_type=F32)


def scores(queries, keys):
    return lax.dot_general(queries, keys, (((1,), (1,)), ((), ())), preferred_element_type=F32)


def mix(weights, values):
    mixed = dot(weights.astype(BF16), values)
    return mixed[:, :LANES], mixed[:, LANES:]


def with_ones(values):
    return jnp.concatenate([values, jnp.ones_like(values)], 1)


def pole_flags():
    lat = lax.axis_index("lat")
    return lat == 0, lat == lax.axis_size("lat") - 1


def low(pair):
    return pl.ds(pl.multiple_of(pair * LANES, LANES), LANES)


def high(pair):
    return pl.ds(pl.multiple_of((pair + PAIRS) * LANES, LANES), LANES)


def close_edge(mask, closed):
    lane = lax.broadcasted_iota(jnp.int32, (1, LANES), 1)
    return jnp.where((lane == LANES - 1) & closed, MASKED, mask.astype(F32)).astype(BF16)


def plain_softmax(queries, chosen, keys, values):
    mixed, total = [], []
    for head in range(2):
        query = head_of(queries, head)
        if chosen is not None:
            query = jnp.concatenate([query, chosen], 1)
        a, b = mix(jnp.exp2(scores(query, keys) * EXPONENT), values)
        mixed.append(a)
        total.append(b)
    return packed(*mixed), packed(*total)


def exact_softmax(queries, chosen, keys, values):
    results = []
    for head in range(2):
        query = head_of(queries, head)
        if chosen is not None:
            query = jnp.concatenate([query, chosen], 1)
        score = scores(query, keys)
        score = score - jnp.max(score, 1, keepdims=True)
        mixed, total = mix(jnp.exp2(score * EXPONENT), values)
        results.append(mixed / total)
    return packed(*results)


def send_east_west_kernel(fkv_ref, ckv_ref, cq_ref, pf_ref, pc_ref, pq_ref, ce_ref, cw_ref, fe_ref, fw_ref):
    channels = cq_ref.shape[1]
    coarse = dot(pc_ref[...], ckv_ref[...])
    query = dot(pq_ref[...], cq_ref[...])
    coarse = jnp.concatenate([coarse[:, :channels] + query, coarse[:, channels:]], 1).astype(BF16)
    ce_ref[...], cw_ref[...] = coarse[:48], coarse[48:]
    fine = dot(pf_ref[...], fkv_ref[...]).astype(BF16)
    fe_ref[...], fw_ref[...] = fine[:SIDE], fine[SIDE:]


def send_band_kernel(fkv_ref, ckv_ref, left_ref, right_ref, south_ref, north_ref):
    for ref, first in ((south_ref, fkv_ref.shape[0] - EDGE), (north_ref, 0)):
        ref[0:EDGE, :] = fkv_ref[first : first + EDGE, :]
        ref[EDGE : EDGE + 48, :] = ckv_ref[...]
        ref[EDGE + 48 : EDGE + 96, :] = left_ref[...]
        ref[EDGE + 96 : EDGE + 144, :] = right_ref[...]


def send_late_kernel(left_ref, right_ref, att_ref, pl_ref, pr_ref, pa_ref, south_ref, north_ref):
    channels = att_ref.shape[1]
    sides = dot(pl_ref[...], left_ref[...]) + dot(pr_ref[...], right_ref[...])
    att = dot(pa_ref[...], att_ref[...])
    late = jnp.concatenate([sides[:, :channels] + att, sides[:, channels:]], 1).astype(BF16)
    south_ref[...], north_ref[...] = late[:LATE_ROWS], late[LATE_ROWS:]


def early_kernel(q_ref, kv_ref, ckv_ref, up_ref, chosen_ref, mask_ref, of_ref, lf_ref, oc_ref, lc_ref):
    up = up_ref[...]
    chosen = chosen_ref[...]

    @pl.loop(0, PAIRS)
    def _(pair):
        lo, hi = low(pair), high(pair)
        up_keys = dot(up, ckv_ref[:, lo]).astype(BF16)
        up_values = with_ones(dot(up, ckv_ref[:, hi]).astype(BF16))
        offset = 0
        for block in range(BLOCKS):
            first, last = own_range(block)
            mask = mask_ref[offset : offset + last - first, :]
            offset += last - first
            keys = jnp.concatenate([kv_ref[first:last, lo], mask], 1)
            values = with_ones(kv_ref[first:last, hi])
            rows = slice(block * BLOCK, (block + 1) * BLOCK)
            queries = q_ref[rows, lo]
            of_ref[rows, lo], lf_ref[rows, lo] = plain_softmax(queries, chosen, keys, values)
            oc_ref[rows, lo], lc_ref[rows, lo] = plain_softmax(queries, None, up_keys, up_values)


def gathered(refs, lanes):
    own, left, right, top, bottom = refs
    pad = jnp.zeros((COARSE_COUNT - 3 * len(BAND), LANES), BF16)
    return jnp.concatenate(
        [own[:, lanes], left[:, lanes], right[:, lanes], top[EDGE:, lanes], bottom[EDGE:, lanes], pad], 0
    )


def coarse_kernel(q_ref, own_ref, left_ref, right_ref, top_ref, bottom_ref, chosen_ref, mask_ref, out_ref):
    parts = (own_ref, left_ref, right_ref, top_ref, bottom_ref)
    is_top, is_bottom = pole_flags()
    band = len(BAND)
    mask = [
        mask_ref[:band, :],
        close_edge(mask_ref[band : 2 * band, :], is_top),
        close_edge(mask_ref[2 * band :, :], is_bottom),
    ]
    mask = jnp.concatenate(mask, 0)
    chosen = chosen_ref[...]

    @pl.loop(0, PAIRS)
    def _(pair):
        lo, hi = low(pair), high(pair)
        keys = jnp.concatenate([gathered(parts, lo), mask], 1)
        values = with_ones(gathered(parts, hi))
        queries = jnp.concatenate([q_ref[:, lo], left_ref[32:48, lo], right_ref[32:48, lo]], 0)
        out_ref[:, lo] = exact_softmax(queries, chosen, keys, values).astype(BF16)


def side_parts(block, left, right, top, bottom, lanes):
    parts = []
    if block == 0:
        parts.append(top[0:EDGE, lanes])
    if block == BLOCKS - 1:
        parts.append(bottom[0:EDGE, lanes])
    for side in (left, right):
        for a, b in lon_slices(block):
            parts.append(side[a:b, lanes])
    return jnp.concatenate(parts, 0)


def side_masks(mask_ref):
    is_top, is_bottom = pole_flags()
    masks, offset = [], 0
    for block in range(BLOCKS):
        mask = mask_ref[offset : offset + SIDE_SIZES[block], :]
        offset += SIDE_SIZES[block]
        if block in (0, BLOCKS - 1):
            edge = close_edge(mask[:EDGE], is_top if block == 0 else is_bottom)
            mask = jnp.concatenate([edge, mask[EDGE:]], 0)
        masks.append(mask)
    return masks


def late_up(parts, table, pair):
    up_keys = dot(table, gathered(parts, low(pair))).astype(BF16)
    return up_keys, dot(table, gathered(parts, high(pair))).astype(BF16)


def pole_table():
    is_top, is_bottom = pole_flags()
    return jnp.where(is_top, 1, jnp.where(is_bottom, 2, 0))


def middle_kernel(
    q_ref, of_ref, lf_ref, oc_ref, lc_ref, left_ref, right_ref, top_ref, bottom_ref,
    ckv_ref, cl_ref, cr_ref, chosen_ref, mask_ref, late_ref, fo_ref, fl_ref, cross_ref,
):
    parts = (ckv_ref, cl_ref, cr_ref, top_ref, bottom_ref)
    late = late_ref[pole_table()]
    chosen = chosen_ref[...]
    masks = side_masks(mask_ref)

    @pl.loop(0, PAIRS)
    def _(pair):
        lo, hi = low(pair), high(pair)
        up_keys, up_values = late_up(parts, late, pair)
        up_values = with_ones(up_values)
        for block in range(BLOCKS):
            sides = (left_ref, right_ref, top_ref, bottom_ref)
            keys = jnp.concatenate([side_parts(block, *sides, lo), masks[block]], 1)
            values = with_ones(side_parts(block, *sides, hi))
            rows = slice(block * BLOCK, (block + 1) * BLOCK)
            queries = q_ref[rows, lo]
            mixed, total = plain_softmax(queries, chosen, keys, values)
            fo_ref[rows, lo] = of_ref[rows, lo] + mixed
            fl_ref[rows, lo] = lf_ref[rows, lo] + total
            mixed, total = plain_softmax(queries, None, up_keys, up_values)
            cross_ref[rows, lo] = settled(oc_ref[rows, lo] + mixed, lc_ref[rows, lo] + total)


def settled(mixed, total):
    fits = (total > LEAST) & (total < MOST)
    return jnp.where(fits, mixed / total, jnp.nan)


def late_kernel(
    q_ref, fo_ref, fl_ref, cross_ref, lt_ref, lb_ref, att_ref, chosen_ref, mask_ref, up_ref, weight_ref,
    kv_hbm, left_ref, right_ref, top_ref, bottom_ref, ckv_ref, cl_ref, cr_ref,
    own_mask_hbm, side_mask_hbm, early_hbm, late_hbm,
    out_ref, joined_ref, bad_ref, kv_ref, own_mask_ref, side_mask_ref, early_ref, late_ref, sems,
):
    cells = q_ref.shape[0]
    is_top, is_bottom = pole_flags()
    pole = pole_table()
    corner_masks = [
        close_edge(mask_ref[:LATE_ROWS, :], is_top), close_edge(mask_ref[LATE_ROWS:, :], is_bottom)
    ]
    corner_rows = (slice(0, EDGE), slice(cells - EDGE, cells))
    corner_chosen = (slice(0, EDGE), slice(BLOCK - EDGE, BLOCK))
    up = up_ref[pole]
    bad_ref[...] = jnp.zeros_like(bad_ref)

    def up_att(pair):
        lo = low(pair)
        return dot(up, jnp.concatenate([att_ref[:, lo], lt_ref[64:96, lo], lb_ref[64:96, lo]], 0))

    @pl.loop(0, PAIRS)
    def _(pair):
        lo, hi = low(pair), high(pair)
        raised = up_att(pair)
        pieces = []
        for rows, picks, mask, late in zip(corner_rows, corner_chosen, corner_masks, (lt_ref, lb_ref)):
            keys = jnp.concatenate([late[:, lo], mask], 1)
            values = with_ones(late[:, hi])
            mixed, total = plain_softmax(q_ref[rows, lo], chosen_ref[picks, :], keys, values)
            pieces.append((rows, fo_ref[rows, lo] + mixed, fl_ref[rows, lo] + total))
        rows = slice(EDGE, cells - EDGE)
        pieces.append((rows, fo_ref[rows, lo], fl_ref[rows, lo]))
        for rows, mixed, total in pieces:
            fine = settled(mixed, total).astype(BF16).astype(F32)
            joined = fine + cross_ref[rows, lo] + raised[rows, :]
            joined_ref[pair, rows, :] = joined.astype(BF16)
            bad_ref[...] += jnp.sum(joined.reshape(-1, 8, LANES) * 0.0, 0)

    @pl.when(jnp.logical_not(jnp.sum(bad_ref[...]) == 0.0))
    def _():
        moves = [(kv_hbm, kv_ref), (own_mask_hbm, own_mask_ref), (side_mask_hbm, side_mask_ref),
                 (early_hbm, early_ref), (late_hbm, late_ref)]
        copies = [pltpu.make_async_copy(a, b, sems.at[n]) for n, (a, b) in enumerate(moves)]
        for copy in copies:
            copy.start()
        for copy in copies:
            copy.wait()
        parts = (ckv_ref, cl_ref, cr_ref, top_ref, bottom_ref)
        sides = (left_ref, right_ref, top_ref, bottom_ref)
        masks = side_masks(side_mask_ref)
        chosen = chosen_ref[...]

        @pl.loop(0, PAIRS)
        def _(pair):
            lo, hi = low(pair), high(pair)
            up_keys, up_values = late_up(parts, late_ref[pole], pair)
            up_keys = jnp.concatenate([dot(early_ref[...], ckv_ref[:, lo]).astype(BF16), up_keys], 0)
            up_values = jnp.concatenate([dot(early_ref[...], ckv_ref[:, hi]).astype(BF16), up_values], 0)
            up_values = with_ones(up_values)
            raised = up_att(pair)
            offset = 0
            for block in range(BLOCKS):
                first, last = own_range(block)
                mask = [own_mask_ref[offset : offset + last - first, :], masks[block]]
                offset += last - first
                keys = [kv_ref[first:last, lo], side_parts(block, *sides, lo)]
                values = [kv_ref[first:last, hi], side_parts(block, *sides, hi)]
                if block in (0, BLOCKS - 1):
                    late = lt_ref if block == 0 else lb_ref
                    mask.append(corner_masks[0 if block == 0 else 1])
                    keys.append(late[:, lo])
                    values.append(late[:, hi])
                keys = jnp.concatenate([jnp.concatenate(keys, 0), jnp.concatenate(mask, 0)], 1)
                values = with_ones(jnp.concatenate(values, 0))
                rows = slice(block * BLOCK, (block + 1) * BLOCK)
                queries = q_ref[rows, lo]
                fine = exact_softmax(queries, chosen, keys, values).astype(BF16).astype(F32)
                cross = exact_softmax(queries, None, up_keys, up_values)
                joined_ref[pair, rows, :] = (fine + cross + raised[rows, :]).astype(BF16)

    joined = jnp.concatenate([joined_ref[n] for n in range(PAIRS)], 1)
    out_ref[...] = dot(joined, weight_ref[...]).astype(BF16)


def constant(table):
    return jnp.asarray(table, BF16)


def call(kernel, name, outs, operands, flops, hbm=(), scratch=(), vmem=28):
    near = pl.BlockSpec(memory_space=pltpu.VMEM)
    far = pl.BlockSpec(memory_space=pl.ANY)
    moved_bytes = sum(x.size * x.dtype.itemsize for x in list(operands) + list(outs))
    return pl.pallas_call(
        kernel,
        in_specs=[far if n in hbm else near for n in range(len(operands))],
        out_specs=[near] * len(outs),
        out_shape=list(outs),
        scratch_shapes=list(scratch),
        compiler_params=pltpu.CompilerParams(vmem_limit_bytes=vmem << 20),
        cost_estimate=pl.CostEstimate(
            flops=int(flops), bytes_accessed=int(moved_bytes), transcendentals=int(flops / 1000)
        ),
        name=name,
    )(*operands)


def shards(fine_query, fine_keyval, coarse_query, coarse_keyval, out_weight):
    channels = fine_query.shape[-1]
    lat, lon = lax.axis_size("lat"), lax.axis_size("lon")
    east = [(i, (i + 1) % lon) for i in range(lon)]
    west = [(b, a) for a, b in east]
    south = [(i, i + 1) for i in range(lat - 1)]
    north = [(b, a) for a, b in south]
    cells = ROWS * COLS
    fq = fine_query.reshape(cells, channels)
    fkv = fine_keyval.reshape(cells, 2 * channels)
    cq = coarse_query.reshape(-1, channels)
    ckv = coarse_keyval.reshape(-1, 2 * channels)
    half = lambda rows: jax.ShapeDtypeStruct((rows, channels), BF16)
    full = lambda rows: jax.ShapeDtypeStruct((rows, 2 * channels), BF16)
    state = jax.ShapeDtypeStruct((cells, channels), F32)

    coarse_east, coarse_west, fine_east, fine_west = call(
        send_east_west_kernel, "send_lon", [full(48), full(48), full(SIDE), full(SIDE)],
        [fkv, ckv, cq, constant(PICK_FINE), constant(PICK_COARSE), constant(PICK_QUERY)], 5e8,
    )
    coarse_left = lax.ppermute(coarse_east, "lon", east)
    coarse_right = lax.ppermute(coarse_west, "lon", west)
    fine_left = lax.ppermute(fine_east, "lon", east)
    fine_right = lax.ppermute(fine_west, "lon", west)

    mid_rows = EDGE + len(BAND)
    band_south, band_north = call(
        send_band_kernel, "send_band", [full(mid_rows)] * 2, [fkv, ckv, coarse_left, coarse_right], 1e6
    )
    mid_top = lax.ppermute(band_south, "lat", south)
    mid_bottom = lax.ppermute(band_north, "lat", north)

    early = call(
        early_kernel, "early", [state] * 4,
        [fq, fkv, ckv, constant(UP_EARLY), constant(FINE_CHOSEN), constant(OWN_MASK)], 1e10,
    )
    mid_top, mid_bottom, early = lax.optimization_barrier((mid_top, mid_bottom, early))

    (coarse_att,) = call(
        coarse_kernel, "coarse", [half(len(COARSE_QUERIES))],
        [cq, ckv, coarse_left, coarse_right, mid_top, mid_bottom, constant(COARSE_CHOSEN), constant(COARSE_MASK)],
        2e9,
    )
    late_south, late_north = call(
        send_late_kernel, "send_late", [full(LATE_ROWS)] * 2,
        [fine_left, fine_right, coarse_att] + [constant(table) for table in LATE_PICKS], 2e8,
    )
    late_top = lax.ppermute(late_south, "lat", south)
    late_bottom = lax.ppermute(late_north, "lat", north)

    sides = [fine_left, fine_right, mid_top, mid_bottom, ckv, coarse_left, coarse_right]
    fine_mixed, fine_total, cross = call(
        middle_kernel, "middle", [state] * 3,
        [fq, *early, *sides, constant(FINE_CHOSEN), constant(SIDE_MASK), constant(UP_LATE)], 6e9,
    )
    (out,) = call(
        late_kernel, "late", [half(cells)],
        [fq, fine_mixed, fine_total, cross, late_top, late_bottom, coarse_att, constant(FINE_CHOSEN),
         constant(CORNER_MASK), constant(UP_ATT), out_weight, fkv, *sides,
         constant(OWN_MASK), constant(SIDE_MASK), constant(UP_EARLY), constant(UP_LATE)],
        3e9,
        hbm=(11, 19, 20, 21, 22),
        scratch=[
            pltpu.VMEM((PAIRS, cells, LANES), BF16), pltpu.VMEM((8, LANES), F32),
            pltpu.VMEM((cells, 2 * channels), BF16), pltpu.VMEM(OWN_MASK.shape, BF16),
            pltpu.VMEM(SIDE_MASK.shape, BF16), pltpu.VMEM(UP_EARLY.shape, BF16),
            pltpu.VMEM(UP_LATE.shape, BF16), pltpu.SemaphoreType.DMA((5,)),
        ],
    )
    return out.reshape(ROWS, COLS, channels)


def solution(mesh):
    tiled = P("lat", "lon", None)
    return jax.shard_map(
        shards, mesh=mesh, in_specs=(tiled,) * 4 + (P(),), out_specs=tiled, check_vma=False
    )
```

```python
import math

import jax
import jax.numpy as jnp
import numpy as np
from jax import lax
from jax.experimental import pallas as pl
from jax.experimental.pallas import tpu as pltpu
from jax.sharding import PartitionSpec as P

HEADS = 8
RADIUS = 6
FACTOR = 4
ROWS, COLS = 24, 32
CROWS, CCOLS = 6, 8
LANES = 128
BLOCK_ROWS = 8
BLOCKS = ROWS // BLOCK_ROWS
BLOCK = BLOCK_ROWS * COLS
MASKED = -16384.0
EXPONENT = 0.125 * math.log2(math.e)
F32 = jnp.float32
BF16 = jnp.bfloat16


ROW_ORDER = list(range(2, 22)) + [0, 1, 22, 23]
LEFT_FINE = [(r, c - RADIUS) for r in ROW_ORDER for c in range(RADIUS)]
RIGHT_FINE = [(r, COLS + c) for r in ROW_ORDER for c in range(RADIUS)]
CORNER_TOP = list(range(0, 24)) + list(range(120, 132))
CORNER_BOTTOM = list(range(96, 120)) + list(range(132, 144))
CORNERS = 36
LATE_ROWS = 96


OWN_BLOCKS = [((0, 10), (0, 16)), ((10, 14), (4, 20)), ((14, 24), (8, 24))]


def corner_keys(top):
    picks = CORNER_BOTTOM if top else CORNER_TOP
    shift = -ROWS if top else ROWS
    keys = [(LEFT_FINE[i][0] + shift, LEFT_FINE[i][1]) for i in picks]
    keys += [(RIGHT_FINE[i][0] + shift, RIGHT_FINE[i][1]) for i in picks]
    return keys + [None] * (LATE_ROWS - len(keys))


def mask_lanes(keys, rows, cols):
    table = np.zeros((len(keys), LANES), np.float32)
    for n, key in enumerate(keys):
        if key is None:
            table[n, : len(rows) + len(cols)] = MASKED
            continue
        for i, row in enumerate(rows):
            if abs(key[0] - row) > RADIUS:
                table[n, i] = MASKED
        for j, col in enumerate(cols):
            if abs(key[1] - col) > RADIUS:
                table[n, len(rows) + j] = MASKED
    return table


def chosen_lanes(queries, rows, cols):
    table = np.zeros((len(queries), LANES), np.float32)
    for n, query in enumerate(queries):
        if query is None:
            continue
        table[n, rows.index(query[0])] = 1.0
        table[n, len(rows) + cols.index(query[1])] = 1.0
        table[n, LANES - 1] = 1.0
    return table


def cells_of(rows, cols):
    return [(r, c) for r in rows for c in cols]


FINE_COLS = list(range(COLS))
EDGE = RADIUS * COLS
GROUP = 8
WEST_COLS, EAST_COLS = list(range(GROUP)), list(range(COLS - GROUP, COLS))
ALL_ROWS = list(range(ROWS))
TOP_ROWS, BOTTOM_ROWS = list(range(RADIUS)), list(range(ROWS - RADIUS, ROWS))
TOP_FINE = cells_of(range(-RADIUS, 0), range(COLS))
BOTTOM_FINE = cells_of(range(ROWS, ROWS + RADIUS), range(COLS))
OWN_FINE = cells_of(ALL_ROWS, FINE_COLS)


def tables_of(queries, keys):
    rows = sorted({q[0] for q in queries})
    cols = sorted({q[1] for q in queries})
    return chosen_lanes(queries, rows, cols), mask_lanes(keys, rows, cols)


def stacked(pairs):
    made = [tables_of(*pair) for pair in pairs]
    return [np.concatenate(tables) for tables in zip(*made)]


OWN_CHOSEN, OWN_MASK = stacked(
    [
        (cells_of(range(*q), FINE_COLS), cells_of(range(*k), FINE_COLS))
        for q, k in OWN_BLOCKS
    ]
)
LON_CHOSEN, LON_MASK = stacked(
    [
        (cells_of(ALL_ROWS, WEST_COLS), LEFT_FINE),
        (cells_of(ALL_ROWS, EAST_COLS), RIGHT_FINE),
    ]
)
LAT_CHOSEN, LAT_MASK = stacked(
    [
        (cells_of(TOP_ROWS, FINE_COLS), TOP_FINE),
        (cells_of(BOTTOM_ROWS, FINE_COLS), BOTTOM_FINE),
    ]
)
CORNER_CHOSEN, CORNER_MASK = stacked(
    [
        (cells_of(TOP_ROWS, WEST_COLS) + cells_of(TOP_ROWS, EAST_COLS), corner_keys(True)),
        (cells_of(BOTTOM_ROWS, WEST_COLS) + cells_of(BOTTOM_ROWS, EAST_COLS), corner_keys(False)),
    ]
)
EXACT_KEYS = (
    OWN_FINE + LEFT_FINE + RIGHT_FINE + TOP_FINE + corner_keys(True) + BOTTOM_FINE + corner_keys(False)
)
EXACT_CHOSEN, EXACT_MASK = stacked(
    [
        (cells_of(range(b * BLOCK_ROWS, (b + 1) * BLOCK_ROWS), FINE_COLS), EXACT_KEYS)
        for b in range(BLOCKS)
    ]
)

CQ_COLS = list(range(-1, CCOLS + 1))
OWN_COARSE = [(r, c) for r in range(CROWS) for c in range(CCOLS)]
LEFT_COARSE = [(r, c - 7) for r in range(CROWS) for c in range(7)] + [None] * CROWS
RIGHT_COARSE = [(r, c + CCOLS) for r in range(CROWS) for c in range(7)] + [None] * CROWS
BAND = OWN_COARSE + LEFT_COARSE + RIGHT_COARSE


def moved(keys, rows):
    return [None if key is None else (key[0] + rows, key[1]) for key in keys]


COARSE_KEYS = BAND + moved(BAND, -CROWS) + moved(BAND, CROWS)
COARSE_COUNT = 512
COARSE_KEYS = COARSE_KEYS + [None] * (COARSE_COUNT - len(COARSE_KEYS))
COARSE_QUERIES = (
    OWN_COARSE
    + [None] * 10
    + [(r, -1) for r in range(CROWS)]
    + [None] * 10
    + [(r, CCOLS) for r in range(CROWS)]
)
COARSE_CHOSEN = chosen_lanes(COARSE_QUERIES, list(range(CROWS)), CQ_COLS)
COARSE_MASK = mask_lanes(COARSE_KEYS, list(range(CROWS)), CQ_COLS)
LATE_ATT = (
    [None] * 8
    + [(0, c) for c in range(CCOLS)]
    + [(0, -1), (0, CCOLS)]
    + [None] * (LATE_ROWS - 2 * CORNERS - 10)
)
ATT_CELLS = COARSE_QUERIES + moved(LATE_ATT, -1) + moved(LATE_ATT, CROWS)


def coefficient(fine):
    coarse, offset = fine // FACTOR, (fine % FACTOR - 1.5) / FACTOR
    taps = {coarse: 1.0 - abs(offset)}
    taps[coarse + (1 if offset > 0 else -1)] = abs(offset)
    return taps


def up_table(fine_cells, coarse_cells, pole):
    where = {cell: n for n, cell in reversed(list(enumerate(coarse_cells))) if cell is not None}
    table = np.zeros((len(fine_cells), len(coarse_cells)), np.float32)
    for n, (row, col) in enumerate(fine_cells):
        for r, a in coefficient(row).items():
            if pole == "top":
                r = max(r, 0)
            if pole == "bottom":
                r = min(r, CROWS - 1)
            for c, b in coefficient(col).items():
                table[n, where[(r, c)]] += a * b
    return table


def poles(fine_cells, coarse_cells):
    return np.stack([up_table(fine_cells, coarse_cells, p) for p in ("none", "top", "bottom")])


FINE_CELLS = [(r, c) for r in range(ROWS) for c in range(COLS)]
INNER = [(r, c) for r in range(2, ROWS - 2) for c in range(2, COLS - 2)]
EARLY_COUNT = 512
EARLY_CELLS = INNER[:EARLY_COUNT]
LATE_CELLS = [cell for cell in FINE_CELLS if cell not in set(EARLY_CELLS)]
UP_EARLY = up_table(EARLY_CELLS, OWN_COARSE, "none")
UP_LATE = poles(LATE_CELLS, COARSE_KEYS)
UP_ATT = poles(FINE_CELLS, ATT_CELLS)


def picked(indices, count):
    table = np.zeros((len(indices), count), np.float32)
    for n, index in enumerate(indices):
        if index is not None:
            table[n, index] = 1.0
    return table


FINE_EAST = [r * COLS + COLS - RADIUS + c for r in ROW_ORDER for c in range(RADIUS)]
FINE_WEST = [r * COLS + c for r in ROW_ORDER for c in range(RADIUS)]
PICK_FINE = picked(FINE_EAST + FINE_WEST, ROWS * COLS)
PICK_COARSE = picked(
    [r * CCOLS + 1 + c for r in range(CROWS) for c in range(7)]
    + [None] * CROWS
    + [r * CCOLS + c for r in range(CROWS) for c in range(7)]
    + [None] * CROWS,
    CROWS * CCOLS,
)
PICK_QUERY = picked(
    [None] * 42
    + [r * CCOLS + CCOLS - 1 for r in range(CROWS)]
    + [None] * 42
    + [r * CCOLS for r in range(CROWS)],
    CROWS * CCOLS,
)
SIDE = len(ROW_ORDER) * RADIUS


def late_picks(corner, row):
    rest = LATE_ROWS - 2 * CORNERS
    left = picked(list(corner) + [None] * (CORNERS + rest), SIDE)
    right = picked([None] * CORNERS + list(corner) + [None] * rest, SIDE)
    cells = [(row, c) for c in range(CCOLS)] + [(row, -1), (row, CCOLS)]
    att = [None] * (2 * CORNERS) + [COARSE_QUERIES.index(cell) for cell in cells]
    att = picked(att + [None] * (LATE_ROWS - len(att)), len(COARSE_QUERIES))
    return left, right, att


LATE_PICKS = [
    np.concatenate(tables)
    for tables in zip(late_picks(CORNER_BOTTOM, CROWS - 1), late_picks(CORNER_TOP, 0))
]


PAIRS = HEADS // 2
LEAST, MOST = 2.0**-80, 2.0**100


def halves():
    return lax.broadcasted_iota(jnp.int32, (1, LANES), 1) < LANES // 2


def head_of(pair, head):
    return jnp.where(halves() == (head == 0), pair, jnp.zeros((), pair.dtype))


def packed(first, second):
    return jnp.where(halves(), first, second)


def dot(a, b):
    return jnp.dot(a, b, preferred_element_type=F32)


def scores(queries, keys):
    return lax.dot_general(queries, keys, (((1,), (1,)), ((), ())), preferred_element_type=F32)


def mix(weights, values):
    mixed = dot(weights.astype(BF16), values)
    return mixed[:, :LANES], mixed[:, LANES:]


def with_ones(values):
    return jnp.concatenate([values, jnp.ones_like(values)], 1)


def even(axis):
    return lax.axis_index(axis) % 2 == 0


def pole_flags():
    lat = lax.axis_index("lat")
    return lat == 0, lat == lax.axis_size("lat") - 1


def pole_table():
    is_top, is_bottom = pole_flags()
    return jnp.where(is_top, 1, jnp.where(is_bottom, 2, 0))


def lanes_of(group):
    if isinstance(group, int):
        return slice(group * LANES, (group + 1) * LANES)
    return pl.ds(pl.multiple_of(group * LANES, LANES), LANES)


def low(pair):
    return lanes_of(pair)


def high(pair):
    return lanes_of(pair + PAIRS)


def close_edge(mask, closed):
    lane = lax.broadcasted_iota(jnp.int32, (1, LANES), 1)
    return jnp.where((lane == LANES - 1) & closed, MASKED, mask.astype(F32)).astype(BF16)


def before_after(axis, first, second, *index):
    a, b = first[index], second[index]
    return jnp.where(even(axis), b, a), jnp.where(even(axis), a, b)


def both_heads(queries, chosen):
    rows = jnp.concatenate([head_of(queries, 0), head_of(queries, 1)], 0)
    if chosen is None:
        return rows
    return jnp.concatenate([rows, jnp.concatenate([chosen, chosen], 0)], 1)


def plain_softmax(queries, chosen, keys, values):
    count = queries.shape[0]
    mixed, total = mix(jnp.exp2(scores(both_heads(queries, chosen), keys) * EXPONENT), values)
    return packed(mixed[:count], mixed[count:]), packed(total[:count], total[count:])


def exact_softmax(queries, chosen, keys, values):
    count = queries.shape[0]
    score = scores(both_heads(queries, chosen), keys)
    score = score - jnp.max(score, 1, keepdims=True)
    mixed, total = mix(jnp.exp2(score * EXPONENT), values)
    result = mixed / total
    return packed(result[:count], result[count:])


def settled(mixed, total):
    fits = (total > LEAST) & (total < MOST)
    return jnp.where(fits, mixed / total, jnp.nan)


def fetch(moves, sems):
    copies = [pltpu.make_async_copy(a, b, sems.at[n]) for n, (a, b) in enumerate(moves)]
    for copy in copies:
        copy.start()
    for copy in copies:
        copy.wait()


def send_first_kernel(
    fkv_hbm, ckv_hbm, cq_hbm, pf_hbm, pc_hbm, pq_hbm, c0_ref, c1_ref, f0_ref, f1_ref, r0_ref, r1_ref,
    fkv_ref, ckv_ref, cq_ref, pf_ref, pc_ref, pq_ref, sems,
):
    fetch(
        [(fkv_hbm, fkv_ref), (ckv_hbm, ckv_ref), (cq_hbm, cq_ref),
         (pf_hbm, pf_ref), (pc_hbm, pc_ref), (pq_hbm, pq_ref)],
        sems,
    )
    cells, channels = fkv_ref.shape[0], cq_ref.shape[1]
    eastward = even("lon")
    coarse = dot(pc_ref[...], ckv_ref[...])
    query = dot(pq_ref[...], cq_ref[...])
    coarse = jnp.concatenate([coarse[:, :channels] + query, coarse[:, channels:]], 1).astype(BF16)
    c0_ref[...] = jnp.where(eastward, coarse[:48], coarse[48:])
    c1_ref[...] = jnp.where(eastward, coarse[48:], coarse[:48])
    fine = dot(pf_ref[...], fkv_ref[...]).astype(BF16)
    f0_ref[...] = jnp.where(eastward, fine[:SIDE], fine[SIDE:])
    f1_ref[...] = jnp.where(eastward, fine[SIDE:], fine[:SIDE])
    southward = even("lat")
    last = cells - EDGE
    r0_ref[...] = fkv_ref[pl.ds(pl.multiple_of(jnp.where(southward, last, 0), EDGE), EDGE), :]
    r1_ref[...] = fkv_ref[pl.ds(pl.multiple_of(jnp.where(southward, 0, last), EDGE), EDGE), :]


def send_band_kernel(ckv_ref, c0_ref, c1_ref, band_ref):
    left, right = before_after("lon", c0_ref, c1_ref, slice(None), slice(None))
    band_ref[0:48, :] = ckv_ref[...]
    band_ref[48:96, :] = left
    band_ref[96:144, :] = right


def send_late_kernel(f0_ref, f1_ref, att_ref, pl_ref, pr_ref, pa_ref, l0_ref, l1_ref):
    channels = att_ref.shape[1]
    left, right = before_after("lon", f0_ref, f1_ref, slice(None), slice(None))
    sides = dot(pl_ref[...], left) + dot(pr_ref[...], right)
    att = dot(pa_ref[...], att_ref[...])
    late = jnp.concatenate([sides[:, :channels] + att, sides[:, channels:]], 1).astype(BF16)
    southward = even("lat")
    l0_ref[...] = jnp.where(southward, late[:LATE_ROWS], late[LATE_ROWS:])
    l1_ref[...] = jnp.where(southward, late[LATE_ROWS:], late[:LATE_ROWS])


def own_kernel(q_ref, kv_ref, chosen_ref, mask_ref, mixed_ref, total_ref):
    for pair in range(PAIRS):
        lo, hi = low(pair), high(pair)
        at = 0
        for (q0, q1), (k0, k1) in OWN_BLOCKS:
            rows = slice(q0 * COLS, q1 * COLS)
            near = slice(k0 * COLS, k1 * COLS)
            mask = mask_ref[at : at + (k1 - k0) * COLS, :]
            at += (k1 - k0) * COLS
            keys = jnp.concatenate([kv_ref[near, lo], mask], 1)
            mixed_ref[rows, lo], total_ref[rows, lo] = plain_softmax(
                q_ref[rows, lo], chosen_ref[rows, :], keys, with_ones(kv_ref[near, hi])
            )


def early_cross_kernel(q_ref, ckv_ref, up_ref, mixed_ref, total_ref):
    up = up_ref[...]

    for pair in range(PAIRS):
        lo, hi = low(pair), high(pair)
        up_keys = dot(up, ckv_ref[:, lo]).astype(BF16)
        up_values = with_ones(dot(up, ckv_ref[:, hi]).astype(BF16))
        for block in range(BLOCKS):
            rows = slice(block * BLOCK, (block + 1) * BLOCK)
            mixed_ref[rows, lo], total_ref[rows, lo] = plain_softmax(
                q_ref[rows, lo], None, up_keys, up_values
            )


def columns(queries, first):
    rows = queries.shape[0] // COLS
    split = queries.astype(F32).reshape(rows, COLS, LANES)[:, first : first + GROUP]
    return split.reshape(rows * GROUP, LANES).astype(BF16)


def lon_kernel(q_ref, f0_ref, f1_ref, chosen_ref, mask_ref, mixed_ref, total_ref):
    strip = ROWS * GROUP

    for pair in range(PAIRS):
        lo, hi = low(pair), high(pair)
        side_keys = before_after("lon", f0_ref, f1_ref, slice(None), lo)
        side_values = before_after("lon", f0_ref, f1_ref, slice(None), hi)
        queries = q_ref[:, lo]
        for n, first in enumerate((0, COLS - GROUP)):
            rows = slice(n * strip, (n + 1) * strip)
            keys = jnp.concatenate([side_keys[n], mask_ref[n * SIDE : (n + 1) * SIDE, :]], 1)
            mixed_ref[rows, lo], total_ref[rows, lo] = plain_softmax(
                columns(queries, first), chosen_ref[rows, :], keys, with_ones(side_values[n])
            )


def gathered(own, coarse, band, lanes):
    left, right = before_after("lon", *coarse, slice(None), lanes)
    top, bottom = before_after("lat", *band, slice(None), lanes)
    pad = jnp.zeros((COARSE_COUNT - 3 * len(BAND), LANES), BF16)
    return jnp.concatenate([own[:, lanes], left, right, top, bottom, pad], 0)


def coarse_kernel(q_ref, own_ref, c0_ref, c1_ref, b0_ref, b1_ref, chosen_ref, mask_ref, out_ref):
    is_top, is_bottom = pole_flags()
    band = len(BAND)
    mask = [
        mask_ref[:band, :],
        close_edge(mask_ref[band : 2 * band, :], is_top),
        close_edge(mask_ref[2 * band :, :], is_bottom),
    ]
    mask = jnp.concatenate(mask, 0)
    chosen = chosen_ref[...]
    for pair in range(PAIRS):
        lo = slice(pair * LANES, (pair + 1) * LANES)
        hi = slice((pair + PAIRS) * LANES, (pair + PAIRS + 1) * LANES)
        keys = jnp.concatenate([gathered(own_ref, (c0_ref, c1_ref), (b0_ref, b1_ref), lo), mask], 1)
        values = with_ones(gathered(own_ref, (c0_ref, c1_ref), (b0_ref, b1_ref), hi))
        left, right = before_after("lon", c0_ref, c1_ref, slice(32, 48), lo)
        queries = jnp.concatenate([q_ref[:, lo], left, right], 0)
        out_ref[:, lo] = exact_softmax(queries, chosen, keys, values).astype(BF16)


def middle_kernel(
    q_ref, oc_ref, lc_ref, ckv_ref, c0_ref, c1_ref, b0_ref, b1_ref, r0_ref, r1_ref,
    chosen_ref, mask_ref, late_ref, cross_ref, mixed_ref, total_ref,
):
    cells = q_ref.shape[0]
    late = late_ref[pole_table()]
    closed = pole_flags()
    masks = [close_edge(mask_ref[n * EDGE : (n + 1) * EDGE, :], closed[n]) for n in range(2)]

    for pair in range(PAIRS):
        lo, hi = low(pair), high(pair)
        coarse = (ckv_ref, (c0_ref, c1_ref), (b0_ref, b1_ref))
        up_keys = dot(late, gathered(*coarse, lo)).astype(BF16)
        up_values = with_ones(dot(late, gathered(*coarse, hi)).astype(BF16))
        edge_keys = before_after("lat", r0_ref, r1_ref, slice(None), lo)
        edge_values = before_after("lat", r0_ref, r1_ref, slice(None), hi)
        for n, first in enumerate((0, cells - EDGE)):
            rows = slice(n * EDGE, (n + 1) * EDGE)
            keys = jnp.concatenate([edge_keys[n], masks[n]], 1)
            mixed_ref[rows, lo], total_ref[rows, lo] = plain_softmax(
                q_ref[first : first + EDGE, lo], chosen_ref[rows, :], keys, with_ones(edge_values[n])
            )
        for block in range(BLOCKS):
            rows = slice(block * BLOCK, (block + 1) * BLOCK)
            mixed, total = plain_softmax(q_ref[rows, lo], None, up_keys, up_values)
            cross_ref[rows, lo] = settled(oc_ref[rows, lo] + mixed, lc_ref[rows, lo] + total)


def late_kernel(
    q_ref, of_ref, lf_ref, om_ref, lm_ref, ot_ref, lt_ref, cross_ref, l0_ref, l1_ref, att_ref,
    chosen_ref, mask_ref, up_ref, weight_ref,
    kv_hbm, f0_ref, f1_ref, r0_ref, r1_ref, ckv_ref, c0_ref, c1_ref, b0_ref, b1_ref,
    exact_chosen_hbm, exact_mask_hbm, early_hbm, late_hbm,
    out_ref, joined_ref, bad_ref, mixed_ref, total_ref,
    kv_ref, exact_chosen_ref, exact_mask_ref, early_ref, late_ref, sems,
):
    cells = q_ref.shape[0]
    closed = pole_flags()
    pole = pole_table()
    up = up_ref[pole]
    masks = [close_edge(mask_ref[n * LATE_ROWS : (n + 1) * LATE_ROWS, :], closed[n]) for n in range(2)]
    strip = ROWS * GROUP
    corner = RADIUS * GROUP
    bad_ref[...] = jnp.zeros_like(bad_ref)

    def raised_att(pair):
        top, bottom = before_after("lat", l0_ref, l1_ref, slice(64, 96), low(pair))
        return dot(up, jnp.concatenate([att_ref[:, low(pair)], top, bottom], 0))

    for pair in range(PAIRS):
        lo, hi = low(pair), high(pair)
        corner_keys = before_after("lat", l0_ref, l1_ref, slice(None), lo)
        corner_values = before_after("lat", l0_ref, l1_ref, slice(None), hi)
        raised = raised_att(pair)
        mixed_ref[...], total_ref[...] = of_ref[:, lo], lf_ref[:, lo]
        for n, first in enumerate((0, cells - EDGE)):
            there, here = slice(first, first + EDGE), slice(n * EDGE, (n + 1) * EDGE)
            mixed_ref[there, :] += ot_ref[here, lo]
            total_ref[there, :] += lt_ref[here, lo]
            queries = q_ref[there, lo]
            queries = jnp.concatenate([columns(queries, 0), columns(queries, COLS - GROUP)], 0)
            keys = jnp.concatenate([corner_keys[n], masks[n]], 1)
            chosen = chosen_ref[2 * n * corner : 2 * (n + 1) * corner, :]
            mixed, total = plain_softmax(queries, chosen, keys, with_ones(corner_values[n]))
            for row in range(RADIUS):
                for side, col in enumerate((0, COLS - GROUP)):
                    at = first + row * COLS + col
                    piece = slice(side * corner + row * GROUP, side * corner + (row + 1) * GROUP)
                    mixed_ref[at : at + GROUP, :] += mixed[piece]
                    total_ref[at : at + GROUP, :] += total[piece]
        for row in range(ROWS):
            for side, col in enumerate((0, COLS - GROUP)):
                at = row * COLS + col
                piece = slice(side * strip + row * GROUP, side * strip + (row + 1) * GROUP)
                mixed_ref[at : at + GROUP, :] += om_ref[piece, lo]
                total_ref[at : at + GROUP, :] += lm_ref[piece, lo]
        fine = settled(mixed_ref[...], total_ref[...]).astype(BF16).astype(F32)
        joined = fine + cross_ref[:, lo] + raised
        joined_ref[pair] = joined.astype(BF16)
        bad_ref[...] += jnp.sum(joined.reshape(-1, 8, LANES) * 0.0, 0)

    @pl.when(jnp.logical_not(jnp.sum(bad_ref[...]) == 0.0))
    def _():
        fetch(
            [(kv_hbm, kv_ref), (exact_chosen_hbm, exact_chosen_ref), (exact_mask_hbm, exact_mask_ref),
             (early_hbm, early_ref), (late_hbm, late_ref)],
            sems,
        )
        coarse = (ckv_ref, (c0_ref, c1_ref), (b0_ref, b1_ref))
        early, late = early_ref[...], late_ref[pole]
        count = len(EXACT_KEYS)
        edges = [cells + 2 * SIDE, cells + 2 * SIDE + EDGE + LATE_ROWS, count]

        @pl.loop(0, PAIRS)
        def _(pair):
            def all_of(lanes):
                left, right = before_after("lon", f0_ref, f1_ref, slice(None), lanes)
                top, bottom = before_after("lat", r0_ref, r1_ref, slice(None), lanes)
                late_top, late_bottom = before_after("lat", l0_ref, l1_ref, slice(None), lanes)
                return jnp.concatenate(
                    [kv_ref[:, lanes], left, right, top, late_top, bottom, late_bottom], 0
                )

            def up_of(lanes):
                first = dot(early, ckv_ref[:, lanes]).astype(BF16)
                return jnp.concatenate([first, dot(late, gathered(*coarse, lanes)).astype(BF16)], 0)

            lo, hi = low(pair), high(pair)
            keys, values = all_of(lo), with_ones(all_of(hi))
            up_keys, up_values = up_of(lo), with_ones(up_of(hi))
            raised = raised_att(pair)
            for block in range(BLOCKS):
                mask = exact_mask_ref[block * count : (block + 1) * count, :]
                mask = [mask[: edges[0]]] + [
                    close_edge(mask[edges[n] : edges[n + 1]], closed[n]) for n in range(2)
                ]
                rows = slice(block * BLOCK, (block + 1) * BLOCK)
                queries = q_ref[rows, lo]
                fine = exact_softmax(
                    queries,
                    exact_chosen_ref[rows, :],
                    jnp.concatenate([keys, jnp.concatenate(mask, 0)], 1),
                    values,
                )
                cross = exact_softmax(queries, None, up_keys, up_values)
                joined = fine.astype(BF16).astype(F32) + cross + raised[rows, :]
                joined_ref[pair, rows, :] = joined.astype(BF16)

    joined = jnp.concatenate([joined_ref[n] for n in range(PAIRS)], 1)
    out_ref[...] = dot(joined, weight_ref[...]).astype(BF16)


def constant(table):
    return jnp.asarray(table, BF16)


def call(kernel, name, outs, operands, flops, hbm=(), scratch=(), vmem=28):
    near = pl.BlockSpec(memory_space=pltpu.VMEM)
    far = pl.BlockSpec(memory_space=pltpu.HBM)
    moved_bytes = sum(x.size * x.dtype.itemsize for x in list(operands) + list(outs))
    return pl.pallas_call(
        kernel,
        in_specs=[far if n in hbm else near for n in range(len(operands))],
        out_specs=[near] * len(outs),
        out_shape=list(outs),
        scratch_shapes=list(scratch),
        compiler_params=pltpu.CompilerParams(vmem_limit_bytes=vmem << 20),
        cost_estimate=pl.CostEstimate(
            flops=int(flops), bytes_accessed=int(moved_bytes), transcendentals=int(flops / 1000)
        ),
        name=name,
    )(*operands)


def swaps(array, other, axis, ring):
    size = lax.axis_size(axis)
    first = [(i, i + 1) for i in range(0, size - 1, 2)]
    second = [(i, (i + 1) % size) for i in range(1, size if ring else size - 1, 2)]
    both = lambda pairs: pairs + [(b, a) for a, b in pairs]
    return lax.ppermute(array, axis, both(first)), lax.ppermute(other, axis, both(second))


def shards(fine_query, fine_keyval, coarse_query, coarse_keyval, out_weight):
    channels = fine_query.shape[-1]
    cells = ROWS * COLS
    fq = fine_query.reshape(cells, channels)
    fkv = fine_keyval.reshape(cells, 2 * channels)
    cq = coarse_query.reshape(-1, channels)
    ckv = coarse_keyval.reshape(-1, 2 * channels)
    half = lambda rows: jax.ShapeDtypeStruct((rows, channels), BF16)
    full = lambda rows: jax.ShapeDtypeStruct((rows, 2 * channels), BF16)
    state = lambda rows: jax.ShapeDtypeStruct((rows, channels), F32)
    after = lax.optimization_barrier

    picks = [constant(PICK_FINE), constant(PICK_COARSE), constant(PICK_QUERY)]
    first = [fkv, ckv, cq] + picks
    c0, c1, f0, f1, r0, r1 = call(
        send_first_kernel, "send_first", [full(48)] * 2 + [full(SIDE)] * 2 + [full(EDGE)] * 2, first, 5e8,
        hbm=range(6), scratch=[pltpu.VMEM(x.shape, BF16) for x in first] + [pltpu.SemaphoreType.DMA((6,))], vmem=56,
    )
    coarse = swaps(c0, c1, "lon", True)
    sides = swaps(f0, f1, "lon", True)
    edges = swaps(r0, r1, "lat", False)

    own = call(
        own_kernel, "own", [state(cells)] * 2, [fq, fkv, constant(OWN_CHOSEN), constant(OWN_MASK)], 5e9
    )
    coarse, own = after((coarse, own))
    (band,) = call(send_band_kernel, "send_band", [full(len(BAND))], [ckv, *coarse], 1e6)
    bands = swaps(band, band, "lat", False)

    fq, _ = after((fq, band))
    early = call(early_cross_kernel, "early_cross", [state(cells)] * 2, [fq, ckv, constant(UP_EARLY)], 5e9)
    sides, _ = after((sides, early))
    lon = call(
        lon_kernel, "lon_strips", [state(2 * ROWS * GROUP)] * 2,
        [fq, *sides, constant(LON_CHOSEN), constant(LON_MASK)], 1.5e9,
    )
    bands, _ = after((bands, lon))
    (coarse_att,) = call(
        coarse_kernel, "coarse", [half(len(COARSE_QUERIES))],
        [cq, ckv, *coarse, *bands, constant(COARSE_CHOSEN), constant(COARSE_MASK)], 2e9,
    )
    late0, late1 = call(
        send_late_kernel, "send_late", [full(LATE_ROWS)] * 2,
        [*sides, coarse_att] + [constant(table) for table in LATE_PICKS], 2e8,
    )
    lates = swaps(late0, late1, "lat", False)

    cross, lat_mixed, lat_total = call(
        middle_kernel, "middle", [state(cells), state(2 * EDGE), state(2 * EDGE)],
        [fq, *early, ckv, *coarse, *bands, *edges, constant(LAT_CHOSEN), constant(LAT_MASK), constant(UP_LATE)],
        5e9,
    )
    exact = [constant(table) for table in (EXACT_CHOSEN, EXACT_MASK, UP_EARLY, UP_LATE)]
    (out,) = call(
        late_kernel, "late", [half(cells)],
        [fq, *own, *lon, lat_mixed, lat_total, cross, *lates, coarse_att, constant(CORNER_CHOSEN),
         constant(CORNER_MASK), constant(UP_ATT), out_weight,
         fkv, *sides, *edges, ckv, *coarse, *bands, *exact],
        3e9,
        hbm=(15, 25, 26, 27, 28),
        scratch=[
            pltpu.VMEM((PAIRS, cells, LANES), BF16), pltpu.VMEM((8, LANES), F32),
            pltpu.VMEM((cells, LANES), F32), pltpu.VMEM((cells, LANES), F32),
            pltpu.VMEM((cells, 2 * channels), BF16),
            *[pltpu.VMEM(x.shape, BF16) for x in exact], pltpu.SemaphoreType.DMA((5,)),
        ],
    )
    return out.reshape(ROWS, COLS, channels)


def solution(mesh):
    tiled = P("lat", "lon", None)
    return jax.shard_map(
        shards, mesh=mesh, in_specs=(tiled,) * 4 + (P(),), out_specs=tiled, check_vma=False
    )
```

```python
import math

import jax
import jax.numpy as jnp
import numpy as np
from jax import lax
from jax.experimental import pallas as pl
from jax.experimental.pallas import tpu as pltpu
from jax.sharding import PartitionSpec as P

HEADS = 8
RADIUS = 6
FACTOR = 4
ROWS, COLS = 24, 32
CROWS, CCOLS = 6, 8
LANES = 128
BLOCK_ROWS = 8
BLOCKS = ROWS // BLOCK_ROWS
BLOCK = BLOCK_ROWS * COLS
MASKED = -16384.0
EXPONENT = 0.125 * math.log2(math.e)
F32 = jnp.float32
BF16 = jnp.bfloat16


ROW_ORDER = list(range(2, 22)) + [0, 1, 22, 23]
LEFT_FINE = [(r, c - RADIUS) for r in ROW_ORDER for c in range(RADIUS)]
RIGHT_FINE = [(r, COLS + c) for r in ROW_ORDER for c in range(RADIUS)]
CORNER_TOP = list(range(0, 24)) + list(range(120, 132))
CORNER_BOTTOM = list(range(96, 120)) + list(range(132, 144))
CORNERS = 36
LATE_ROWS = 96


OWN_BLOCKS = [((0, 10), (0, 16)), ((10, 14), (4, 20)), ((14, 24), (8, 24))]


def corner_keys(top):
    picks = CORNER_BOTTOM if top else CORNER_TOP
    shift = -ROWS if top else ROWS
    keys = [(LEFT_FINE[i][0] + shift, LEFT_FINE[i][1]) for i in picks]
    keys += [(RIGHT_FINE[i][0] + shift, RIGHT_FINE[i][1]) for i in picks]
    return keys + [None] * (LATE_ROWS - len(keys))


def mask_lanes(keys, rows, cols):
    table = np.zeros((len(keys), LANES), np.float32)
    for n, key in enumerate(keys):
        if key is None:
            table[n, : len(rows) + len(cols)] = MASKED
            continue
        for i, row in enumerate(rows):
            if abs(key[0] - row) > RADIUS:
                table[n, i] = MASKED
        for j, col in enumerate(cols):
            if abs(key[1] - col) > RADIUS:
                table[n, len(rows) + j] = MASKED
    return table


def chosen_lanes(queries, rows, cols):
    table = np.zeros((len(queries), LANES), np.float32)
    for n, query in enumerate(queries):
        if query is None:
            continue
        table[n, rows.index(query[0])] = 1.0
        table[n, len(rows) + cols.index(query[1])] = 1.0
        table[n, LANES - 1] = 1.0
    return table


def cells_of(rows, cols):
    return [(r, c) for r in rows for c in cols]


FINE_COLS = list(range(COLS))
EDGE = RADIUS * COLS
GROUP = 8
WEST_COLS, EAST_COLS = list(range(GROUP)), list(range(COLS - GROUP, COLS))
ALL_ROWS = list(range(ROWS))
TOP_ROWS, BOTTOM_ROWS = list(range(RADIUS)), list(range(ROWS - RADIUS, ROWS))
TOP_FINE = cells_of(range(-RADIUS, 0), range(COLS))
BOTTOM_FINE = cells_of(range(ROWS, ROWS + RADIUS), range(COLS))
OWN_FINE = cells_of(ALL_ROWS, FINE_COLS)


def tables_of(queries, keys):
    rows = sorted({q[0] for q in queries})
    cols = sorted({q[1] for q in queries})
    return chosen_lanes(queries, rows, cols), mask_lanes(keys, rows, cols)


def stacked(pairs):
    made = [tables_of(*pair) for pair in pairs]
    return [np.concatenate(tables) for tables in zip(*made)]


OWN_CHOSEN, OWN_MASK = stacked(
    [
        (cells_of(range(*q), FINE_COLS), cells_of(range(*k), FINE_COLS))
        for q, k in OWN_BLOCKS
    ]
)
LON_CHOSEN, LON_MASK = stacked(
    [
        (cells_of(ALL_ROWS, WEST_COLS), LEFT_FINE),
        (cells_of(ALL_ROWS, EAST_COLS), RIGHT_FINE),
    ]
)
LAT_CHOSEN, LAT_MASK = stacked(
    [
        (cells_of(TOP_ROWS, FINE_COLS), TOP_FINE),
        (cells_of(BOTTOM_ROWS, FINE_COLS), BOTTOM_FINE),
    ]
)
CORNER_CHOSEN, CORNER_MASK = stacked(
    [
        (cells_of(TOP_ROWS, WEST_COLS) + cells_of(TOP_ROWS, EAST_COLS), corner_keys(True)),
        (cells_of(BOTTOM_ROWS, WEST_COLS) + cells_of(BOTTOM_ROWS, EAST_COLS), corner_keys(False)),
    ]
)
EXACT_KEYS = (
    OWN_FINE + LEFT_FINE + RIGHT_FINE + TOP_FINE + corner_keys(True) + BOTTOM_FINE + corner_keys(False)
)
EXACT_CHOSEN, EXACT_MASK = stacked(
    [
        (cells_of(range(b * BLOCK_ROWS, (b + 1) * BLOCK_ROWS), FINE_COLS), EXACT_KEYS)
        for b in range(BLOCKS)
    ]
)

CQ_COLS = list(range(-1, CCOLS + 1))
OWN_COARSE = [(r, c) for r in range(CROWS) for c in range(CCOLS)]
LEFT_COARSE = [(r, c - 7) for r in range(CROWS) for c in range(7)] + [None] * CROWS
RIGHT_COARSE = [(r, c + CCOLS) for r in range(CROWS) for c in range(7)] + [None] * CROWS
BAND = OWN_COARSE + LEFT_COARSE + RIGHT_COARSE


def moved(keys, rows):
    return [None if key is None else (key[0] + rows, key[1]) for key in keys]


COARSE_KEYS = BAND + moved(BAND, -CROWS) + moved(BAND, CROWS)
COARSE_COUNT = 512
COARSE_KEYS = COARSE_KEYS + [None] * (COARSE_COUNT - len(COARSE_KEYS))
COARSE_QUERIES = (
    OWN_COARSE
    + [None] * 10
    + [(r, -1) for r in range(CROWS)]
    + [None] * 10
    + [(r, CCOLS) for r in range(CROWS)]
)
COARSE_CHOSEN = chosen_lanes(COARSE_QUERIES, list(range(CROWS)), CQ_COLS)
COARSE_MASK = mask_lanes(COARSE_KEYS, list(range(CROWS)), CQ_COLS)
LATE_ATT = (
    [None] * 8
    + [(0, c) for c in range(CCOLS)]
    + [(0, -1), (0, CCOLS)]
    + [None] * (LATE_ROWS - 2 * CORNERS - 10)
)
ATT_CELLS = COARSE_QUERIES + moved(LATE_ATT, -1) + moved(LATE_ATT, CROWS)


def coefficient(fine):
    coarse, offset = fine // FACTOR, (fine % FACTOR - 1.5) / FACTOR
    taps = {coarse: 1.0 - abs(offset)}
    taps[coarse + (1 if offset > 0 else -1)] = abs(offset)
    return taps


def up_table(fine_cells, coarse_cells, pole):
    where = {cell: n for n, cell in reversed(list(enumerate(coarse_cells))) if cell is not None}
    table = np.zeros((len(fine_cells), len(coarse_cells)), np.float32)
    for n, (row, col) in enumerate(fine_cells):
        for r, a in coefficient(row).items():
            if pole == "top":
                r = max(r, 0)
            if pole == "bottom":
                r = min(r, CROWS - 1)
            for c, b in coefficient(col).items():
                table[n, where[(r, c)]] += a * b
    return table


def poles(fine_cells, coarse_cells):
    return np.stack([up_table(fine_cells, coarse_cells, p) for p in ("none", "top", "bottom")])


FINE_CELLS = [(r, c) for r in range(ROWS) for c in range(COLS)]
INNER = [(r, c) for r in range(2, ROWS - 2) for c in range(2, COLS - 2)]
EARLY_COUNT = 512
EARLY_CELLS = INNER[:EARLY_COUNT]
LATE_CELLS = [cell for cell in FINE_CELLS if cell not in set(EARLY_CELLS)]
UP_EARLY = up_table(EARLY_CELLS, OWN_COARSE, "none")
UP_LATE = poles(LATE_CELLS, COARSE_KEYS)
UP_ATT = poles(FINE_CELLS, ATT_CELLS)


def picked(indices, count):
    table = np.zeros((len(indices), count), np.float32)
    for n, index in enumerate(indices):
        if index is not None:
            table[n, index] = 1.0
    return table


FINE_EAST = [r * COLS + COLS - RADIUS + c for r in ROW_ORDER for c in range(RADIUS)]
FINE_WEST = [r * COLS + c for r in ROW_ORDER for c in range(RADIUS)]
PICK_FINE = picked(FINE_EAST + FINE_WEST, ROWS * COLS)
PICK_COARSE = picked(
    [r * CCOLS + 1 + c for r in range(CROWS) for c in range(7)]
    + [None] * CROWS
    + [r * CCOLS + c for r in range(CROWS) for c in range(7)]
    + [None] * CROWS,
    CROWS * CCOLS,
)
PICK_QUERY = picked(
    [None] * 42
    + [r * CCOLS + CCOLS - 1 for r in range(CROWS)]
    + [None] * 42
    + [r * CCOLS for r in range(CROWS)],
    CROWS * CCOLS,
)
SIDE = len(ROW_ORDER) * RADIUS


def late_picks(corner, row):
    rest = LATE_ROWS - 2 * CORNERS
    left = picked(list(corner) + [None] * (CORNERS + rest), SIDE)
    right = picked([None] * CORNERS + list(corner) + [None] * rest, SIDE)
    cells = [(row, c) for c in range(CCOLS)] + [(row, -1), (row, CCOLS)]
    att = [None] * (2 * CORNERS) + [COARSE_QUERIES.index(cell) for cell in cells]
    att = picked(att + [None] * (LATE_ROWS - len(att)), len(COARSE_QUERIES))
    return left, right, att


LATE_PICKS = [
    np.concatenate(tables)
    for tables in zip(late_picks(CORNER_BOTTOM, CROWS - 1), late_picks(CORNER_TOP, 0))
]


PAIRS = HEADS // 2
LEAST, MOST = 2.0**-80, 2.0**100


def halves():
    return lax.broadcasted_iota(jnp.int32, (1, LANES), 1) < LANES // 2


def head_of(pair, head):
    return jnp.where(halves() == (head == 0), pair, jnp.zeros((), pair.dtype))


def packed(first, second):
    return jnp.where(halves(), first, second)


def dot(a, b):
    return jnp.dot(a, b, preferred_element_type=F32)


def scores(queries, keys):
    return lax.dot_general(queries, keys, (((1,), (1,)), ((), ())), preferred_element_type=F32)


def mix(weights, values):
    mixed = dot(weights.astype(BF16), values)
    return mixed[:, :LANES], mixed[:, LANES:]


def with_ones(values):
    return jnp.concatenate([values, jnp.ones_like(values)], 1)


def even(axis):
    return lax.axis_index(axis) % 2 == 0


def pole_flags():
    lat = lax.axis_index("lat")
    return lat == 0, lat == lax.axis_size("lat") - 1


def pole_table():
    is_top, is_bottom = pole_flags()
    return jnp.where(is_top, 1, jnp.where(is_bottom, 2, 0))


def lanes_of(group):
    if isinstance(group, int):
        return slice(group * LANES, (group + 1) * LANES)
    return pl.ds(pl.multiple_of(group * LANES, LANES), LANES)


def low(pair):
    return lanes_of(pair)


def high(pair):
    return lanes_of(pair + PAIRS)


def close_edge(mask, closed):
    lane = lax.broadcasted_iota(jnp.int32, (1, LANES), 1)
    return jnp.where((lane == LANES - 1) & closed, MASKED, mask.astype(F32)).astype(BF16)


def before_after(axis, first, second, *index):
    a, b = first[index], second[index]
    if axis == "lat":
        return a, b
    return jnp.where(even(axis), b, a), jnp.where(even(axis), a, b)


def both_heads(queries, chosen):
    rows = jnp.concatenate([head_of(queries, 0), head_of(queries, 1)], 0)
    if chosen is None:
        return rows
    return jnp.concatenate([rows, jnp.concatenate([chosen, chosen], 0)], 1)


def plain_softmax(queries, chosen, keys, values):
    count = queries.shape[0]
    mixed, total = mix(jnp.exp2(scores(both_heads(queries, chosen), keys) * EXPONENT), values)
    return packed(mixed[:count], mixed[count:]), packed(total[:count], total[count:])


def exact_softmax(queries, chosen, keys, values):
    count = queries.shape[0]
    score = scores(both_heads(queries, chosen), keys)
    score = score - jnp.max(score, 1, keepdims=True)
    mixed, total = mix(jnp.exp2(score * EXPONENT), values)
    result = mixed / total
    return packed(result[:count], result[count:])


def settled(mixed, total):
    fits = (total > LEAST) & (total < MOST)
    return jnp.where(fits, mixed / total, jnp.nan)


def fetch(moves, sems):
    copies = [pltpu.make_async_copy(a, b, sems.at[n]) for n, (a, b) in enumerate(moves)]
    for copy in copies:
        copy.start()
    for copy in copies:
        copy.wait()


def send_coarse_kernel(ckv_hbm, cq_hbm, c0_ref, c1_ref, ckv_ref, cq_ref, sems):
    fetch([(ckv_hbm, ckv_ref), (cq_hbm, cq_ref)], sems)
    channels = cq_ref.shape[1]
    n = lax.broadcasted_iota(jnp.int32, (48, CROWS * CCOLS), 0)
    cell = lax.broadcasted_iota(jnp.int32, (48, CROWS * CCOLS), 1)
    row = (n * 37) >> 8
    sides = []
    for first, col in ((1, CCOLS - 1), (0, 0)):
        keyval = (n < 42) & (cell == row * CCOLS + first + n - row * 7)
        query = (n >= 42) & (cell == (n - 42) * CCOLS + col)
        both = dot(keyval.astype(F32).astype(BF16), ckv_ref[...])
        query = dot(query.astype(F32).astype(BF16), cq_ref[...])
        sides.append(jnp.concatenate([both[:, :channels] + query, both[:, channels:]], 1).astype(BF16))
    eastward = even("lon")
    c0_ref[...] = jnp.where(eastward, sides[0], sides[1])
    c1_ref[...] = jnp.where(eastward, sides[1], sides[0])


def send_fine_kernel(fkv_ref, pick_ref, f0_ref, f1_ref, r0_ref, r1_ref):
    cells = fkv_ref.shape[0]
    fine = dot(pick_ref[...], fkv_ref[...]).astype(BF16)
    eastward = even("lon")
    f0_ref[...] = jnp.where(eastward, fine[:SIDE], fine[SIDE:])
    f1_ref[...] = jnp.where(eastward, fine[SIDE:], fine[:SIDE])
    r0_ref[...] = fkv_ref[cells - EDGE :, :]
    r1_ref[...] = fkv_ref[:EDGE, :]


def send_band_kernel(ckv_ref, c0_ref, c1_ref, band_ref):
    left, right = before_after("lon", c0_ref, c1_ref, slice(None), slice(None))
    band_ref[0:48, :] = ckv_ref[...]
    band_ref[48:96, :] = left
    band_ref[96:144, :] = right


def send_late_kernel(f0_ref, f1_ref, att_ref, pl_ref, pr_ref, pa_ref, l0_ref, l1_ref):
    channels = att_ref.shape[1]
    left, right = before_after("lon", f0_ref, f1_ref, slice(None), slice(None))
    sides = dot(pl_ref[...], left) + dot(pr_ref[...], right)
    att = dot(pa_ref[...], att_ref[...])
    late = jnp.concatenate([sides[:, :channels] + att, sides[:, channels:]], 1).astype(BF16)
    l0_ref[...], l1_ref[...] = late[:LATE_ROWS], late[LATE_ROWS:]


def own_kernel(q_ref, kv_ref, chosen_ref, mask_ref, mixed_ref, total_ref):
    for pair in range(PAIRS):
        lo, hi = low(pair), high(pair)
        at = 0
        for (q0, q1), (k0, k1) in OWN_BLOCKS:
            rows = slice(q0 * COLS, q1 * COLS)
            near = slice(k0 * COLS, k1 * COLS)
            mask = mask_ref[at : at + (k1 - k0) * COLS, :]
            at += (k1 - k0) * COLS
            keys = jnp.concatenate([kv_ref[near, lo], mask], 1)
            mixed_ref[rows, lo], total_ref[rows, lo] = plain_softmax(
                q_ref[rows, lo], chosen_ref[rows, :], keys, with_ones(kv_ref[near, hi])
            )


CROSS_ROWS = 256


def raise_pair(table, keys, values):
    both = dot(table, jnp.concatenate([keys, values], 1)).astype(BF16)
    return both[:, :LANES], with_ones(both[:, LANES:])


def early_cross_kernel(q_ref, ckv_ref, up_ref, mixed_ref, total_ref):
    up = up_ref[...]
    for pair in range(PAIRS):
        lo, hi = low(pair), high(pair)
        up_keys, up_values = raise_pair(up, ckv_ref[:, lo], ckv_ref[:, hi])
        for first in range(0, q_ref.shape[0], CROSS_ROWS):
            rows = slice(first, first + CROSS_ROWS)
            mixed_ref[rows, lo], total_ref[rows, lo] = plain_softmax(
                q_ref[rows, lo], None, up_keys, up_values
            )


def columns(queries, first):
    rows = queries.shape[0] // COLS
    split = queries.astype(F32).reshape(rows, COLS, LANES)[:, first : first + GROUP]
    return split.reshape(rows * GROUP, LANES).astype(BF16)


def lon_kernel(q_ref, f0_ref, f1_ref, chosen_ref, mask_ref, om_ref, ot_ref, mixed_ref, total_ref):
    strip = ROWS * GROUP
    for pair in range(PAIRS):
        lo, hi = low(pair), high(pair)
        keys = before_after("lon", f0_ref, f1_ref, slice(None), lo)
        values = before_after("lon", f0_ref, f1_ref, slice(None), hi)
        queries = q_ref[:, lo]
        for n, first in enumerate((0, COLS - GROUP)):
            mixed, total = plain_softmax(
                columns(queries, first),
                chosen_ref[n * strip : (n + 1) * strip, :],
                jnp.concatenate([keys[n], mask_ref[n * SIDE : (n + 1) * SIDE, :]], 1),
                with_ones(values[n]),
            )
            for row in range(ROWS):
                at = slice(row * COLS + first, row * COLS + first + GROUP)
                piece = slice(row * GROUP, (row + 1) * GROUP)
                mixed_ref[at, lo] = om_ref[at, lo] + mixed[piece]
                total_ref[at, lo] = ot_ref[at, lo] + total[piece]


def lat_kernel(q_ref, r0_ref, r1_ref, chosen_ref, mask_ref, om_ref, ot_ref, mixed_ref, total_ref):
    cells = q_ref.shape[0]
    closed = pole_flags()
    masks = [close_edge(mask_ref[n * EDGE : (n + 1) * EDGE, :], closed[n]) for n in range(2)]
    for pair in range(PAIRS):
        lo, hi = low(pair), high(pair)
        keys = before_after("lat", r0_ref, r1_ref, slice(None), lo)
        values = before_after("lat", r0_ref, r1_ref, slice(None), hi)
        for n, first in enumerate((0, cells - EDGE)):
            rows = slice(first, first + EDGE)
            mixed, total = plain_softmax(
                q_ref[rows, lo],
                chosen_ref[n * EDGE : (n + 1) * EDGE, :],
                jnp.concatenate([keys[n], masks[n]], 1),
                with_ones(values[n]),
            )
            mixed_ref[rows, lo] = om_ref[rows, lo] + mixed
            total_ref[rows, lo] = ot_ref[rows, lo] + total


def gathered(own, coarse, band, lanes):
    left, right = before_after("lon", *coarse, slice(None), lanes)
    top, bottom = before_after("lat", *band, slice(None), lanes)
    pad = jnp.zeros((COARSE_COUNT - 3 * len(BAND), LANES), BF16)
    return jnp.concatenate([own[:, lanes], left, right, top, bottom, pad], 0)


def coarse_kernel(q_ref, own_ref, c0_ref, c1_ref, b0_ref, b1_ref, chosen_ref, mask_ref, out_ref):
    is_top, is_bottom = pole_flags()
    band = len(BAND)
    mask = [
        mask_ref[:band, :],
        close_edge(mask_ref[band : 2 * band, :], is_top),
        close_edge(mask_ref[2 * band :, :], is_bottom),
    ]
    mask = jnp.concatenate(mask, 0)
    chosen = chosen_ref[...]
    for pair in range(PAIRS):
        lo = slice(pair * LANES, (pair + 1) * LANES)
        hi = slice((pair + PAIRS) * LANES, (pair + PAIRS + 1) * LANES)
        keys = jnp.concatenate([gathered(own_ref, (c0_ref, c1_ref), (b0_ref, b1_ref), lo), mask], 1)
        values = with_ones(gathered(own_ref, (c0_ref, c1_ref), (b0_ref, b1_ref), hi))
        left, right = before_after("lon", c0_ref, c1_ref, slice(32, 48), lo)
        queries = jnp.concatenate([q_ref[:, lo], left, right], 0)
        out_ref[:, lo] = exact_softmax(queries, chosen, keys, values).astype(BF16)


def late_cross_kernel(q_ref, oc_ref, lc_ref, ckv_ref, c0_ref, c1_ref, b0_ref, b1_ref, late_ref, cross_ref):
    late = late_ref[pole_table()]
    coarse = (ckv_ref, (c0_ref, c1_ref), (b0_ref, b1_ref))
    for pair in range(PAIRS):
        lo, hi = low(pair), high(pair)
        up_keys, up_values = raise_pair(late, gathered(*coarse, lo), gathered(*coarse, hi))
        for first in range(0, q_ref.shape[0], CROSS_ROWS):
            rows = slice(first, first + CROSS_ROWS)
            mixed, total = plain_softmax(q_ref[rows, lo], None, up_keys, up_values)
            cross_ref[rows, lo] = settled(oc_ref[rows, lo] + mixed, lc_ref[rows, lo] + total)


def late_kernel(
    q_ref, mixed_ref, total_ref, cross_ref, l0_ref, l1_ref, att_ref,
    chosen_ref, mask_ref, up_ref, weight_ref,
    kv_hbm, f0_ref, f1_ref, r0_ref, r1_ref, ckv_ref, c0_ref, c1_ref, b0_ref, b1_ref,
    exact_chosen_hbm, exact_mask_hbm, early_hbm, late_hbm,
    out_ref, joined_ref, bad_ref,
    kv_ref, exact_chosen_ref, exact_mask_ref, early_ref, late_ref, sems,
):
    cells = q_ref.shape[0]
    closed = pole_flags()
    pole = pole_table()
    up = up_ref[pole]
    masks = [close_edge(mask_ref[n * LATE_ROWS : (n + 1) * LATE_ROWS, :], closed[n]) for n in range(2)]
    corner = RADIUS * GROUP
    bad = jnp.zeros((8, LANES), F32)

    def raised_att(group, count):
        lanes = slice(group * LANES, (group + count) * LANES)
        if count == 1:
            lanes = low(group)
        top, bottom = before_after("lat", l0_ref, l1_ref, slice(64, 96), lanes)
        return dot(up, jnp.concatenate([att_ref[:, lanes], top, bottom], 0))

    def cornered(sums, part):
        west, east = part[:corner].reshape(-1, GROUP, LANES), part[corner:].reshape(-1, GROUP, LANES)
        rows = sums.reshape(-1, COLS, LANES)
        rows = jnp.concatenate(
            [rows[:, :GROUP] + west, rows[:, GROUP : COLS - GROUP], rows[:, COLS - GROUP :] + east], 1
        )
        return rows.reshape(-1, LANES)

    raised = [raised_att(pair, 2) for pair in range(0, PAIRS, 2)]
    for pair in range(PAIRS):
        lo, hi = low(pair), high(pair)
        corner_keys = before_after("lat", l0_ref, l1_ref, slice(None), lo)
        corner_values = before_after("lat", l0_ref, l1_ref, slice(None), hi)
        lift = raised[pair // 2][:, pair % 2 * LANES : (pair % 2 + 1) * LANES]
        inner = slice(EDGE, cells - EDGE)
        pieces = [(inner, mixed_ref[inner, lo], total_ref[inner, lo])]
        for n, first in enumerate((0, cells - EDGE)):
            rows = slice(first, first + EDGE)
            queries = q_ref[rows, lo]
            queries = jnp.concatenate([columns(queries, 0), columns(queries, COLS - GROUP)], 0)
            keys = jnp.concatenate([corner_keys[n], masks[n]], 1)
            chosen = chosen_ref[2 * n * corner : 2 * (n + 1) * corner, :]
            mixed, total = plain_softmax(queries, chosen, keys, with_ones(corner_values[n]))
            pieces.append((rows, cornered(mixed_ref[rows, lo], mixed), cornered(total_ref[rows, lo], total)))
        for rows, mixed, total in pieces:
            fine = settled(mixed, total).astype(BF16).astype(F32)
            joined = fine + cross_ref[rows, lo] + lift[rows]
            joined_ref[pair, rows, :] = joined.astype(BF16)
            bad += jnp.sum(joined.reshape(-1, 8, LANES) * 0.0, 0)
    bad_ref[...] = bad

    @pl.when(jnp.logical_not(jnp.sum(bad_ref[...]) == 0.0))
    def _():
        fetch(
            [(kv_hbm, kv_ref), (exact_chosen_hbm, exact_chosen_ref), (exact_mask_hbm, exact_mask_ref),
             (early_hbm, early_ref), (late_hbm, late_ref)],
            sems,
        )
        coarse = (ckv_ref, (c0_ref, c1_ref), (b0_ref, b1_ref))
        early, late = early_ref[...], late_ref[pole]
        count = len(EXACT_KEYS)
        edges = [cells + 2 * SIDE, cells + 2 * SIDE + EDGE + LATE_ROWS, count]

        @pl.loop(0, PAIRS)
        def _(pair):
            def all_of(lanes):
                left, right = before_after("lon", f0_ref, f1_ref, slice(None), lanes)
                top, bottom = before_after("lat", r0_ref, r1_ref, slice(None), lanes)
                late_top, late_bottom = before_after("lat", l0_ref, l1_ref, slice(None), lanes)
                return jnp.concatenate(
                    [kv_ref[:, lanes], left, right, top, late_top, bottom, late_bottom], 0
                )

            def up_of(lanes):
                first = dot(early, ckv_ref[:, lanes]).astype(BF16)
                return jnp.concatenate([first, dot(late, gathered(*coarse, lanes)).astype(BF16)], 0)

            lo, hi = low(pair), high(pair)
            keys, values = all_of(lo), with_ones(all_of(hi))
            up_keys, up_values = up_of(lo), with_ones(up_of(hi))
            raised = raised_att(pair, 1)
            for block in range(BLOCKS):
                mask = exact_mask_ref[block * count : (block + 1) * count, :]
                mask = [mask[: edges[0]]] + [
                    close_edge(mask[edges[n] : edges[n + 1]], closed[n]) for n in range(2)
                ]
                rows = slice(block * BLOCK, (block + 1) * BLOCK)
                queries = q_ref[rows, lo]
                fine = exact_softmax(
                    queries,
                    exact_chosen_ref[rows, :],
                    jnp.concatenate([keys, jnp.concatenate(mask, 0)], 1),
                    values,
                )
                cross = exact_softmax(queries, None, up_keys, up_values)
                joined = fine.astype(BF16).astype(F32) + cross + raised[rows, :]
                joined_ref[pair, rows, :] = joined.astype(BF16)

    joined = jnp.concatenate([joined_ref[n] for n in range(PAIRS)], 1)
    out_ref[...] = dot(joined, weight_ref[...]).astype(BF16)


def constant(table):
    return jnp.asarray(table, BF16)


def call(kernel, name, outs, operands, flops, hbm=(), scratch=(), vmem=28, aliases={}):
    near = pl.BlockSpec(memory_space=pltpu.VMEM)
    far = pl.BlockSpec(memory_space=pltpu.HBM)
    moved_bytes = sum(x.size * x.dtype.itemsize for x in list(operands) + list(outs))
    return pl.pallas_call(
        kernel,
        in_specs=[far if n in hbm else near for n in range(len(operands))],
        out_specs=[near] * len(outs),
        out_shape=list(outs),
        scratch_shapes=list(scratch),
        input_output_aliases=dict(aliases),
        compiler_params=pltpu.CompilerParams(vmem_limit_bytes=vmem << 20),
        cost_estimate=pl.CostEstimate(
            flops=int(flops), bytes_accessed=int(moved_bytes), transcendentals=int(flops / 1000)
        ),
        name=name,
    )(*operands)


def swap(array, above):
    size = lax.axis_size("lon")
    pairs = [(i, (i + 1) % size) for i in range(0 if above else 1, size, 2)]
    return lax.ppermute(array, "lon", pairs + [(b, a) for a, b in pairs])


def shift(array, step):
    size = lax.axis_size("lat")
    return lax.ppermute(array, "lat", [(i, (i + step) % size) for i in range(size)])


def ring(southward, northward):
    return shift(southward, 1), shift(northward, -1)


def shards(fine_query, fine_keyval, coarse_query, coarse_keyval, out_weight):
    channels = fine_query.shape[-1]
    cells = ROWS * COLS
    fq = fine_query.reshape(cells, channels)
    fkv = fine_keyval.reshape(cells, 2 * channels)
    cq = coarse_query.reshape(-1, channels)
    ckv = coarse_keyval.reshape(-1, 2 * channels)
    half = lambda rows: jax.ShapeDtypeStruct((rows, channels), BF16)
    full = lambda rows: jax.ShapeDtypeStruct((rows, 2 * channels), BF16)
    state = lambda rows: jax.ShapeDtypeStruct((rows, channels), F32)
    after = lax.optimization_barrier

    c0, c1 = call(
        send_coarse_kernel, "send_coarse", [full(48)] * 2, [ckv, cq], 1e10, hbm=range(2),
        scratch=[pltpu.VMEM(ckv.shape, BF16), pltpu.VMEM(cq.shape, BF16), pltpu.SemaphoreType.DMA((2,))],
        vmem=8,
    )
    coarse0, coarse1 = swap(c0, True), swap(c1, False)
    near_kv, _ = after((fkv, c0))
    f0, f1, r0, r1 = call(
        send_fine_kernel, "send_fine", [full(SIDE)] * 2 + [full(EDGE)] * 2, [near_kv, constant(PICK_FINE)], 5e9
    )
    edge0 = shift(r0, 1)
    side0 = swap(f0, True)
    f1, coarse0, coarse1, r0 = after((f1, coarse0, coarse1, r0))
    coarse = (coarse0, coarse1)
    sides = (side0, swap(f1, False))
    ckv, _ = after((ckv, f1))
    (band,) = call(send_band_kernel, "send_band", [full(len(BAND))], [ckv, *coarse], 1e6)
    bands = ring(band, band)
    fq, near_kv, _ = after((fq, near_kv, band))
    own = call(
        own_kernel, "own", [state(cells)] * 2, [fq, near_kv, constant(OWN_CHOSEN), constant(OWN_MASK)], 5e9
    )
    fq, own = after((fq, own))
    early = call(early_cross_kernel, "early_cross", [state(cells)] * 2, [fq, ckv, constant(UP_EARLY)], 5e9)
    bands, early, r1 = after((bands, early, r1))
    edges = (edge0, shift(r1, -1))
    (coarse_att,) = call(
        coarse_kernel, "coarse", [half(len(COARSE_QUERIES))],
        [cq, ckv, *coarse, *bands, constant(COARSE_CHOSEN), constant(COARSE_MASK)], 2e9,
    )
    late0, late1 = call(
        send_late_kernel, "send_late", [full(LATE_ROWS)] * 2,
        [*sides, coarse_att] + [constant(table) for table in LATE_PICKS], 2e8,
    )
    lates = ring(late0, late1)
    fq, _ = after((fq, late0))
    (cross,) = call(
        late_cross_kernel, "late_cross", [state(cells)], [fq, *early, ckv, *coarse, *bands, constant(UP_LATE)], 4e9
    )
    fq, cross = after((fq, cross))
    sums = call(
        lon_kernel, "lon_strips", [state(cells)] * 2,
        [fq, *sides, constant(LON_CHOSEN), constant(LON_MASK), *own], 1e8, aliases={5: 0, 6: 1},
    )
    fq, sums, _ = after((fq, sums, cross))
    sums = call(
        lat_kernel, "lat_strips", [state(cells)] * 2,
        [fq, *edges, constant(LAT_CHOSEN), constant(LAT_MASK), *sums], 1e8, aliases={5: 0, 6: 1},
    )
    exact = [constant(table) for table in (EXACT_CHOSEN, EXACT_MASK, UP_EARLY, UP_LATE)]
    (out,) = call(
        late_kernel, "late", [half(cells)],
        [fq, *sums, cross, *lates, coarse_att, constant(CORNER_CHOSEN),
         constant(CORNER_MASK), constant(UP_ATT), out_weight,
         near_kv, *sides, *edges, ckv, *coarse, *bands, *exact],
        3e9,
        hbm=(11, 21, 22, 23, 24),
        scratch=[
            pltpu.VMEM((PAIRS, cells, LANES), BF16), pltpu.VMEM((8, LANES), F32),
            pltpu.VMEM((cells, 2 * channels), BF16),
            *[pltpu.VMEM(x.shape, BF16) for x in exact], pltpu.SemaphoreType.DMA((5,)),
        ],
    )
    return out.reshape(ROWS, COLS, channels)


def solution(mesh):
    tiled = P("lat", "lon", None)
    return jax.shard_map(
        shards, mesh=mesh, in_specs=(tiled,) * 4 + (P(),), out_specs=tiled, check_vma=False
    )
```

```python
import math

import jax
import jax.numpy as jnp
import numpy as np
from jax import lax
from jax.experimental import pallas as pl
from jax.experimental.pallas import tpu as pltpu
from jax.sharding import PartitionSpec as P

HEADS = 8
RADIUS = 6
FACTOR = 4
ROWS, COLS = 24, 32
CROWS, CCOLS = 6, 8
LANES = 128
BLOCK_ROWS = 8
BLOCKS = ROWS // BLOCK_ROWS
BLOCK = BLOCK_ROWS * COLS
MASKED = -16384.0
EXPONENT = 0.125 * math.log2(math.e)
F32 = jnp.float32
BF16 = jnp.bfloat16


ROW_ORDER = list(range(2, 22)) + [0, 1, 22, 23]
LEFT_FINE = [(r, c - RADIUS) for r in ROW_ORDER for c in range(RADIUS)]
RIGHT_FINE = [(r, COLS + c) for r in ROW_ORDER for c in range(RADIUS)]
CORNER_TOP = list(range(0, 24)) + list(range(120, 132))
CORNER_BOTTOM = list(range(96, 120)) + list(range(132, 144))
CORNERS = 36
LATE_ROWS = 80
ATT_ROWS = 64


OWN_BLOCKS = [((0, 10), (0, 16)), ((10, 14), (4, 20)), ((14, 24), (8, 24))]


def corner_keys(top):
    picks = CORNER_BOTTOM if top else CORNER_TOP
    shift = -ROWS if top else ROWS
    keys = [(LEFT_FINE[i][0] + shift, LEFT_FINE[i][1]) for i in picks]
    keys += [(RIGHT_FINE[i][0] + shift, RIGHT_FINE[i][1]) for i in picks]
    return keys + [None] * (LATE_ROWS - len(keys))


def mask_lanes(keys, rows, cols):
    table = np.zeros((len(keys), LANES), np.float32)
    for n, key in enumerate(keys):
        if key is None:
            table[n, : len(rows) + len(cols)] = MASKED
            continue
        for i, row in enumerate(rows):
            if abs(key[0] - row) > RADIUS:
                table[n, i] = MASKED
        for j, col in enumerate(cols):
            if abs(key[1] - col) > RADIUS:
                table[n, len(rows) + j] = MASKED
    return table


def chosen_lanes(queries, rows, cols):
    table = np.zeros((len(queries), LANES), np.float32)
    for n, query in enumerate(queries):
        if query is None:
            continue
        table[n, rows.index(query[0])] = 1.0
        table[n, len(rows) + cols.index(query[1])] = 1.0
        table[n, LANES - 1] = 1.0
    return table


def cells_of(rows, cols):
    return [(r, c) for r in rows for c in cols]


FINE_COLS = list(range(COLS))
EDGE = RADIUS * COLS
GROUP = 8
WEST_COLS, EAST_COLS = list(range(GROUP)), list(range(COLS - GROUP, COLS))
ALL_ROWS = list(range(ROWS))
TOP_ROWS, BOTTOM_ROWS = list(range(RADIUS)), list(range(ROWS - RADIUS, ROWS))
TOP_FINE = cells_of(range(-RADIUS, 0), range(COLS))
BOTTOM_FINE = cells_of(range(ROWS, ROWS + RADIUS), range(COLS))
OWN_FINE = cells_of(ALL_ROWS, FINE_COLS)


def tables_of(queries, keys):
    rows = sorted({q[0] for q in queries})
    cols = sorted({q[1] for q in queries})
    return chosen_lanes(queries, rows, cols), mask_lanes(keys, rows, cols)


def stacked(pairs):
    made = [tables_of(*pair) for pair in pairs]
    return [np.concatenate(tables) for tables in zip(*made)]


OWN_CHOSEN, OWN_MASK = stacked(
    [
        (cells_of(range(*q), FINE_COLS), cells_of(range(*k), FINE_COLS))
        for q, k in OWN_BLOCKS
    ]
)
LON_CHOSEN, LON_MASK = stacked(
    [
        (cells_of(ALL_ROWS, WEST_COLS), LEFT_FINE),
        (cells_of(ALL_ROWS, EAST_COLS), RIGHT_FINE),
    ]
)
LAT_CHOSEN, LAT_MASK = stacked(
    [
        (cells_of(TOP_ROWS, FINE_COLS), TOP_FINE),
        (cells_of(BOTTOM_ROWS, FINE_COLS), BOTTOM_FINE),
    ]
)
CORNER_CHOSEN, CORNER_MASK = stacked(
    [
        (cells_of(TOP_ROWS, WEST_COLS) + cells_of(TOP_ROWS, EAST_COLS), corner_keys(True)),
        (cells_of(BOTTOM_ROWS, WEST_COLS) + cells_of(BOTTOM_ROWS, EAST_COLS), corner_keys(False)),
    ]
)
EXACT_KEYS = (
    OWN_FINE + LEFT_FINE + RIGHT_FINE + TOP_FINE + corner_keys(True) + BOTTOM_FINE + corner_keys(False)
)
EXACT_CHOSEN, EXACT_MASK = stacked(
    [
        (cells_of(range(b * BLOCK_ROWS, (b + 1) * BLOCK_ROWS), FINE_COLS), EXACT_KEYS)
        for b in range(BLOCKS)
    ]
)

CQ_COLS = list(range(-1, CCOLS + 1))
OWN_COARSE = [(r, c) for r in range(CROWS) for c in range(CCOLS)]
LEFT_COARSE = [(r, c - 7) for r in range(CROWS) for c in range(7)] + [None] * CROWS
RIGHT_COARSE = [(r, c + CCOLS) for r in range(CROWS) for c in range(7)] + [None] * CROWS
BAND = OWN_COARSE + LEFT_COARSE + RIGHT_COARSE


def moved(keys, rows):
    return [None if key is None else (key[0] + rows, key[1]) for key in keys]


COARSE_KEYS = BAND + moved(BAND, -CROWS) + moved(BAND, CROWS)
COARSE_COUNT = 512
COARSE_KEYS = COARSE_KEYS + [None] * (COARSE_COUNT - len(COARSE_KEYS))
COARSE_QUERIES = (
    OWN_COARSE
    + [None] * 10
    + [(r, -1) for r in range(CROWS)]
    + [None] * 10
    + [(r, CCOLS) for r in range(CROWS)]
)
COARSE_CHOSEN = chosen_lanes(COARSE_QUERIES, list(range(CROWS)), CQ_COLS)
COARSE_MASK = mask_lanes(COARSE_KEYS, list(range(CROWS)), CQ_COLS)
LATE_CELLS_OF_ROW = [(0, c) for c in range(CCOLS)] + [(0, -1), (0, CCOLS)]


def late_cells(part):
    cells = LATE_CELLS_OF_ROW[part::2]
    before = 2 * CORNERS - ATT_ROWS
    return [None] * before + cells + [None] * (LATE_ROWS - ATT_ROWS - before - len(cells))


LATE_ATT = late_cells(0) + late_cells(1)
ATT_CELLS = COARSE_QUERIES + moved(LATE_ATT, -1) + moved(LATE_ATT, CROWS)


def coefficient(fine):
    coarse, offset = fine // FACTOR, (fine % FACTOR - 1.5) / FACTOR
    taps = {coarse: 1.0 - abs(offset)}
    taps[coarse + (1 if offset > 0 else -1)] = abs(offset)
    return taps


def up_table(fine_cells, coarse_cells, pole):
    where = {cell: n for n, cell in reversed(list(enumerate(coarse_cells))) if cell is not None}
    table = np.zeros((len(fine_cells), len(coarse_cells)), np.float32)
    for n, (row, col) in enumerate(fine_cells):
        for r, a in coefficient(row).items():
            if pole == "top":
                r = max(r, 0)
            if pole == "bottom":
                r = min(r, CROWS - 1)
            for c, b in coefficient(col).items():
                table[n, where[(r, c)]] += a * b
    return table


def poles(fine_cells, coarse_cells):
    return np.stack([up_table(fine_cells, coarse_cells, p) for p in ("none", "top", "bottom")])


FINE_CELLS = [(r, c) for r in range(ROWS) for c in range(COLS)]
INNER = [(r, c) for r in range(2, ROWS - 2) for c in range(2, COLS - 2)]
EARLY_COUNT = 512
EARLY_CELLS = INNER[:EARLY_COUNT]
LATE_CELLS = [cell for cell in FINE_CELLS if cell not in set(EARLY_CELLS)]
UP_EARLY = up_table(EARLY_CELLS, OWN_COARSE, "none")
UP_LATE = poles(LATE_CELLS, COARSE_KEYS)
UP_ATT = poles(FINE_CELLS, ATT_CELLS)


def picked(indices, count):
    table = np.zeros((len(indices), count), np.float32)
    for n, index in enumerate(indices):
        if index is not None:
            table[n, index] = 1.0
    return table


FINE_EAST = [r * COLS + COLS - RADIUS + c for r in ROW_ORDER for c in range(RADIUS)]
FINE_WEST = [r * COLS + c for r in ROW_ORDER for c in range(RADIUS)]
PICK_FINE = picked(FINE_EAST + FINE_WEST, ROWS * COLS)
PICK_COARSE = picked(
    [r * CCOLS + 1 + c for r in range(CROWS) for c in range(7)]
    + [None] * CROWS
    + [r * CCOLS + c for r in range(CROWS) for c in range(7)]
    + [None] * CROWS,
    CROWS * CCOLS,
)
PICK_QUERY = picked(
    [None] * 42
    + [r * CCOLS + CCOLS - 1 for r in range(CROWS)]
    + [None] * 42
    + [r * CCOLS for r in range(CROWS)],
    CROWS * CCOLS,
)
SIDE = len(ROW_ORDER) * RADIUS


def late_picks(corner, row):
    rest = LATE_ROWS - 2 * CORNERS
    left = picked(list(corner) + [None] * (CORNERS + rest), SIDE)
    right = picked([None] * CORNERS + list(corner) + [None] * rest, SIDE)
    tables = [left, right]
    for part in range(2):
        cells = moved(late_cells(part), row)
        att = [None if cell is None else COARSE_QUERIES.index(cell) for cell in cells]
        tables.append(picked([None] * ATT_ROWS + att, len(COARSE_QUERIES)))
    return tables


LATE_PICKS = [
    np.concatenate(tables)
    for tables in zip(late_picks(CORNER_BOTTOM, CROWS - 1), late_picks(CORNER_TOP, 0))
]


PAIRS = HEADS // 2
LEAST, MOST = 2.0**-80, 2.0**100


def halves():
    return lax.broadcasted_iota(jnp.int32, (1, LANES), 1) < LANES // 2


def head_of(pair, head):
    return jnp.where(halves() == (head == 0), pair, jnp.zeros((), pair.dtype))


def packed(first, second):
    return jnp.where(halves(), first, second)


def dot(a, b):
    return jnp.dot(a, b, preferred_element_type=F32)


def scores(queries, keys):
    return lax.dot_general(queries, keys, (((1,), (1,)), ((), ())), preferred_element_type=F32)


def mix(weights, values):
    mixed = dot(weights.astype(BF16), values)
    return mixed[:, :LANES], mixed[:, LANES:]


def with_ones(values):
    return jnp.concatenate([values, jnp.ones_like(values)], 1)


def even(axis):
    return lax.axis_index(axis) % 2 == 0


def pole_flags():
    lat = lax.axis_index("lat")
    return lat == 0, lat == lax.axis_size("lat") - 1


def pole_table():
    is_top, is_bottom = pole_flags()
    return jnp.where(is_top, 1, jnp.where(is_bottom, 2, 0))


def lanes_of(group):
    if isinstance(group, int):
        return slice(group * LANES, (group + 1) * LANES)
    return pl.ds(pl.multiple_of(group * LANES, LANES), LANES)


def low(pair):
    return lanes_of(pair)


def high(pair):
    return lanes_of(pair + PAIRS)


def close_edge(mask, closed):
    lane = lax.broadcasted_iota(jnp.int32, (1, LANES), 1)
    return jnp.where((lane == LANES - 1) & closed, MASKED, mask.astype(F32)).astype(BF16)


def before_after(axis, first, second, *index):
    a, b = first[index], second[index]
    if axis == "lat":
        return a, b
    return jnp.where(even(axis), b, a), jnp.where(even(axis), a, b)


def both_heads(queries, chosen):
    rows = jnp.concatenate([head_of(queries, 0), head_of(queries, 1)], 0)
    if chosen is None:
        return rows
    return jnp.concatenate([rows, jnp.concatenate([chosen, chosen], 0)], 1)


def plain_softmax(queries, chosen, keys, values):
    count = queries.shape[0]
    mixed, total = mix(jnp.exp2(scores(both_heads(queries, chosen), keys) * EXPONENT), values)
    return packed(mixed[:count], mixed[count:]), packed(total[:count], total[count:])


def exact_softmax(queries, chosen, keys, values):
    count = queries.shape[0]
    score = scores(both_heads(queries, chosen), keys)
    score = score - jnp.max(score, 1, keepdims=True)
    mixed, total = mix(jnp.exp2(score * EXPONENT), values)
    result = mixed / total
    return packed(result[:count], result[count:])


def settled(mixed, total):
    fits = (total > LEAST) & (total < MOST)
    return jnp.where(fits, mixed / total, jnp.nan)


def fetch(moves, sems):
    copies = [pltpu.make_async_copy(a, b, sems.at[n]) for n, (a, b) in enumerate(moves)]
    for copy in copies:
        copy.start()
    for copy in copies:
        copy.wait()


def send_coarse_kernel(both_ref, c0_ref, c1_ref):
    channels = both_ref.shape[1] // 3
    n = lax.broadcasted_iota(jnp.int32, (48, CROWS * CCOLS), 0)
    cell = lax.broadcasted_iota(jnp.int32, (48, CROWS * CCOLS), 1)
    row = (n * 37) >> 8
    sides = []
    for first, col in ((1, CCOLS - 1), (0, 0)):
        keyval = (n < 42) & (cell == row * CCOLS + first + n - row * 7)
        query = (n >= 42) & (cell == (n - 42) * CCOLS + col)
        both = dot(keyval.astype(F32).astype(BF16), both_ref[:, : 2 * channels])
        query = dot(query.astype(F32).astype(BF16), both_ref[:, 2 * channels :])
        sides.append(jnp.concatenate([both[:, :channels] + query, both[:, channels:]], 1).astype(BF16))
    eastward = even("lon")
    c0_ref[...] = jnp.where(eastward, sides[0], sides[1])
    c1_ref[...] = jnp.where(eastward, sides[1], sides[0])


def send_fine_kernel(fkv_ref, pick_ref, f0_ref, f1_ref, r0_ref, r1_ref):
    cells = fkv_ref.shape[0]
    fine = dot(pick_ref[...], fkv_ref[...]).astype(BF16)
    eastward = even("lon")
    f0_ref[...] = jnp.where(eastward, fine[:SIDE], fine[SIDE:])
    f1_ref[...] = jnp.where(eastward, fine[SIDE:], fine[:SIDE])
    r0_ref[...] = fkv_ref[cells - EDGE :, :]
    r1_ref[...] = fkv_ref[:EDGE, :]


def send_band_kernel(ckv_ref, c0_ref, c1_ref, band_ref):
    left, right = before_after("lon", c0_ref, c1_ref, slice(None), slice(None))
    band_ref[0:48, :] = ckv_ref[...]
    band_ref[48:96, :] = left
    band_ref[96:144, :] = right


def send_late_kernel(f0_ref, f1_ref, att_ref, pl_ref, pr_ref, pa_ref, pb_ref, l0_ref, l1_ref):
    left, right = before_after("lon", f0_ref, f1_ref, slice(None), slice(None))
    sides = dot(pl_ref[...], left) + dot(pr_ref[...], right)
    att = jnp.concatenate([dot(pa_ref[...], att_ref[...]), dot(pb_ref[...], att_ref[...])], 1)
    late = (sides + att).astype(BF16)
    l0_ref[...], l1_ref[...] = late[:LATE_ROWS], late[LATE_ROWS:]


def own_kernel(q_ref, kv_ref, chosen_ref, mask_ref, mixed_ref, total_ref):
    for pair in range(PAIRS):
        lo, hi = low(pair), high(pair)
        at = 0
        for (q0, q1), (k0, k1) in OWN_BLOCKS:
            rows = slice(q0 * COLS, q1 * COLS)
            near = slice(k0 * COLS, k1 * COLS)
            mask = mask_ref[at : at + (k1 - k0) * COLS, :]
            at += (k1 - k0) * COLS
            keys = jnp.concatenate([kv_ref[near, lo], mask], 1)
            mixed_ref[rows, lo], total_ref[rows, lo] = plain_softmax(
                q_ref[rows, lo], chosen_ref[rows, :], keys, with_ones(kv_ref[near, hi])
            )


CROSS_ROWS = 768


def raise_pair(table, keys, values):
    both = dot(table, jnp.concatenate([keys, values], 1)).astype(BF16)
    return both[:, :LANES], with_ones(both[:, LANES:])


def early_cross_kernel(q_ref, ckv_ref, up_ref, mixed_ref, total_ref):
    up = up_ref[...]
    raised = [raise_pair(up, ckv_ref[:, low(pair)], ckv_ref[:, high(pair)]) for pair in range(PAIRS)]
    for pair in range(PAIRS):
        lo = low(pair)
        up_keys, up_values = raised[pair]
        for first in range(0, q_ref.shape[0], CROSS_ROWS):
            rows = slice(first, first + CROSS_ROWS)
            mixed_ref[rows, lo], total_ref[rows, lo] = plain_softmax(
                q_ref[rows, lo], None, up_keys, up_values
            )


def columns(queries, first):
    rows = queries.shape[0] // COLS
    split = queries.astype(F32).reshape(rows, COLS, LANES)[:, first : first + GROUP]
    return split.reshape(rows * GROUP, LANES).astype(BF16)


def lon_kernel(q_ref, f0_ref, f1_ref, chosen_ref, mask_ref, om_ref, ot_ref, mixed_ref, total_ref):
    strip = ROWS * GROUP
    for pair in range(PAIRS):
        lo, hi = low(pair), high(pair)
        keys = before_after("lon", f0_ref, f1_ref, slice(None), lo)
        values = before_after("lon", f0_ref, f1_ref, slice(None), hi)
        queries = q_ref[:, lo]
        for n, first in enumerate((0, COLS - GROUP)):
            mixed, total = plain_softmax(
                columns(queries, first),
                chosen_ref[n * strip : (n + 1) * strip, :],
                jnp.concatenate([keys[n], mask_ref[n * SIDE : (n + 1) * SIDE, :]], 1),
                with_ones(values[n]),
            )
            for row in range(ROWS):
                at = slice(row * COLS + first, row * COLS + first + GROUP)
                piece = slice(row * GROUP, (row + 1) * GROUP)
                mixed_ref[at, lo] = om_ref[at, lo] + mixed[piece]
                total_ref[at, lo] = ot_ref[at, lo] + total[piece]


def lat_kernel(q_ref, r0_ref, r1_ref, chosen_ref, mask_ref, om_ref, ot_ref, mixed_ref, total_ref):
    cells = q_ref.shape[0]
    closed = pole_flags()
    masks = [close_edge(mask_ref[n * EDGE : (n + 1) * EDGE, :], closed[n]) for n in range(2)]
    for pair in range(PAIRS):
        lo, hi = low(pair), high(pair)
        keys = before_after("lat", r0_ref, r1_ref, slice(None), lo)
        values = before_after("lat", r0_ref, r1_ref, slice(None), hi)
        for n, first in enumerate((0, cells - EDGE)):
            rows = slice(first, first + EDGE)
            mixed, total = plain_softmax(
                q_ref[rows, lo],
                chosen_ref[n * EDGE : (n + 1) * EDGE, :],
                jnp.concatenate([keys[n], masks[n]], 1),
                with_ones(values[n]),
            )
            mixed_ref[rows, lo] = om_ref[rows, lo] + mixed
            total_ref[rows, lo] = ot_ref[rows, lo] + total


def gathered(own, coarse, band, lanes):
    left, right = before_after("lon", *coarse, slice(None), lanes)
    top, bottom = before_after("lat", *band, slice(None), lanes)
    pad = jnp.zeros((COARSE_COUNT - 3 * len(BAND), LANES), BF16)
    return jnp.concatenate([own[:, lanes], left, right, top, bottom, pad], 0)


def coarse_kernel(q_ref, own_ref, c0_ref, c1_ref, b0_ref, b1_ref, chosen_ref, mask_ref, out_ref):
    is_top, is_bottom = pole_flags()
    band = len(BAND)
    mask = [
        mask_ref[:band, :],
        close_edge(mask_ref[band : 2 * band, :], is_top),
        close_edge(mask_ref[2 * band :, :], is_bottom),
    ]
    mask = jnp.concatenate(mask, 0)
    chosen = chosen_ref[...]
    for pair in range(PAIRS):
        lo = slice(pair * LANES, (pair + 1) * LANES)
        hi = slice((pair + PAIRS) * LANES, (pair + PAIRS + 1) * LANES)
        keys = jnp.concatenate([gathered(own_ref, (c0_ref, c1_ref), (b0_ref, b1_ref), lo), mask], 1)
        values = with_ones(gathered(own_ref, (c0_ref, c1_ref), (b0_ref, b1_ref), hi))
        left, right = before_after("lon", c0_ref, c1_ref, slice(32, 48), lo)
        queries = jnp.concatenate([q_ref[:, lo], left, right], 0)
        out_ref[:, lo] = exact_softmax(queries, chosen, keys, values).astype(BF16)


def late_cross_kernel(q_ref, oc_ref, lc_ref, ckv_ref, c0_ref, c1_ref, b0_ref, b1_ref, late_ref, cross_ref):
    late = late_ref[pole_table()]
    coarse = (ckv_ref, (c0_ref, c1_ref), (b0_ref, b1_ref))
    raised = [
        raise_pair(late, gathered(*coarse, low(pair)), gathered(*coarse, high(pair))) for pair in range(PAIRS)
    ]
    for pair in range(PAIRS):
        lo = low(pair)
        up_keys, up_values = raised[pair]
        for first in range(0, q_ref.shape[0], CROSS_ROWS):
            rows = slice(first, first + CROSS_ROWS)
            mixed, total = plain_softmax(q_ref[rows, lo], None, up_keys, up_values)
            cross_ref[rows, lo] = settled(oc_ref[rows, lo] + mixed, lc_ref[rows, lo] + total)


def late_kernel(
    q_ref, mixed_ref, total_ref, cross_ref, l0_ref, l1_ref, att_ref,
    chosen_ref, mask_ref, up_ref, weight_ref,
    kv_hbm, f0_ref, f1_ref, r0_ref, r1_ref, ckv_ref, c0_ref, c1_ref, b0_ref, b1_ref,
    exact_chosen_hbm, exact_mask_hbm, early_hbm, late_hbm,
    out_ref, joined_ref, bad_ref,
    kv_ref, exact_chosen_ref, exact_mask_ref, early_ref, late_ref, sems,
):
    cells = q_ref.shape[0]
    closed = pole_flags()
    pole = pole_table()
    up = up_ref[pole]
    masks = [close_edge(mask_ref[n * LATE_ROWS : (n + 1) * LATE_ROWS, :], closed[n]) for n in range(2)]
    corner = RADIUS * GROUP
    bad = jnp.zeros((8, LANES), F32)

    def raised_att(group, count):
        lanes = [slice((n + group) * LANES, (n + group + count) * LANES) for n in (0, PAIRS)]
        if count == 1:
            lanes = [low(group), high(group)]
        tops, bottoms = zip(*[before_after("lat", l0_ref, l1_ref, slice(ATT_ROWS, None), at) for at in lanes])
        return dot(up, jnp.concatenate([att_ref[:, lanes[0]], *tops, *bottoms], 0))

    def cornered(sums, part):
        west, east = part[:corner].reshape(-1, GROUP, LANES), part[corner:].reshape(-1, GROUP, LANES)
        rows = sums.reshape(-1, COLS, LANES)
        rows = jnp.concatenate(
            [rows[:, :GROUP] + west, rows[:, GROUP : COLS - GROUP], rows[:, COLS - GROUP :] + east], 1
        )
        return rows.reshape(-1, LANES)

    raised = [raised_att(pair, 2) for pair in range(0, PAIRS, 2)]
    for pair in range(PAIRS):
        lo, hi = low(pair), high(pair)
        corner_keys = before_after("lat", l0_ref, l1_ref, slice(None), lo)
        corner_values = before_after("lat", l0_ref, l1_ref, slice(None), hi)
        lift = raised[pair // 2][:, pair % 2 * LANES : (pair % 2 + 1) * LANES]
        inner = slice(EDGE, cells - EDGE)
        pieces = [(inner, mixed_ref[inner, lo], total_ref[inner, lo])]
        for n, first in enumerate((0, cells - EDGE)):
            rows = slice(first, first + EDGE)
            queries = q_ref[rows, lo]
            queries = jnp.concatenate([columns(queries, 0), columns(queries, COLS - GROUP)], 0)
            keys = jnp.concatenate([corner_keys[n], masks[n]], 1)
            chosen = chosen_ref[2 * n * corner : 2 * (n + 1) * corner, :]
            mixed, total = plain_softmax(queries, chosen, keys, with_ones(corner_values[n]))
            pieces.append((rows, cornered(mixed_ref[rows, lo], mixed), cornered(total_ref[rows, lo], total)))
        for rows, mixed, total in pieces:
            fine = settled(mixed, total).astype(BF16).astype(F32)
            joined = fine + cross_ref[rows, lo] + lift[rows]
            joined_ref[pair, rows, :] = joined.astype(BF16)
            bad += jnp.sum(joined.reshape(-1, 8, LANES) * 0.0, 0)
    bad_ref[...] = bad

    @pl.when(jnp.logical_not(jnp.sum(bad_ref[...]) == 0.0))
    def _():
        fetch(
            [(kv_hbm, kv_ref), (exact_chosen_hbm, exact_chosen_ref), (exact_mask_hbm, exact_mask_ref),
             (early_hbm, early_ref), (late_hbm, late_ref)],
            sems,
        )
        coarse = (ckv_ref, (c0_ref, c1_ref), (b0_ref, b1_ref))
        early, late = early_ref[...], late_ref[pole]
        count = len(EXACT_KEYS)
        edges = [cells + 2 * SIDE, cells + 2 * SIDE + EDGE + LATE_ROWS, count]

        @pl.loop(0, PAIRS)
        def _(pair):
            def all_of(lanes):
                left, right = before_after("lon", f0_ref, f1_ref, slice(None), lanes)
                top, bottom = before_after("lat", r0_ref, r1_ref, slice(None), lanes)
                late_top, late_bottom = before_after("lat", l0_ref, l1_ref, slice(None), lanes)
                return jnp.concatenate(
                    [kv_ref[:, lanes], left, right, top, late_top, bottom, late_bottom], 0
                )

            def up_of(lanes):
                first = dot(early, ckv_ref[:, lanes]).astype(BF16)
                return jnp.concatenate([first, dot(late, gathered(*coarse, lanes)).astype(BF16)], 0)

            lo, hi = low(pair), high(pair)
            keys, values = all_of(lo), with_ones(all_of(hi))
            up_keys, up_values = up_of(lo), with_ones(up_of(hi))
            raised = raised_att(pair, 1)
            for block in range(BLOCKS):
                mask = exact_mask_ref[block * count : (block + 1) * count, :]
                mask = [mask[: edges[0]]] + [
                    close_edge(mask[edges[n] : edges[n + 1]], closed[n]) for n in range(2)
                ]
                rows = slice(block * BLOCK, (block + 1) * BLOCK)
                queries = q_ref[rows, lo]
                fine = exact_softmax(
                    queries,
                    exact_chosen_ref[rows, :],
                    jnp.concatenate([keys, jnp.concatenate(mask, 0)], 1),
                    values,
                )
                cross = exact_softmax(queries, None, up_keys, up_values)
                joined = fine.astype(BF16).astype(F32) + cross + raised[rows, :]
                joined_ref[pair, rows, :] = joined.astype(BF16)

    joined = jnp.concatenate([joined_ref[n] for n in range(PAIRS)], 1)
    out_ref[...] = dot(joined, weight_ref[...]).astype(BF16)


def constant(table):
    return jnp.asarray(table, BF16)


def call(kernel, name, outs, operands, flops, hbm=(), scratch=(), vmem=28, aliases={}):
    near = pl.BlockSpec(memory_space=pltpu.VMEM)
    far = pl.BlockSpec(memory_space=pltpu.HBM)
    moved_bytes = sum(x.size * x.dtype.itemsize for x in list(operands) + list(outs))
    return pl.pallas_call(
        kernel,
        in_specs=[far if n in hbm else near for n in range(len(operands))],
        out_specs=[near] * len(outs),
        out_shape=list(outs),
        scratch_shapes=list(scratch),
        input_output_aliases=dict(aliases),
        compiler_params=pltpu.CompilerParams(vmem_limit_bytes=vmem << 20),
        cost_estimate=pl.CostEstimate(
            flops=int(flops), bytes_accessed=int(moved_bytes), transcendentals=int(flops / 1000)
        ),
        name=name,
    )(*operands)


def swap(array, above):
    size = lax.axis_size("lon")
    pairs = [(i, (i + 1) % size) for i in range(0 if above else 1, size, 2)]
    return lax.ppermute(array, "lon", pairs + [(b, a) for a, b in pairs])


def shift(array, step):
    size = lax.axis_size("lat")
    return lax.ppermute(array, "lat", [(i, (i + step) % size) for i in range(size)])


def ring(southward, northward):
    return shift(southward, 1), shift(northward, -1)


def shards(fine_query, fine_keyval, coarse_query, coarse_keyval, out_weight):
    channels = fine_query.shape[-1]
    cells = ROWS * COLS
    fq = fine_query.reshape(cells, channels)
    fkv = fine_keyval.reshape(cells, 2 * channels)
    cq = coarse_query.reshape(-1, channels)
    ckv = coarse_keyval.reshape(-1, 2 * channels)
    half = lambda rows: jax.ShapeDtypeStruct((rows, channels), BF16)
    full = lambda rows: jax.ShapeDtypeStruct((rows, 2 * channels), BF16)
    state = lambda rows: jax.ShapeDtypeStruct((rows, channels), F32)
    after = lax.optimization_barrier

    c0, c1 = call(
        send_coarse_kernel, "send_coarse", [full(48)] * 2, [jnp.concatenate([ckv, cq], 1)], 1e10, vmem=8
    )
    coarse0, coarse1 = swap(c0, True), swap(c1, False)
    near_kv, _ = after((fkv, c0))
    f0, f1, r0, r1 = call(
        send_fine_kernel, "send_fine", [full(SIDE)] * 2 + [full(EDGE)] * 2, [near_kv, constant(PICK_FINE)], 5e9
    )
    edge0 = shift(r0, 1)
    side0 = swap(f0, True)
    f1, coarse0, coarse1, r0 = after((f1, coarse0, coarse1, r0))
    coarse = (coarse0, coarse1)
    sides = (side0, swap(f1, False))
    ckv, _ = after((ckv, f1))
    (band,) = call(send_band_kernel, "send_band", [full(len(BAND))], [ckv, *coarse], 1e6)
    bands = ring(band, band)
    fq, near_kv, _ = after((fq, near_kv, band))
    own = call(
        own_kernel, "own", [state(cells)] * 2, [fq, near_kv, constant(OWN_CHOSEN), constant(OWN_MASK)], 5e9
    )
    fq, own = after((fq, own))
    early = call(early_cross_kernel, "early_cross", [state(cells)] * 2, [fq, ckv, constant(UP_EARLY)], 5e9)
    bands, early, r1 = after((bands, early, r1))
    edges = (edge0, shift(r1, -1))
    (coarse_att,) = call(
        coarse_kernel, "coarse", [half(len(COARSE_QUERIES))],
        [cq, ckv, *coarse, *bands, constant(COARSE_CHOSEN), constant(COARSE_MASK)], 2e9,
    )
    late0, late1 = call(
        send_late_kernel, "send_late", [full(LATE_ROWS)] * 2,
        [*sides, coarse_att] + [constant(table) for table in LATE_PICKS], 2e8,
    )
    lates = ring(late0, late1)
    fq, _ = after((fq, late0))
    (cross,) = call(
        late_cross_kernel, "late_cross", [state(cells)], [fq, *early, ckv, *coarse, *bands, constant(UP_LATE)], 4e9
    )
    fq, cross = after((fq, cross))
    sums = call(
        lon_kernel, "lon_strips", [state(cells)] * 2,
        [fq, *sides, constant(LON_CHOSEN), constant(LON_MASK), *own], 1e8, aliases={5: 0, 6: 1},
    )
    fq, sums, _ = after((fq, sums, cross))
    sums = call(
        lat_kernel, "lat_strips", [state(cells)] * 2,
        [fq, *edges, constant(LAT_CHOSEN), constant(LAT_MASK), *sums], 1e8, aliases={5: 0, 6: 1},
    )
    exact = [constant(table) for table in (EXACT_CHOSEN, EXACT_MASK, UP_EARLY, UP_LATE)]
    (out,) = call(
        late_kernel, "late", [half(cells)],
        [fq, *sums, cross, *lates, coarse_att, constant(CORNER_CHOSEN),
         constant(CORNER_MASK), constant(UP_ATT), out_weight,
         near_kv, *sides, *edges, ckv, *coarse, *bands, *exact],
        3e9,
        hbm=(11, 21, 22, 23, 24),
        scratch=[
            pltpu.VMEM((PAIRS, cells, LANES), BF16), pltpu.VMEM((8, LANES), F32),
            pltpu.VMEM((cells, 2 * channels), BF16),
            *[pltpu.VMEM(x.shape, BF16) for x in exact], pltpu.SemaphoreType.DMA((5,)),
        ],
    )
    return out.reshape(ROWS, COLS, channels)


def solution(mesh):
    tiled = P("lat", "lon", None)
    return jax.shard_map(
        shards, mesh=mesh, in_specs=(tiled,) * 4 + (P(),), out_specs=tiled, check_vma=False
    )
```

```python
import math

import jax
import jax.numpy as jnp
import numpy as np
from jax import lax
from jax.experimental import pallas as pl
from jax.experimental.pallas import tpu as pltpu
from jax.sharding import PartitionSpec as P

HEADS = 8
RADIUS = 6
FACTOR = 4
ROWS, COLS = 24, 32
CROWS, CCOLS = 6, 8
LANES = 128
BLOCK_ROWS = 8
BLOCKS = ROWS // BLOCK_ROWS
BLOCK = BLOCK_ROWS * COLS
MASKED = -16384.0
EXPONENT = 0.125 * math.log2(math.e)
F32 = jnp.float32
BF16 = jnp.bfloat16


ROW_ORDER = list(range(2, 22)) + [0, 1, 22, 23]
LEFT_FINE = [(r, c - RADIUS) for r in ROW_ORDER for c in range(RADIUS)]
RIGHT_FINE = [(r, COLS + c) for r in ROW_ORDER for c in range(RADIUS)]
CORNER_TOP = list(range(0, 24)) + list(range(120, 132))
CORNER_BOTTOM = list(range(96, 120)) + list(range(132, 144))
CORNERS = 36
LATE_ROWS = 80
ATT_ROWS = 64


OWN_BLOCKS = [((0, 10), (0, 16)), ((10, 14), (4, 20)), ((14, 24), (8, 24))]


def corner_keys(top):
    picks = CORNER_BOTTOM if top else CORNER_TOP
    shift = -ROWS if top else ROWS
    keys = [(LEFT_FINE[i][0] + shift, LEFT_FINE[i][1]) for i in picks]
    keys += [(RIGHT_FINE[i][0] + shift, RIGHT_FINE[i][1]) for i in picks]
    return keys + [None] * (LATE_ROWS - len(keys))


def mask_lanes(keys, rows, cols):
    table = np.zeros((len(keys), LANES), np.float32)
    for n, key in enumerate(keys):
        if key is None:
            table[n, : len(rows) + len(cols)] = MASKED
            continue
        for i, row in enumerate(rows):
            if abs(key[0] - row) > RADIUS:
                table[n, i] = MASKED
        for j, col in enumerate(cols):
            if abs(key[1] - col) > RADIUS:
                table[n, len(rows) + j] = MASKED
    return table


def chosen_lanes(queries, rows, cols):
    table = np.zeros((len(queries), LANES), np.float32)
    for n, query in enumerate(queries):
        if query is None:
            continue
        table[n, rows.index(query[0])] = 1.0
        table[n, len(rows) + cols.index(query[1])] = 1.0
        table[n, LANES - 1] = 1.0
    return table


def cells_of(rows, cols):
    return [(r, c) for r in rows for c in cols]


FINE_COLS = list(range(COLS))
EDGE = RADIUS * COLS
GROUP = 8
WEST_COLS, EAST_COLS = list(range(GROUP)), list(range(COLS - GROUP, COLS))
ALL_ROWS = list(range(ROWS))
TOP_ROWS, BOTTOM_ROWS = list(range(RADIUS)), list(range(ROWS - RADIUS, ROWS))
TOP_FINE = cells_of(range(-RADIUS, 0), range(COLS))
BOTTOM_FINE = cells_of(range(ROWS, ROWS + RADIUS), range(COLS))
OWN_FINE = cells_of(ALL_ROWS, FINE_COLS)


def tables_of(queries, keys):
    rows = sorted({q[0] for q in queries})
    cols = sorted({q[1] for q in queries})
    return chosen_lanes(queries, rows, cols), mask_lanes(keys, rows, cols)


def stacked(pairs):
    made = [tables_of(*pair) for pair in pairs]
    return [np.concatenate(tables) for tables in zip(*made)]


OWN_CHOSEN, OWN_MASK = stacked(
    [
        (cells_of(range(*q), FINE_COLS), cells_of(range(*k), FINE_COLS))
        for q, k in OWN_BLOCKS
    ]
)
LON_CHOSEN, LON_MASK = stacked(
    [
        (cells_of(ALL_ROWS, WEST_COLS), LEFT_FINE),
        (cells_of(ALL_ROWS, EAST_COLS), RIGHT_FINE),
    ]
)
LAT_CHOSEN, LAT_MASK = stacked(
    [
        (cells_of(TOP_ROWS, FINE_COLS), TOP_FINE),
        (cells_of(BOTTOM_ROWS, FINE_COLS), BOTTOM_FINE),
    ]
)
CORNER_CHOSEN, CORNER_MASK = stacked(
    [
        (cells_of(TOP_ROWS, WEST_COLS) + cells_of(TOP_ROWS, EAST_COLS), corner_keys(True)),
        (cells_of(BOTTOM_ROWS, WEST_COLS) + cells_of(BOTTOM_ROWS, EAST_COLS), corner_keys(False)),
    ]
)
EXACT_KEYS = (
    OWN_FINE + LEFT_FINE + RIGHT_FINE + TOP_FINE + corner_keys(True) + BOTTOM_FINE + corner_keys(False)
)
EXACT_CHOSEN, EXACT_MASK = stacked(
    [
        (cells_of(range(b * BLOCK_ROWS, (b + 1) * BLOCK_ROWS), FINE_COLS), EXACT_KEYS)
        for b in range(BLOCKS)
    ]
)

CQ_COLS = list(range(-1, CCOLS + 1))
OWN_COARSE = [(r, c) for r in range(CROWS) for c in range(CCOLS)]
LEFT_COARSE = [(r, c - 7) for r in range(CROWS) for c in range(7)] + [None] * CROWS
RIGHT_COARSE = [(r, c + CCOLS) for r in range(CROWS) for c in range(7)] + [None] * CROWS
BAND = OWN_COARSE + LEFT_COARSE + RIGHT_COARSE


def moved(keys, rows):
    return [None if key is None else (key[0] + rows, key[1]) for key in keys]


COARSE_KEYS = BAND + moved(BAND, -CROWS) + moved(BAND, CROWS)
COARSE_COUNT = 512
COARSE_KEYS = COARSE_KEYS + [None] * (COARSE_COUNT - len(COARSE_KEYS))
COARSE_QUERIES = (
    OWN_COARSE
    + [None] * 10
    + [(r, -1) for r in range(CROWS)]
    + [None] * 10
    + [(r, CCOLS) for r in range(CROWS)]
)
COARSE_CHOSEN = chosen_lanes(COARSE_QUERIES, list(range(CROWS)), CQ_COLS)
COARSE_MASK = mask_lanes(COARSE_KEYS, list(range(CROWS)), CQ_COLS)
LATE_CELLS_OF_ROW = [(0, c) for c in range(CCOLS)] + [(0, -1), (0, CCOLS)]


def late_cells(part):
    cells = LATE_CELLS_OF_ROW[part::2]
    before = 2 * CORNERS - ATT_ROWS
    return [None] * before + cells + [None] * (LATE_ROWS - ATT_ROWS - before - len(cells))


LATE_ATT = late_cells(0) + late_cells(1)
ATT_CELLS = COARSE_QUERIES + moved(LATE_ATT, -1) + moved(LATE_ATT, CROWS)


def coefficient(fine):
    coarse, offset = fine // FACTOR, (fine % FACTOR - 1.5) / FACTOR
    taps = {coarse: 1.0 - abs(offset)}
    taps[coarse + (1 if offset > 0 else -1)] = abs(offset)
    return taps


def up_table(fine_cells, coarse_cells, pole):
    where = {cell: n for n, cell in reversed(list(enumerate(coarse_cells))) if cell is not None}
    table = np.zeros((len(fine_cells), len(coarse_cells)), np.float32)
    for n, (row, col) in enumerate(fine_cells):
        for r, a in coefficient(row).items():
            if pole == "top":
                r = max(r, 0)
            if pole == "bottom":
                r = min(r, CROWS - 1)
            for c, b in coefficient(col).items():
                table[n, where[(r, c)]] += a * b
    return table


def poles(fine_cells, coarse_cells):
    return np.stack([up_table(fine_cells, coarse_cells, p) for p in ("none", "top", "bottom")])


FINE_CELLS = [(r, c) for r in range(ROWS) for c in range(COLS)]
INNER = [(r, c) for r in range(2, ROWS - 2) for c in range(2, COLS - 2)]
EARLY_COUNT = 512
EARLY_CELLS = INNER[:EARLY_COUNT]
LATE_CELLS = [cell for cell in FINE_CELLS if cell not in set(EARLY_CELLS)]
UP_EARLY = up_table(EARLY_CELLS, OWN_COARSE, "none")
UP_LATE = poles(LATE_CELLS, COARSE_KEYS)
INNER_CELLS = FINE_CELLS[EDGE:-EDGE]
UP_INNER = up_table(INNER_CELLS, COARSE_QUERIES, "none")
UP_OUTER = poles(FINE_CELLS[:EDGE] + FINE_CELLS[-EDGE:], ATT_CELLS)


def picked(indices, count):
    table = np.zeros((len(indices), count), np.float32)
    for n, index in enumerate(indices):
        if index is not None:
            table[n, index] = 1.0
    return table


FINE_EAST = [r * COLS + COLS - RADIUS + c for r in ROW_ORDER for c in range(RADIUS)]
FINE_WEST = [r * COLS + c for r in ROW_ORDER for c in range(RADIUS)]
PICK_FINE = picked(FINE_EAST + FINE_WEST, ROWS * COLS)
PICK_COARSE = picked(
    [r * CCOLS + 1 + c for r in range(CROWS) for c in range(7)]
    + [None] * CROWS
    + [r * CCOLS + c for r in range(CROWS) for c in range(7)]
    + [None] * CROWS,
    CROWS * CCOLS,
)
PICK_QUERY = picked(
    [None] * 42
    + [r * CCOLS + CCOLS - 1 for r in range(CROWS)]
    + [None] * 42
    + [r * CCOLS for r in range(CROWS)],
    CROWS * CCOLS,
)
SIDE = len(ROW_ORDER) * RADIUS


def late_picks(corner, row):
    rest = LATE_ROWS - 2 * CORNERS
    left = picked(list(corner) + [None] * (CORNERS + rest), SIDE)
    right = picked([None] * CORNERS + list(corner) + [None] * rest, SIDE)
    tables = [left, right]
    for part in range(2):
        cells = moved(late_cells(part), row)
        att = [None if cell is None else COARSE_QUERIES.index(cell) for cell in cells]
        tables.append(picked([None] * ATT_ROWS + att, len(COARSE_QUERIES)))
    return tables


LATE_PICKS = [
    np.concatenate(tables)
    for tables in zip(late_picks(CORNER_BOTTOM, CROWS - 1), late_picks(CORNER_TOP, 0))
]


PAIRS = HEADS // 2
LEAST, MOST = 2.0**-80, 2.0**100


def halves():
    return lax.broadcasted_iota(jnp.int32, (1, LANES), 1) < LANES // 2


def head_of(pair, head):
    return jnp.where(halves() == (head == 0), pair, jnp.zeros((), pair.dtype))


def packed(first, second):
    return jnp.where(halves(), first, second)


def dot(a, b):
    return jnp.dot(a, b, preferred_element_type=F32)


def scores(queries, keys):
    return lax.dot_general(queries, keys, (((1,), (1,)), ((), ())), preferred_element_type=F32)


def mix(weights, values):
    mixed = dot(weights.astype(BF16), values)
    return mixed[:, :LANES], mixed[:, LANES:]


def with_ones(values):
    return jnp.concatenate([values, jnp.ones_like(values)], 1)


def even(axis):
    return lax.axis_index(axis) % 2 == 0


def pole_flags():
    lat = lax.axis_index("lat")
    return lat == 0, lat == lax.axis_size("lat") - 1


def pole_table():
    is_top, is_bottom = pole_flags()
    return jnp.where(is_top, 1, jnp.where(is_bottom, 2, 0))


def lanes_of(group):
    if isinstance(group, int):
        return slice(group * LANES, (group + 1) * LANES)
    return pl.ds(pl.multiple_of(group * LANES, LANES), LANES)


def low(pair):
    return lanes_of(pair)


def high(pair):
    return lanes_of(pair + PAIRS)


def close_edge(mask, closed):
    lane = lax.broadcasted_iota(jnp.int32, (1, LANES), 1)
    return jnp.where((lane == LANES - 1) & closed, MASKED, mask.astype(F32)).astype(BF16)


def before_after(axis, first, second, *index):
    a, b = first[index], second[index]
    if axis == "lat":
        return a, b
    return jnp.where(even(axis), b, a), jnp.where(even(axis), a, b)


def both_heads(queries, chosen):
    rows = jnp.concatenate([head_of(queries, 0), head_of(queries, 1)], 0)
    if chosen is None:
        return rows
    return jnp.concatenate([rows, jnp.concatenate([chosen, chosen], 0)], 1)


def plain_softmax(queries, chosen, keys, values):
    count = queries.shape[0]
    mixed, total = mix(jnp.exp2(scores(both_heads(queries, chosen), keys) * EXPONENT), values)
    return packed(mixed[:count], mixed[count:]), packed(total[:count], total[count:])


def exact_softmax(queries, chosen, keys, values):
    count = queries.shape[0]
    score = scores(both_heads(queries, chosen), keys)
    score = score - jnp.max(score, 1, keepdims=True)
    mixed, total = mix(jnp.exp2(score * EXPONENT), values)
    result = mixed / total
    return packed(result[:count], result[count:])


def settled(mixed, total):
    fits = (total > LEAST) & (total < MOST)
    return jnp.where(fits, mixed / total, jnp.nan)


def fetch(moves, sems):
    copies = [pltpu.make_async_copy(a, b, sems.at[n]) for n, (a, b) in enumerate(moves)]
    for copy in copies:
        copy.start()
    for copy in copies:
        copy.wait()


def send_coarse_kernel(both_ref, c0_ref, c1_ref):
    channels = both_ref.shape[1] // 3
    n = lax.broadcasted_iota(jnp.int32, (48, CROWS * CCOLS), 0)
    cell = lax.broadcasted_iota(jnp.int32, (48, CROWS * CCOLS), 1)
    row = (n * 37) >> 8
    sides = []
    for first, col in ((1, CCOLS - 1), (0, 0)):
        keyval = (n < 42) & (cell == row * CCOLS + first + n - row * 7)
        query = (n >= 42) & (cell == (n - 42) * CCOLS + col)
        both = dot(keyval.astype(F32).astype(BF16), both_ref[:, : 2 * channels])
        query = dot(query.astype(F32).astype(BF16), both_ref[:, 2 * channels :])
        sides.append(jnp.concatenate([both[:, :channels] + query, both[:, channels:]], 1).astype(BF16))
    eastward = even("lon")
    c0_ref[...] = jnp.where(eastward, sides[0], sides[1])
    c1_ref[...] = jnp.where(eastward, sides[1], sides[0])


def send_fine_kernel(fkv_ref, pick_ref, f0_ref, f1_ref, r0_ref, r1_ref):
    cells = fkv_ref.shape[0]
    fine = dot(pick_ref[...], fkv_ref[...]).astype(BF16)
    eastward = even("lon")
    f0_ref[...] = jnp.where(eastward, fine[:SIDE], fine[SIDE:])
    f1_ref[...] = jnp.where(eastward, fine[SIDE:], fine[:SIDE])
    r0_ref[...] = fkv_ref[cells - EDGE :, :]
    r1_ref[...] = fkv_ref[:EDGE, :]


def send_band_kernel(ckv_ref, c0_ref, c1_ref, band_ref):
    left, right = before_after("lon", c0_ref, c1_ref, slice(None), slice(None))
    band_ref[0:48, :] = ckv_ref[...]
    band_ref[48:96, :] = left
    band_ref[96:144, :] = right


def send_late_kernel(f0_ref, f1_ref, att_ref, pl_ref, pr_ref, pa_ref, pb_ref, l0_ref, l1_ref):
    left, right = before_after("lon", f0_ref, f1_ref, slice(None), slice(None))
    sides = dot(pl_ref[...], left) + dot(pr_ref[...], right)
    att = jnp.concatenate([dot(pa_ref[...], att_ref[...]), dot(pb_ref[...], att_ref[...])], 1)
    late = (sides + att).astype(BF16)
    l0_ref[...], l1_ref[...] = late[:LATE_ROWS], late[LATE_ROWS:]


def own_kernel(q_ref, kv_ref, chosen_ref, mask_ref, mixed_ref, total_ref):
    for pair in range(PAIRS):
        lo, hi = low(pair), high(pair)
        at = 0
        for (q0, q1), (k0, k1) in OWN_BLOCKS:
            rows = slice(q0 * COLS, q1 * COLS)
            near = slice(k0 * COLS, k1 * COLS)
            mask = mask_ref[at : at + (k1 - k0) * COLS, :]
            at += (k1 - k0) * COLS
            keys = jnp.concatenate([kv_ref[near, lo], mask], 1)
            mixed_ref[rows, lo], total_ref[rows, lo] = plain_softmax(
                q_ref[rows, lo], chosen_ref[rows, :], keys, with_ones(kv_ref[near, hi])
            )


CROSS_ROWS = 768


def raise_pair(table, keys, values):
    both = dot(table, jnp.concatenate([keys, values], 1)).astype(BF16)
    return both[:, :LANES], with_ones(both[:, LANES:])


def early_cross_kernel(q_ref, ckv_ref, up_ref, mixed_ref, total_ref):
    up = up_ref[...]
    raised = [raise_pair(up, ckv_ref[:, low(pair)], ckv_ref[:, high(pair)]) for pair in range(PAIRS)]
    for pair in range(PAIRS):
        lo = low(pair)
        up_keys, up_values = raised[pair]
        for first in range(0, q_ref.shape[0], CROSS_ROWS):
            rows = slice(first, first + CROSS_ROWS)
            mixed_ref[rows, lo], total_ref[rows, lo] = plain_softmax(
                q_ref[rows, lo], None, up_keys, up_values
            )


def columns(queries, first):
    rows = queries.shape[0] // COLS
    split = queries.astype(F32).reshape(rows, COLS, LANES)[:, first : first + GROUP]
    return split.reshape(rows * GROUP, LANES).astype(BF16)


def lon_kernel(q_ref, f0_ref, f1_ref, chosen_ref, mask_ref, om_ref, ot_ref, mixed_ref, total_ref):
    strip = ROWS * GROUP
    for pair in range(PAIRS):
        lo, hi = low(pair), high(pair)
        keys = before_after("lon", f0_ref, f1_ref, slice(None), lo)
        values = before_after("lon", f0_ref, f1_ref, slice(None), hi)
        queries = q_ref[:, lo]
        for n, first in enumerate((0, COLS - GROUP)):
            mixed, total = plain_softmax(
                columns(queries, first),
                chosen_ref[n * strip : (n + 1) * strip, :],
                jnp.concatenate([keys[n], mask_ref[n * SIDE : (n + 1) * SIDE, :]], 1),
                with_ones(values[n]),
            )
            for row in range(ROWS):
                at = slice(row * COLS + first, row * COLS + first + GROUP)
                piece = slice(row * GROUP, (row + 1) * GROUP)
                mixed_ref[at, lo] = om_ref[at, lo] + mixed[piece]
                total_ref[at, lo] = ot_ref[at, lo] + total[piece]


def lat_kernel(q_ref, r0_ref, r1_ref, chosen_ref, mask_ref, om_ref, ot_ref, mixed_ref, total_ref):
    cells = q_ref.shape[0]
    closed = pole_flags()
    masks = [close_edge(mask_ref[n * EDGE : (n + 1) * EDGE, :], closed[n]) for n in range(2)]
    for pair in range(PAIRS):
        lo, hi = low(pair), high(pair)
        keys = before_after("lat", r0_ref, r1_ref, slice(None), lo)
        values = before_after("lat", r0_ref, r1_ref, slice(None), hi)
        for n, first in enumerate((0, cells - EDGE)):
            rows = slice(first, first + EDGE)
            mixed, total = plain_softmax(
                q_ref[rows, lo],
                chosen_ref[n * EDGE : (n + 1) * EDGE, :],
                jnp.concatenate([keys[n], masks[n]], 1),
                with_ones(values[n]),
            )
            mixed_ref[rows, lo] = om_ref[rows, lo] + mixed
            total_ref[rows, lo] = ot_ref[rows, lo] + total


def gathered(own, coarse, band, lanes):
    left, right = before_after("lon", *coarse, slice(None), lanes)
    top, bottom = before_after("lat", *band, slice(None), lanes)
    pad = jnp.zeros((COARSE_COUNT - 3 * len(BAND), LANES), BF16)
    return jnp.concatenate([own[:, lanes], left, right, top, bottom, pad], 0)


def coarse_kernel(q_ref, own_ref, c0_ref, c1_ref, b0_ref, b1_ref, chosen_ref, mask_ref, out_ref):
    is_top, is_bottom = pole_flags()
    band = len(BAND)
    mask = [
        mask_ref[:band, :],
        close_edge(mask_ref[band : 2 * band, :], is_top),
        close_edge(mask_ref[2 * band :, :], is_bottom),
    ]
    mask = jnp.concatenate(mask, 0)
    chosen = chosen_ref[...]
    for pair in range(PAIRS):
        lo = slice(pair * LANES, (pair + 1) * LANES)
        hi = slice((pair + PAIRS) * LANES, (pair + PAIRS + 1) * LANES)
        keys = jnp.concatenate([gathered(own_ref, (c0_ref, c1_ref), (b0_ref, b1_ref), lo), mask], 1)
        values = with_ones(gathered(own_ref, (c0_ref, c1_ref), (b0_ref, b1_ref), hi))
        left, right = before_after("lon", c0_ref, c1_ref, slice(32, 48), lo)
        queries = jnp.concatenate([q_ref[:, lo], left, right], 0)
        out_ref[:, lo] = exact_softmax(queries, chosen, keys, values).astype(BF16)


def late_cross_kernel(q_ref, oc_ref, lc_ref, ckv_ref, c0_ref, c1_ref, b0_ref, b1_ref, late_ref, cross_ref):
    late = late_ref[pole_table()]
    coarse = (ckv_ref, (c0_ref, c1_ref), (b0_ref, b1_ref))
    raised = [
        raise_pair(late, gathered(*coarse, low(pair)), gathered(*coarse, high(pair))) for pair in range(PAIRS)
    ]
    for pair in range(PAIRS):
        lo = low(pair)
        up_keys, up_values = raised[pair]
        for first in range(0, q_ref.shape[0], CROSS_ROWS):
            rows = slice(first, first + CROSS_ROWS)
            mixed, total = plain_softmax(q_ref[rows, lo], None, up_keys, up_values)
            cross_ref[rows, lo] = settled(oc_ref[rows, lo] + mixed, lc_ref[rows, lo] + total)


def join(mixed, total, cross, raised):
    fine = settled(mixed, total).astype(BF16).astype(F32)
    joined = fine + cross + raised
    return joined.astype(BF16), jnp.sum(joined.reshape(-1, 8, LANES) * 0.0, 0)


def inner_kernel(mixed_ref, total_ref, cross_ref, att_ref, up_ref, weight_ref, out_ref, bad_ref):
    rows = slice(EDGE, mixed_ref.shape[0] - EDGE)
    raised = dot(up_ref[...], att_ref[...])
    parts = [
        join(mixed_ref[rows, low(n)], total_ref[rows, low(n)], cross_ref[rows, low(n)], raised[:, low(n)])
        for n in range(PAIRS)
    ]
    bad_ref[...] = sum(bad for _, bad in parts)
    joined = jnp.concatenate([piece for piece, _ in parts], 1)
    out_ref[...] = dot(joined, weight_ref[...]).astype(BF16)


def late_kernel(
    q_ref, mixed_ref, total_ref, cross_ref, l0_ref, l1_ref, att_ref,
    chosen_ref, mask_ref, up_ref, weight_ref, inner_ref, inner_bad_ref,
    kv_hbm, f0_ref, f1_ref, r0_ref, r1_ref, ckv_ref, c0_ref, c1_ref, b0_ref, b1_ref,
    exact_chosen_hbm, exact_mask_hbm, early_hbm, late_hbm, up_inner_hbm,
    out_ref, joined_ref, bad_ref,
    kv_ref, exact_chosen_ref, exact_mask_ref, early_ref, late_ref, up_inner_ref, sems,
):
    cells = q_ref.shape[0]
    closed = pole_flags()
    pole = pole_table()
    up = up_ref[pole]
    masks = [close_edge(mask_ref[n * LATE_ROWS : (n + 1) * LATE_ROWS, :], closed[n]) for n in range(2)]
    corner = RADIUS * GROUP
    bad = inner_bad_ref[...]

    def raised_att(group, count):
        lanes = [slice((n + group) * LANES, (n + group + count) * LANES) for n in (0, PAIRS)]
        if count == 1:
            lanes = [low(group), high(group)]
        tops, bottoms = zip(*[before_after("lat", l0_ref, l1_ref, slice(ATT_ROWS, None), at) for at in lanes])
        return dot(up, jnp.concatenate([att_ref[:, lanes[0]], *tops, *bottoms], 0))

    def cornered(sums, part):
        west, east = part[:corner].reshape(-1, GROUP, LANES), part[corner:].reshape(-1, GROUP, LANES)
        rows = sums.reshape(-1, COLS, LANES)
        rows = jnp.concatenate(
            [rows[:, :GROUP] + west, rows[:, GROUP : COLS - GROUP], rows[:, COLS - GROUP :] + east], 1
        )
        return rows.reshape(-1, LANES)

    raised = [raised_att(pair, 2) for pair in range(0, PAIRS, 2)]
    parts = []
    for pair in range(PAIRS):
        lo, hi = low(pair), high(pair)
        corner_keys = before_after("lat", l0_ref, l1_ref, slice(None), lo)
        corner_values = before_after("lat", l0_ref, l1_ref, slice(None), hi)
        lift = raised[pair // 2][:, pair % 2 * LANES : (pair % 2 + 1) * LANES]
        pieces = []
        for n, first in enumerate((0, cells - EDGE)):
            rows = slice(first, first + EDGE)
            queries = q_ref[rows, lo]
            queries = jnp.concatenate([columns(queries, 0), columns(queries, COLS - GROUP)], 0)
            keys = jnp.concatenate([corner_keys[n], masks[n]], 1)
            chosen = chosen_ref[2 * n * corner : 2 * (n + 1) * corner, :]
            mixed, total = plain_softmax(queries, chosen, keys, with_ones(corner_values[n]))
            mixed, total = cornered(mixed_ref[rows, lo], mixed), cornered(total_ref[rows, lo], total)
            piece, wrong = join(mixed, total, cross_ref[rows, lo], lift[n * EDGE : (n + 1) * EDGE])
            pieces.append(piece)
            bad += wrong
        parts.append(jnp.concatenate(pieces, 0))
    bad_ref[...] = bad
    outer = dot(jnp.concatenate(parts, 1), weight_ref[...]).astype(BF16)
    out_ref[:EDGE, :] = outer[:EDGE]
    out_ref[EDGE : cells - EDGE, :] = inner_ref[...]
    out_ref[cells - EDGE :, :] = outer[EDGE:]

    @pl.when(jnp.logical_not(jnp.sum(bad_ref[...]) == 0.0))
    def _():
        fetch(
            [(kv_hbm, kv_ref), (exact_chosen_hbm, exact_chosen_ref), (exact_mask_hbm, exact_mask_ref),
             (early_hbm, early_ref), (late_hbm, late_ref), (up_inner_hbm, up_inner_ref)],
            sems,
        )
        coarse = (ckv_ref, (c0_ref, c1_ref), (b0_ref, b1_ref))
        early, late = early_ref[...], late_ref[pole]
        count = len(EXACT_KEYS)
        edges = [cells + 2 * SIDE, cells + 2 * SIDE + EDGE + LATE_ROWS, count]

        @pl.loop(0, PAIRS)
        def _(pair):
            def all_of(lanes):
                left, right = before_after("lon", f0_ref, f1_ref, slice(None), lanes)
                top, bottom = before_after("lat", r0_ref, r1_ref, slice(None), lanes)
                late_top, late_bottom = before_after("lat", l0_ref, l1_ref, slice(None), lanes)
                return jnp.concatenate(
                    [kv_ref[:, lanes], left, right, top, late_top, bottom, late_bottom], 0
                )

            def up_of(lanes):
                first = dot(early, ckv_ref[:, lanes]).astype(BF16)
                return jnp.concatenate([first, dot(late, gathered(*coarse, lanes)).astype(BF16)], 0)

            lo, hi = low(pair), high(pair)
            keys, values = all_of(lo), with_ones(all_of(hi))
            up_keys, up_values = up_of(lo), with_ones(up_of(hi))
            outer, inner = raised_att(pair, 1), dot(up_inner_ref[...], att_ref[:, lo])
            raised = jnp.concatenate([outer[:EDGE], inner, outer[EDGE:]], 0)
            for block in range(BLOCKS):
                mask = exact_mask_ref[block * count : (block + 1) * count, :]
                mask = [mask[: edges[0]]] + [
                    close_edge(mask[edges[n] : edges[n + 1]], closed[n]) for n in range(2)
                ]
                rows = slice(block * BLOCK, (block + 1) * BLOCK)
                queries = q_ref[rows, lo]
                fine = exact_softmax(
                    queries,
                    exact_chosen_ref[rows, :],
                    jnp.concatenate([keys, jnp.concatenate(mask, 0)], 1),
                    values,
                )
                cross = exact_softmax(queries, None, up_keys, up_values)
                joined = fine.astype(BF16).astype(F32) + cross + raised[rows, :]
                joined_ref[pair, rows, :] = joined.astype(BF16)

        joined = jnp.concatenate([joined_ref[n] for n in range(PAIRS)], 1)
        out_ref[...] = dot(joined, weight_ref[...]).astype(BF16)


def constant(table):
    return jnp.asarray(table, BF16)


def call(kernel, name, outs, operands, flops, hbm=(), scratch=(), vmem=28, aliases={}):
    near = pl.BlockSpec(memory_space=pltpu.VMEM)
    far = pl.BlockSpec(memory_space=pltpu.HBM)
    moved_bytes = sum(x.size * x.dtype.itemsize for x in list(operands) + list(outs))
    return pl.pallas_call(
        kernel,
        in_specs=[far if n in hbm else near for n in range(len(operands))],
        out_specs=[near] * len(outs),
        out_shape=list(outs),
        scratch_shapes=list(scratch),
        input_output_aliases=dict(aliases),
        compiler_params=pltpu.CompilerParams(vmem_limit_bytes=vmem << 20),
        cost_estimate=pl.CostEstimate(
            flops=int(flops), bytes_accessed=int(moved_bytes if flops > 1e9 else moved_bytes // 16), transcendentals=int(flops / 1000)
        ),
        name=name,
    )(*operands)


def swap(array, above):
    size = lax.axis_size("lon")
    pairs = [(i, (i + 1) % size) for i in range(0 if above else 1, size, 2)]
    return lax.ppermute(array, "lon", pairs + [(b, a) for a, b in pairs])


def shift(array, step):
    size = lax.axis_size("lat")
    return lax.ppermute(array, "lat", [(i, (i + step) % size) for i in range(size)])


def ring(southward, northward):
    return shift(southward, 1), shift(northward, -1)


def shards(fine_query, fine_keyval, coarse_query, coarse_keyval, out_weight):
    channels = fine_query.shape[-1]
    cells = ROWS * COLS
    fq = fine_query.reshape(cells, channels)
    fkv = fine_keyval.reshape(cells, 2 * channels)
    cq = coarse_query.reshape(-1, channels)
    ckv = coarse_keyval.reshape(-1, 2 * channels)
    half = lambda rows: jax.ShapeDtypeStruct((rows, channels), BF16)
    full = lambda rows: jax.ShapeDtypeStruct((rows, 2 * channels), BF16)
    state = lambda rows: jax.ShapeDtypeStruct((rows, channels), F32)
    after = lax.optimization_barrier

    c0, c1 = call(
        send_coarse_kernel, "send_coarse", [full(48)] * 2, [jnp.concatenate([ckv, cq], 1)], 1e10, vmem=8
    )
    coarse0, coarse1 = swap(c0, True), swap(c1, False)
    near_kv, _ = after((fkv, c0))
    f0, f1, r0, r1 = call(
        send_fine_kernel, "send_fine", [full(SIDE)] * 2 + [full(EDGE)] * 2, [near_kv, constant(PICK_FINE)], 5e9
    )
    edge0 = shift(r0, 1)
    side0 = swap(f0, True)
    f1, coarse0, coarse1, r0 = after((f1, coarse0, coarse1, r0))
    coarse = (coarse0, coarse1)
    sides = (side0, swap(f1, False))
    ckv, _ = after((ckv, f1))
    (band,) = call(send_band_kernel, "send_band", [full(len(BAND))], [ckv, *coarse], 1e6)
    bands = ring(band, band)
    fq, near_kv, _ = after((fq, near_kv, band))
    own = call(
        own_kernel, "own", [state(cells)] * 2, [fq, near_kv, constant(OWN_CHOSEN), constant(OWN_MASK)], 5e9
    )
    fq, own = after((fq, own))
    early = call(early_cross_kernel, "early_cross", [state(cells)] * 2, [fq, ckv, constant(UP_EARLY)], 5e9)
    bands, early, r1 = after((bands, early, r1))
    edges = (edge0, shift(r1, -1))
    (coarse_att,) = call(
        coarse_kernel, "coarse", [half(len(COARSE_QUERIES))],
        [cq, ckv, *coarse, *bands, constant(COARSE_CHOSEN), constant(COARSE_MASK)], 2e9,
    )
    late0, late1 = call(
        send_late_kernel, "send_late", [full(LATE_ROWS)] * 2,
        [*sides, coarse_att] + [constant(table) for table in LATE_PICKS], 2e8,
    )
    lates = ring(late0, late1)
    fq, _ = after((fq, late0))
    (cross,) = call(
        late_cross_kernel, "late_cross", [state(cells)], [fq, *early, ckv, *coarse, *bands, constant(UP_LATE)], 1e8
    )
    fq, cross = after((fq, cross))
    sums = call(
        lon_kernel, "lon_strips", [state(cells)] * 2,
        [fq, *sides, constant(LON_CHOSEN), constant(LON_MASK), *own], 1e8, aliases={5: 0, 6: 1},
    )
    inner, inner_bad = call(
        inner_kernel, "inner", [half(cells - 2 * EDGE), jax.ShapeDtypeStruct((8, LANES), F32)],
        [*sums, cross, coarse_att, constant(UP_INNER), out_weight], 1e8,
    )
    fq, sums, _ = after((fq, sums, inner))
    sums = call(
        lat_kernel, "lat_strips", [state(cells)] * 2,
        [fq, *edges, constant(LAT_CHOSEN), constant(LAT_MASK), *sums], 1e8, aliases={5: 0, 6: 1},
    )
    exact = [constant(table) for table in (EXACT_CHOSEN, EXACT_MASK, UP_EARLY, UP_LATE, UP_INNER)]
    (out,) = call(
        late_kernel, "late", [half(cells)],
        [fq, *sums, cross, *lates, coarse_att, constant(CORNER_CHOSEN),
         constant(CORNER_MASK), constant(UP_OUTER), out_weight, inner, inner_bad,
         near_kv, *sides, *edges, ckv, *coarse, *bands, *exact],
        3e9,
        hbm=(13, 23, 24, 25, 26, 27),
        scratch=[
            pltpu.VMEM((PAIRS, cells, LANES), BF16), pltpu.VMEM((8, LANES), F32),
            pltpu.VMEM((cells, 2 * channels), BF16),
            *[pltpu.VMEM(x.shape, BF16) for x in exact], pltpu.SemaphoreType.DMA((6,)),
        ],
    )
    return out.reshape(ROWS, COLS, channels)


def solution(mesh):
    tiled = P("lat", "lon", None)
    return jax.shard_map(
        shards, mesh=mesh, in_specs=(tiled,) * 4 + (P(),), out_specs=tiled, check_vma=False
    )
```

```python
import functools
import math

import jax
import jax.numpy as jnp
import numpy as np
from jax import lax
from jax.experimental import pallas as pl
from jax.experimental.pallas import tpu as pltpu
from jax.sharding import PartitionSpec as P

HEADS = 8
RADIUS = 6
FACTOR = 4
ROWS, COLS = 24, 32
CROWS, CCOLS = 6, 8
LANES = 128
BLOCK_ROWS = 8
BLOCKS = ROWS // BLOCK_ROWS
BLOCK = BLOCK_ROWS * COLS
MASKED = -16384.0
EXPONENT = 0.125 * math.log2(math.e)
F32 = jnp.float32
BF16 = jnp.bfloat16


ROW_ORDER = list(range(2, 22)) + [0, 1, 22, 23]
LEFT_FINE = [(r, c - RADIUS) for r in ROW_ORDER for c in range(RADIUS)]
RIGHT_FINE = [(r, COLS + c) for r in ROW_ORDER for c in range(RADIUS)]
CORNER_TOP = list(range(0, 24)) + list(range(120, 132))
CORNER_BOTTOM = list(range(96, 120)) + list(range(132, 144))
CORNERS = 36
LATE_ROWS = 80
ATT_ROWS = 64


OWN_BLOCKS = [((0, 10), (0, 16)), ((10, 14), (4, 20)), ((14, 24), (8, 24))]


def corner_keys(top):
    picks = CORNER_BOTTOM if top else CORNER_TOP
    shift = -ROWS if top else ROWS
    keys = [(LEFT_FINE[i][0] + shift, LEFT_FINE[i][1]) for i in picks]
    keys += [(RIGHT_FINE[i][0] + shift, RIGHT_FINE[i][1]) for i in picks]
    return keys + [None] * (LATE_ROWS - len(keys))


def mask_lanes(keys, rows, cols):
    table = np.zeros((len(keys), LANES), np.float32)
    for n, key in enumerate(keys):
        if key is None:
            table[n, : len(rows) + len(cols)] = MASKED
            continue
        for i, row in enumerate(rows):
            if abs(key[0] - row) > RADIUS:
                table[n, i] = MASKED
        for j, col in enumerate(cols):
            if abs(key[1] - col) > RADIUS:
                table[n, len(rows) + j] = MASKED
    return table


def chosen_lanes(queries, rows, cols):
    table = np.zeros((len(queries), LANES), np.float32)
    for n, query in enumerate(queries):
        if query is None:
            continue
        table[n, rows.index(query[0])] = 1.0
        table[n, len(rows) + cols.index(query[1])] = 1.0
        table[n, LANES - 1] = 1.0
    return table


def cells_of(rows, cols):
    return [(r, c) for r in rows for c in cols]


FINE_COLS = list(range(COLS))
EDGE = RADIUS * COLS
GROUP = 8
WEST_COLS, EAST_COLS = list(range(GROUP)), list(range(COLS - GROUP, COLS))
ALL_ROWS = list(range(ROWS))
TOP_ROWS, BOTTOM_ROWS = list(range(RADIUS)), list(range(ROWS - RADIUS, ROWS))
TOP_FINE = cells_of(range(-RADIUS, 0), range(COLS))
BOTTOM_FINE = cells_of(range(ROWS, ROWS + RADIUS), range(COLS))
OWN_FINE = cells_of(ALL_ROWS, FINE_COLS)


def tables_of(queries, keys):
    rows = sorted({q[0] for q in queries})
    cols = sorted({q[1] for q in queries})
    return chosen_lanes(queries, rows, cols), mask_lanes(keys, rows, cols)


def stacked(pairs):
    made = [tables_of(*pair) for pair in pairs]
    return [np.concatenate(tables) for tables in zip(*made)]


OWN_CHOSEN, OWN_MASK = stacked(
    [
        (cells_of(range(*q), FINE_COLS), cells_of(range(*k), FINE_COLS))
        for q, k in OWN_BLOCKS
    ]
)
LON_CHOSEN, LON_MASK = stacked(
    [
        (cells_of(ALL_ROWS, WEST_COLS), LEFT_FINE),
        (cells_of(ALL_ROWS, EAST_COLS), RIGHT_FINE),
    ]
)
LAT_CHOSEN, LAT_MASK = stacked(
    [
        (cells_of(TOP_ROWS, FINE_COLS), TOP_FINE),
        (cells_of(BOTTOM_ROWS, FINE_COLS), BOTTOM_FINE),
    ]
)
OUTER_COLS = (WEST_COLS, EAST_COLS)
CORNER_CHOSEN, CORNER_MASK = tables_of(
    [cell for rows in (TOP_ROWS, BOTTOM_ROWS) for cols in OUTER_COLS for cell in cells_of(rows, cols)],
    corner_keys(True) + corner_keys(False),
)
EXACT_KEYS = (
    OWN_FINE + LEFT_FINE + RIGHT_FINE + TOP_FINE + corner_keys(True) + BOTTOM_FINE + corner_keys(False)
)
EXACT_CHOSEN, EXACT_MASK = stacked(
    [
        (cells_of(range(b * BLOCK_ROWS, (b + 1) * BLOCK_ROWS), FINE_COLS), EXACT_KEYS)
        for b in range(BLOCKS)
    ]
)

CQ_COLS = list(range(-1, CCOLS + 1))
OWN_COARSE = [(r, c) for r in range(CROWS) for c in range(CCOLS)]
LEFT_COARSE = [(r, c - 7) for r in range(CROWS) for c in range(7)] + [None] * CROWS
RIGHT_COARSE = [(r, c + CCOLS) for r in range(CROWS) for c in range(7)] + [None] * CROWS
BAND = OWN_COARSE + LEFT_COARSE + RIGHT_COARSE


def moved(keys, rows):
    return [None if key is None else (key[0] + rows, key[1]) for key in keys]


COARSE_KEYS = BAND + moved(BAND, -CROWS) + moved(BAND, CROWS)
COARSE_COUNT = 512
COARSE_KEYS = COARSE_KEYS + [None] * (COARSE_COUNT - len(COARSE_KEYS))
COARSE_QUERIES = (
    OWN_COARSE
    + [None] * 10
    + [(r, -1) for r in range(CROWS)]
    + [None] * 10
    + [(r, CCOLS) for r in range(CROWS)]
)
COARSE_CHOSEN = chosen_lanes(COARSE_QUERIES, list(range(CROWS)), CQ_COLS)
COARSE_MASK = mask_lanes(COARSE_KEYS, list(range(CROWS)), CQ_COLS)
LATE_CELLS_OF_ROW = [(0, c) for c in range(CCOLS)] + [(0, -1), (0, CCOLS)]


def late_cells(part):
    cells = LATE_CELLS_OF_ROW[part::2]
    before = 2 * CORNERS - ATT_ROWS
    return [None] * before + cells + [None] * (LATE_ROWS - ATT_ROWS - before - len(cells))


LATE_ATT = late_cells(0) + late_cells(1)
ATT_CELLS = COARSE_QUERIES + moved(LATE_ATT, -1) + moved(LATE_ATT, CROWS)


def coefficient(fine):
    coarse, offset = fine // FACTOR, (fine % FACTOR - 1.5) / FACTOR
    taps = {coarse: 1.0 - abs(offset)}
    taps[coarse + (1 if offset > 0 else -1)] = abs(offset)
    return taps


def up_table(fine_cells, coarse_cells, pole):
    where = {cell: n for n, cell in reversed(list(enumerate(coarse_cells))) if cell is not None}
    table = np.zeros((len(fine_cells), len(coarse_cells)), np.float32)
    for n, (row, col) in enumerate(fine_cells):
        for r, a in coefficient(row).items():
            if pole == "top":
                r = max(r, 0)
            if pole == "bottom":
                r = min(r, CROWS - 1)
            for c, b in coefficient(col).items():
                table[n, where[(r, c)]] += a * b
    return table


def poles(fine_cells, coarse_cells):
    return np.stack([up_table(fine_cells, coarse_cells, p) for p in ("none", "top", "bottom")])


FINE_CELLS = [(r, c) for r in range(ROWS) for c in range(COLS)]
INNER = [(r, c) for r in range(2, ROWS - 2) for c in range(2, COLS - 2)]
EARLY_COUNT = 512
EARLY_CELLS = INNER[:EARLY_COUNT]
LATE_CELLS = [cell for cell in FINE_CELLS if cell not in set(EARLY_CELLS)]
UP_EARLY = up_table(EARLY_CELLS, OWN_COARSE, "none")
UP_LATE = poles(LATE_CELLS, COARSE_KEYS)
INNER_CELLS = FINE_CELLS[EDGE:-EDGE]
UP_INNER = up_table(INNER_CELLS, COARSE_QUERIES, "none")
UP_OUTER = poles(FINE_CELLS[:EDGE] + FINE_CELLS[-EDGE:], ATT_CELLS)


def picked(indices, count):
    table = np.zeros((len(indices), count), np.float32)
    for n, index in enumerate(indices):
        if index is not None:
            table[n, index] = 1.0
    return table


FINE_EAST = [r * COLS // 2 + COLS // 2 - RADIUS + c for r in ROW_ORDER for c in range(RADIUS)]
FINE_WEST = [r * COLS // 2 + c for r in ROW_ORDER for c in range(RADIUS)]
PICK_FINE = picked(FINE_EAST + FINE_WEST, ROWS * COLS // 2)
SIDE = len(ROW_ORDER) * RADIUS


def late_picks(corner, row):
    rest = LATE_ROWS - 2 * CORNERS
    left = picked(list(corner) + [None] * (CORNERS + rest), SIDE)
    right = picked([None] * CORNERS + list(corner) + [None] * rest, SIDE)
    tables = [left, right]
    for part in range(2):
        cells = moved(late_cells(part), row)
        att = [None if cell is None else COARSE_QUERIES.index(cell) for cell in cells]
        tables.append(picked([None] * ATT_ROWS + att, len(COARSE_QUERIES)))
    return tables


LATE_PICKS = [
    np.concatenate(tables)
    for tables in zip(late_picks(CORNER_BOTTOM, CROWS - 1), late_picks(CORNER_TOP, 0))
]


PAIRS = HEADS // 2
LEAST, MOST = 2.0**-80, 2.0**100


def halves():
    return lax.broadcasted_iota(jnp.int32, (1, LANES), 1) < LANES // 2


def head_of(pair, head):
    return jnp.where(halves() == (head == 0), pair, jnp.zeros((), pair.dtype))


def packed(first, second):
    return jnp.where(halves(), first, second)


def dot(a, b):
    return jnp.dot(a, b, preferred_element_type=F32)


def scores(queries, keys):
    return lax.dot_general(queries, keys, (((1,), (1,)), ((), ())), preferred_element_type=F32)


def mix(weights, values):
    mixed = dot(weights.astype(BF16), values)
    return mixed[:, :LANES], mixed[:, LANES:]


def with_ones(values):
    return jnp.concatenate([values, jnp.ones_like(values)], 1)


def even(axis):
    return lax.axis_index(axis) % 2 == 0


def pole_flags():
    lat = lax.axis_index("lat")
    return lat == 0, lat == lax.axis_size("lat") - 1


def pole_table():
    is_top, is_bottom = pole_flags()
    return jnp.where(is_top, 1, jnp.where(is_bottom, 2, 0))


def lanes_of(group):
    if isinstance(group, int):
        return slice(group * LANES, (group + 1) * LANES)
    return pl.ds(pl.multiple_of(group * LANES, LANES), LANES)


def low(pair):
    return lanes_of(pair)


def high(pair):
    return lanes_of(pair + PAIRS)


def close_edge(mask, closed):
    lane = lax.broadcasted_iota(jnp.int32, (1, LANES), 1)
    return jnp.where((lane == LANES - 1) & closed, MASKED, mask.astype(F32)).astype(BF16)


def before_after(axis, first, second, *index):
    a, b = first[index], second[index]
    if axis == "lat":
        return a, b
    return jnp.where(even(axis), b, a), jnp.where(even(axis), a, b)


def both_heads(queries, chosen):
    rows = jnp.concatenate([head_of(queries, 0), head_of(queries, 1)], 0)
    if chosen is None:
        return rows
    return jnp.concatenate([rows, jnp.concatenate([chosen, chosen], 0)], 1)


def plain_softmax(queries, chosen, keys, values):
    count = queries.shape[0]
    mixed, total = mix(jnp.exp2(scores(both_heads(queries, chosen), keys) * EXPONENT), values)
    return packed(mixed[:count], mixed[count:]), packed(total[:count], total[count:])


def exact_softmax(queries, chosen, keys, values):
    count = queries.shape[0]
    score = scores(both_heads(queries, chosen), keys)
    score = score - jnp.max(score, 1, keepdims=True)
    mixed, total = mix(jnp.exp2(score * EXPONENT), values)
    result = mixed / total
    return packed(result[:count], result[count:])


def settled(mixed, total):
    fits = (total > LEAST) & (total < MOST)
    return jnp.where(fits, mixed / total, jnp.nan)


def fetch(moves, sems):
    copies = [pltpu.make_async_copy(a, b, sems.at[n]) for n, (a, b) in enumerate(moves)]
    for copy in copies:
        copy.start()
    for copy in copies:
        copy.wait()


def send_coarse_kernel(both_ref, c0_ref, c1_ref):
    channels = both_ref.shape[1] // 3
    n = lax.broadcasted_iota(jnp.int32, (48, CROWS * CCOLS), 0)
    cell = lax.broadcasted_iota(jnp.int32, (48, CROWS * CCOLS), 1)
    row = (n * 37) >> 8
    sides = []
    for first, col in ((1, CCOLS - 1), (0, 0)):
        keyval = (n < 42) & (cell == row * CCOLS + first + n - row * 7)
        query = (n >= 42) & (cell == (n - 42) * CCOLS + col)
        both = dot(keyval.astype(F32).astype(BF16), both_ref[:, : 2 * channels])
        query = dot(query.astype(F32).astype(BF16), both_ref[:, 2 * channels :])
        sides.append(jnp.concatenate([both[:, :channels] + query, both[:, channels:]], 1).astype(BF16))
    eastward = even("lon")
    c0_ref[...] = jnp.where(eastward, sides[0], sides[1])
    c1_ref[...] = jnp.where(eastward, sides[1], sides[0])


def send_fine_kernel(fkv_ref, pick_ref, f0_ref, f1_ref, r0_ref, r1_ref):
    cells = fkv_ref.shape[0]
    halves_of_rows = fkv_ref[...].reshape(ROWS, COLS, -1)
    east = halves_of_rows[:, COLS // 2 :].reshape(ROWS * COLS // 2, -1)
    west = halves_of_rows[:, : COLS // 2].reshape(ROWS * COLS // 2, -1)
    fine = [dot(pick_ref[:SIDE], east).astype(BF16), dot(pick_ref[SIDE:], west).astype(BF16)]
    eastward = even("lon")
    f0_ref[...] = jnp.where(eastward, fine[0], fine[1])
    f1_ref[...] = jnp.where(eastward, fine[1], fine[0])
    r0_ref[...] = fkv_ref[cells - EDGE :, :]
    r1_ref[...] = fkv_ref[:EDGE, :]


def send_band_kernel(ckv_ref, c0_ref, c1_ref, band_ref):
    left, right = before_after("lon", c0_ref, c1_ref, slice(None), slice(None))
    band_ref[0:48, :] = ckv_ref[...]
    band_ref[48:96, :] = left
    band_ref[96:144, :] = right


def send_late_kernel(f0_ref, f1_ref, att_ref, pl_ref, pr_ref, pa_ref, pb_ref, l0_ref, l1_ref):
    left, right = before_after("lon", f0_ref, f1_ref, slice(None), slice(None))
    sides = dot(pl_ref[...], left) + dot(pr_ref[...], right)
    att = jnp.concatenate([dot(pa_ref[...], att_ref[...]), dot(pb_ref[...], att_ref[...])], 1)
    late = (sides + att).astype(BF16)
    l0_ref[...], l1_ref[...] = late[:LATE_ROWS], late[LATE_ROWS:]


def own_kernel(blocks, q_ref, kv_ref, chosen_ref, mask_ref, *refs):
    mixed_ref, total_ref = refs[-2:]
    for pair in range(PAIRS):
        lo, hi = low(pair), high(pair)
        for block in blocks:
            (q0, q1), (k0, k1) = OWN_BLOCKS[block]
            rows = slice(q0 * COLS, q1 * COLS)
            near = slice(k0 * COLS, k1 * COLS)
            size = (k1 - k0) * COLS
            mask = mask_ref[block * size : (block + 1) * size, :]
            keys = jnp.concatenate([kv_ref[near, lo], mask], 1)
            mixed_ref[rows, lo], total_ref[rows, lo] = plain_softmax(
                q_ref[rows, lo], chosen_ref[rows, :], keys, with_ones(kv_ref[near, hi])
            )


CROSS_ROWS = 768


def raise_pair(table, keys, values):
    both = dot(table, jnp.concatenate([keys, values], 1)).astype(BF16)
    return both[:, :LANES], with_ones(both[:, LANES:])


def early_cross_kernel(q_ref, ckv_ref, up_ref, mixed_ref, total_ref):
    up = up_ref[...]
    raised = [raise_pair(up, ckv_ref[:, low(pair)], ckv_ref[:, high(pair)]) for pair in range(PAIRS)]
    for pair in range(PAIRS):
        lo = low(pair)
        up_keys, up_values = raised[pair]
        for first in range(0, q_ref.shape[0], CROSS_ROWS):
            rows = slice(first, first + CROSS_ROWS)
            mixed_ref[rows, lo], total_ref[rows, lo] = plain_softmax(
                q_ref[rows, lo], None, up_keys, up_values
            )


def columns(queries, first):
    rows = queries.shape[0] // COLS
    split = queries.astype(F32).reshape(rows, COLS, LANES)[:, first : first + GROUP]
    return split.reshape(rows * GROUP, LANES).astype(BF16)


def lon_kernel(q_ref, f0_ref, f1_ref, chosen_ref, mask_ref, om_ref, ot_ref, mixed_ref, total_ref):
    strip = ROWS * GROUP
    for pair in range(PAIRS):
        lo, hi = low(pair), high(pair)
        keys = before_after("lon", f0_ref, f1_ref, slice(None), lo)
        values = before_after("lon", f0_ref, f1_ref, slice(None), hi)
        queries = q_ref[:, lo]
        for n, first in enumerate((0, COLS - GROUP)):
            mixed, total = plain_softmax(
                columns(queries, first),
                chosen_ref[n * strip : (n + 1) * strip, :],
                jnp.concatenate([keys[n], mask_ref[n * SIDE : (n + 1) * SIDE, :]], 1),
                with_ones(values[n]),
            )
            for row in range(ROWS):
                at = slice(row * COLS + first, row * COLS + first + GROUP)
                piece = slice(row * GROUP, (row + 1) * GROUP)
                mixed_ref[at, lo] = om_ref[at, lo] + mixed[piece]
                total_ref[at, lo] = ot_ref[at, lo] + total[piece]


def lat_kernel(q_ref, r0_ref, r1_ref, chosen_ref, mask_ref, om_ref, ot_ref, mixed_ref, total_ref):
    cells = q_ref.shape[0]
    closed = pole_flags()
    masks = [close_edge(mask_ref[n * EDGE : (n + 1) * EDGE, :], closed[n]) for n in range(2)]
    for pair in range(PAIRS):
        lo, hi = low(pair), high(pair)
        keys = before_after("lat", r0_ref, r1_ref, slice(None), lo)
        values = before_after("lat", r0_ref, r1_ref, slice(None), hi)
        for n, first in enumerate((0, cells - EDGE)):
            rows = slice(first, first + EDGE)
            mixed, total = plain_softmax(
                q_ref[rows, lo],
                chosen_ref[n * EDGE : (n + 1) * EDGE, :],
                jnp.concatenate([keys[n], masks[n]], 1),
                with_ones(values[n]),
            )
            mixed_ref[rows, lo] = om_ref[rows, lo] + mixed
            total_ref[rows, lo] = ot_ref[rows, lo] + total


def gathered(own, coarse, band, lanes):
    left, right = before_after("lon", *coarse, slice(None), lanes)
    top, bottom = before_after("lat", *band, slice(None), lanes)
    pad = jnp.zeros((COARSE_COUNT - 3 * len(BAND), LANES), BF16)
    return jnp.concatenate([own[:, lanes], left, right, top, bottom, pad], 0)


def coarse_kernel(q_ref, own_ref, c0_ref, c1_ref, b0_ref, b1_ref, chosen_ref, mask_ref, out_ref):
    is_top, is_bottom = pole_flags()
    band = len(BAND)
    mask = [
        mask_ref[:band, :],
        close_edge(mask_ref[band : 2 * band, :], is_top),
        close_edge(mask_ref[2 * band :, :], is_bottom),
    ]
    mask = jnp.concatenate(mask, 0)
    chosen = chosen_ref[...]
    for pair in range(PAIRS):
        lo = slice(pair * LANES, (pair + 1) * LANES)
        hi = slice((pair + PAIRS) * LANES, (pair + PAIRS + 1) * LANES)
        keys = jnp.concatenate([gathered(own_ref, (c0_ref, c1_ref), (b0_ref, b1_ref), lo), mask], 1)
        values = with_ones(gathered(own_ref, (c0_ref, c1_ref), (b0_ref, b1_ref), hi))
        left, right = before_after("lon", c0_ref, c1_ref, slice(32, 48), lo)
        queries = jnp.concatenate([q_ref[:, lo], left, right], 0)
        out_ref[:, lo] = exact_softmax(queries, chosen, keys, values).astype(BF16)


def late_cross_kernel(q_ref, oc_ref, lc_ref, ckv_ref, c0_ref, c1_ref, b0_ref, b1_ref, late_ref, cross_ref):
    late = late_ref[pole_table()]
    coarse = (ckv_ref, (c0_ref, c1_ref), (b0_ref, b1_ref))
    raised = [
        raise_pair(late, gathered(*coarse, low(pair)), gathered(*coarse, high(pair))) for pair in range(PAIRS)
    ]
    for pair in range(PAIRS):
        lo = low(pair)
        up_keys, up_values = raised[pair]
        for first in range(0, q_ref.shape[0], CROSS_ROWS):
            rows = slice(first, first + CROSS_ROWS)
            mixed, total = plain_softmax(q_ref[rows, lo], None, up_keys, up_values)
            cross_ref[rows, lo] = settled(oc_ref[rows, lo] + mixed, lc_ref[rows, lo] + total)


def join(mixed, total, cross, raised):
    fine = settled(mixed, total).astype(BF16).astype(F32)
    joined = fine + cross + raised
    return joined.astype(BF16), jnp.sum(joined.reshape(-1, 8, LANES) * 0.0, 0)


def inner_kernel(mixed_ref, total_ref, cross_ref, att_ref, up_ref, weight_ref, out_ref, bad_ref):
    rows = slice(EDGE, mixed_ref.shape[0] - EDGE)
    raised = dot(up_ref[...], att_ref[...])
    parts = [
        join(mixed_ref[rows, low(n)], total_ref[rows, low(n)], cross_ref[rows, low(n)], raised[:, low(n)])
        for n in range(PAIRS)
    ]
    bad_ref[...] = sum(bad for _, bad in parts)
    joined = jnp.concatenate([piece for piece, _ in parts], 1)
    out_ref[...] = dot(joined, weight_ref[...]).astype(BF16)


def late_kernel(
    q_ref, mixed_ref, total_ref, cross_ref, l0_ref, l1_ref, att_ref,
    chosen_ref, mask_ref, up_ref, weight_ref, inner_ref, inner_bad_ref,
    kv_hbm, f0_ref, f1_ref, r0_ref, r1_ref, ckv_ref, c0_ref, c1_ref, b0_ref, b1_ref,
    exact_chosen_hbm, exact_mask_hbm, early_hbm, late_hbm, up_inner_hbm,
    out_ref, joined_ref, bad_ref,
    kv_ref, exact_chosen_ref, exact_mask_ref, early_ref, late_ref, up_inner_ref, sems,
):
    cells = q_ref.shape[0]
    closed = pole_flags()
    pole = pole_table()
    up = up_ref[pole]
    mask = [close_edge(mask_ref[n * LATE_ROWS : (n + 1) * LATE_ROWS, :], closed[n]) for n in range(2)]
    mask = jnp.concatenate(mask, 0)
    corner = RADIUS * GROUP
    bad = inner_bad_ref[...]

    def raised_att(group, count):
        lanes = [slice((n + group) * LANES, (n + group + count) * LANES) for n in (0, PAIRS)]
        if count == 1:
            lanes = [low(group), high(group)]
        tops, bottoms = zip(*[before_after("lat", l0_ref, l1_ref, slice(ATT_ROWS, None), at) for at in lanes])
        return dot(up, jnp.concatenate([att_ref[:, lanes[0]], *tops, *bottoms], 0))

    def cornered(sums, part):
        west, east = part[:corner].reshape(-1, GROUP, LANES), part[corner:].reshape(-1, GROUP, LANES)
        rows = sums.reshape(-1, COLS, LANES)
        rows = jnp.concatenate(
            [rows[:, :GROUP] + west, rows[:, GROUP : COLS - GROUP], rows[:, COLS - GROUP :] + east], 1
        )
        return rows.reshape(-1, LANES)

    raised = [raised_att(pair, 2) for pair in range(0, PAIRS, 2)]
    parts = []
    for pair in range(PAIRS):
        lo, hi = low(pair), high(pair)
        corner_keys = before_after("lat", l0_ref, l1_ref, slice(None), lo)
        corner_values = before_after("lat", l0_ref, l1_ref, slice(None), hi)
        lift = raised[pair // 2][:, pair % 2 * LANES : (pair % 2 + 1) * LANES]
        outer = [slice(0, EDGE), slice(cells - EDGE, cells)]
        queries = [columns(q_ref[rows, lo], first) for rows in outer for first in (0, COLS - GROUP)]
        keys = jnp.concatenate([jnp.concatenate(corner_keys, 0), mask], 1)
        values = with_ones(jnp.concatenate(corner_values, 0))
        mixed, total = plain_softmax(jnp.concatenate(queries, 0), chosen_ref[...], keys, values)
        pieces = []
        for n, rows in enumerate(outer):
            at = slice(2 * n * corner, 2 * (n + 1) * corner)
            piece, wrong = join(
                cornered(mixed_ref[rows, lo], mixed[at]),
                cornered(total_ref[rows, lo], total[at]),
                cross_ref[rows, lo],
                lift[n * EDGE : (n + 1) * EDGE],
            )
            pieces.append(piece)
            bad += wrong
        parts.append(jnp.concatenate(pieces, 0))
    bad_ref[...] = bad
    outer = dot(jnp.concatenate(parts, 1), weight_ref[...]).astype(BF16)
    out_ref[:EDGE, :] = outer[:EDGE]
    out_ref[EDGE : cells - EDGE, :] = inner_ref[...]
    out_ref[cells - EDGE :, :] = outer[EDGE:]

    @pl.when(jnp.logical_not(jnp.sum(bad_ref[...]) == 0.0))
    def _():
        fetch(
            [(kv_hbm, kv_ref), (exact_chosen_hbm, exact_chosen_ref), (exact_mask_hbm, exact_mask_ref),
             (early_hbm, early_ref), (late_hbm, late_ref), (up_inner_hbm, up_inner_ref)],
            sems,
        )
        coarse = (ckv_ref, (c0_ref, c1_ref), (b0_ref, b1_ref))
        early, late = early_ref[...], late_ref[pole]
        count = len(EXACT_KEYS)
        edges = [cells + 2 * SIDE, cells + 2 * SIDE + EDGE + LATE_ROWS, count]

        @pl.loop(0, PAIRS)
        def _(pair):
            def all_of(lanes):
                left, right = before_after("lon", f0_ref, f1_ref, slice(None), lanes)
                top, bottom = before_after("lat", r0_ref, r1_ref, slice(None), lanes)
                late_top, late_bottom = before_after("lat", l0_ref, l1_ref, slice(None), lanes)
                return jnp.concatenate(
                    [kv_ref[:, lanes], left, right, top, late_top, bottom, late_bottom], 0
                )

            def up_of(lanes):
                first = dot(early, ckv_ref[:, lanes]).astype(BF16)
                return jnp.concatenate([first, dot(late, gathered(*coarse, lanes)).astype(BF16)], 0)

            lo, hi = low(pair), high(pair)
            keys, values = all_of(lo), with_ones(all_of(hi))
            up_keys, up_values = up_of(lo), with_ones(up_of(hi))
            outer, inner = raised_att(pair, 1), dot(up_inner_ref[...], att_ref[:, lo])
            raised = jnp.concatenate([outer[:EDGE], inner, outer[EDGE:]], 0)
            for block in range(BLOCKS):
                mask = exact_mask_ref[block * count : (block + 1) * count, :]
                mask = [mask[: edges[0]]] + [
                    close_edge(mask[edges[n] : edges[n + 1]], closed[n]) for n in range(2)
                ]
                rows = slice(block * BLOCK, (block + 1) * BLOCK)
                queries = q_ref[rows, lo]
                fine = exact_softmax(
                    queries,
                    exact_chosen_ref[rows, :],
                    jnp.concatenate([keys, jnp.concatenate(mask, 0)], 1),
                    values,
                )
                cross = exact_softmax(queries, None, up_keys, up_values)
                joined = fine.astype(BF16).astype(F32) + cross + raised[rows, :]
                joined_ref[pair, rows, :] = joined.astype(BF16)

        joined = jnp.concatenate([joined_ref[n] for n in range(PAIRS)], 1)
        out_ref[...] = dot(joined, weight_ref[...]).astype(BF16)


def constant(table):
    return jnp.asarray(table, BF16)


def call(kernel, name, outs, operands, flops, hbm=(), scratch=(), vmem=28, aliases={}):
    near = pl.BlockSpec(memory_space=pltpu.VMEM)
    far = pl.BlockSpec(memory_space=pltpu.HBM)
    moved_bytes = sum(x.size * x.dtype.itemsize for x in list(operands) + list(outs))
    return pl.pallas_call(
        kernel,
        in_specs=[far if n in hbm else near for n in range(len(operands))],
        out_specs=[near] * len(outs),
        out_shape=list(outs),
        scratch_shapes=list(scratch),
        input_output_aliases=dict(aliases),
        compiler_params=pltpu.CompilerParams(vmem_limit_bytes=vmem << 20),
        cost_estimate=pl.CostEstimate(
            flops=int(flops), bytes_accessed=int(moved_bytes if flops > 1e9 else moved_bytes // 16), transcendentals=int(flops / 1000)
        ),
        name=name,
    )(*operands)


def swap(array, above):
    size = lax.axis_size("lon")
    pairs = [(i, (i + 1) % size) for i in range(0 if above else 1, size, 2)]
    return lax.ppermute(array, "lon", pairs + [(b, a) for a, b in pairs])


def shift(array, step):
    size = lax.axis_size("lat")
    return lax.ppermute(array, "lat", [(i, (i + step) % size) for i in range(size)])


def ring(southward, northward):
    return shift(southward, 1), shift(northward, -1)


def shards(fine_query, fine_keyval, coarse_query, coarse_keyval, out_weight):
    channels = fine_query.shape[-1]
    cells = ROWS * COLS
    fq = fine_query.reshape(cells, channels)
    fkv = fine_keyval.reshape(cells, 2 * channels)
    cq = coarse_query.reshape(-1, channels)
    ckv = coarse_keyval.reshape(-1, 2 * channels)
    half = lambda rows: jax.ShapeDtypeStruct((rows, channels), BF16)
    full = lambda rows: jax.ShapeDtypeStruct((rows, 2 * channels), BF16)
    state = lambda rows: jax.ShapeDtypeStruct((rows, channels), F32)
    after = lax.optimization_barrier

    c0, c1 = call(
        send_coarse_kernel, "send_coarse", [full(48)] * 2, [jnp.concatenate([ckv, cq], 1)], 1e10, vmem=8
    )
    coarse0, coarse1 = swap(c0, True), swap(c1, False)
    near_kv, _ = after((fkv, c0))
    f0, f1, r0, r1 = call(
        send_fine_kernel, "send_fine", [full(SIDE)] * 2 + [full(EDGE)] * 2, [near_kv, constant(PICK_FINE)], 5e9
    )
    edge0 = shift(r0, 1)
    side0 = swap(f0, True)
    own_tables = [constant(OWN_CHOSEN), constant(OWN_MASK)]
    fq, near_kv, _ = after((fq, near_kv, f0))
    own = call(
        functools.partial(own_kernel, (0,)), "own_first", [state(cells)] * 2, [fq, near_kv, *own_tables], 2e9
    )
    f1, coarse0, coarse1, r0, own = after((f1, coarse0, coarse1, r0, own))
    coarse = (coarse0, coarse1)
    sides = (side0, swap(f1, False))
    ckv, _ = after((ckv, f1))
    (band,) = call(send_band_kernel, "send_band", [full(len(BAND))], [ckv, *coarse], 1e6)
    bands = ring(band, band)
    fq, near_kv, _ = after((fq, near_kv, band))
    own = call(
        functools.partial(own_kernel, (1, 2)), "own", [state(cells)] * 2, [fq, near_kv, *own_tables, *own], 3e9,
        aliases={4: 0, 5: 1},
    )
    fq, own = after((fq, own))
    early = call(early_cross_kernel, "early_cross", [state(cells)] * 2, [fq, ckv, constant(UP_EARLY)], 5e9)
    bands, early, r1 = after((bands, early, r1))
    edges = (edge0, shift(r1, -1))
    (coarse_att,) = call(
        coarse_kernel, "coarse", [half(len(COARSE_QUERIES))],
        [cq, ckv, *coarse, *bands, constant(COARSE_CHOSEN), constant(COARSE_MASK)], 2e9,
    )
    late0, late1 = call(
        send_late_kernel, "send_late", [full(LATE_ROWS)] * 2,
        [*sides, coarse_att] + [constant(table) for table in LATE_PICKS], 2e8,
    )
    lates = ring(late0, late1)
    fq, _ = after((fq, late0))
    (cross,) = call(
        late_cross_kernel, "late_cross", [state(cells)], [fq, *early, ckv, *coarse, *bands, constant(UP_LATE)], 1e8
    )
    fq, cross = after((fq, cross))
    sums = call(
        lon_kernel, "lon_strips", [state(cells)] * 2,
        [fq, *sides, constant(LON_CHOSEN), constant(LON_MASK), *own], 1e8, aliases={5: 0, 6: 1},
    )
    inner, inner_bad = call(
        inner_kernel, "inner", [half(cells - 2 * EDGE), jax.ShapeDtypeStruct((8, LANES), F32)],
        [*sums, cross, coarse_att, constant(UP_INNER), out_weight], 1e8,
    )
    fq, sums, _ = after((fq, sums, inner))
    sums = call(
        lat_kernel, "lat_strips", [state(cells)] * 2,
        [fq, *edges, constant(LAT_CHOSEN), constant(LAT_MASK), *sums], 1e8, aliases={5: 0, 6: 1},
    )
    exact = [constant(table) for table in (EXACT_CHOSEN, EXACT_MASK, UP_EARLY, UP_LATE, UP_INNER)]
    (out,) = call(
        late_kernel, "late", [half(cells)],
        [fq, *sums, cross, *lates, coarse_att, constant(CORNER_CHOSEN),
         constant(CORNER_MASK), constant(UP_OUTER), out_weight, inner, inner_bad,
         near_kv, *sides, *edges, ckv, *coarse, *bands, *exact],
        3e9,
        hbm=(13, 23, 24, 25, 26, 27),
        scratch=[
            pltpu.VMEM((PAIRS, cells, LANES), BF16), pltpu.VMEM((8, LANES), F32),
            pltpu.VMEM((cells, 2 * channels), BF16),
            *[pltpu.VMEM(x.shape, BF16) for x in exact], pltpu.SemaphoreType.DMA((6,)),
        ],
    )
    return out.reshape(ROWS, COLS, channels)


def solution(mesh):
    tiled = P("lat", "lon", None)
    return jax.shard_map(
        shards, mesh=mesh, in_specs=(tiled,) * 4 + (P(),), out_specs=tiled, check_vma=False
    )
```

```python
import functools
import math

import jax
import jax.numpy as jnp
import numpy as np
from jax import lax
from jax.experimental import pallas as pl
from jax.experimental.pallas import tpu as pltpu
from jax.sharding import PartitionSpec as P

HEADS = 8
RADIUS = 6
FACTOR = 4
ROWS, COLS = 24, 32
CROWS, CCOLS = 6, 8
LANES = 128
BLOCK_ROWS = 8
BLOCKS = ROWS // BLOCK_ROWS
BLOCK = BLOCK_ROWS * COLS
MASKED = -16384.0
EXPONENT = 0.125 * math.log2(math.e)
F32 = jnp.float32
BF16 = jnp.bfloat16


ROW_ORDER = list(range(2, 22)) + [0, 1, 22, 23]
LEFT_FINE = [(r, c - RADIUS) for r in ROW_ORDER for c in range(RADIUS)]
RIGHT_FINE = [(r, COLS + c) for r in ROW_ORDER for c in range(RADIUS)]
CORNER_TOP = list(range(0, 24)) + list(range(120, 132))
CORNER_BOTTOM = list(range(96, 120)) + list(range(132, 144))
CORNERS = 36
LATE_ROWS = 80
ATT_ROWS = 64


OWN_BLOCKS = [((0, 10), (0, 16)), ((10, 14), (4, 20)), ((14, 24), (8, 24))]


def corner_keys(top):
    picks = CORNER_BOTTOM if top else CORNER_TOP
    shift = -ROWS if top else ROWS
    keys = [(LEFT_FINE[i][0] + shift, LEFT_FINE[i][1]) for i in picks]
    keys += [(RIGHT_FINE[i][0] + shift, RIGHT_FINE[i][1]) for i in picks]
    return keys + [None] * (LATE_ROWS - len(keys))


def mask_lanes(keys, rows, cols):
    table = np.zeros((len(keys), LANES), np.float32)
    for n, key in enumerate(keys):
        if key is None:
            table[n, : len(rows) + len(cols)] = MASKED
            continue
        for i, row in enumerate(rows):
            if abs(key[0] - row) > RADIUS:
                table[n, i] = MASKED
        for j, col in enumerate(cols):
            if abs(key[1] - col) > RADIUS:
                table[n, len(rows) + j] = MASKED
    return table


def chosen_lanes(queries, rows, cols):
    table = np.zeros((len(queries), LANES), np.float32)
    for n, query in enumerate(queries):
        if query is None:
            continue
        table[n, rows.index(query[0])] = 1.0
        table[n, len(rows) + cols.index(query[1])] = 1.0
        table[n, LANES - 1] = 1.0
    return table


def cells_of(rows, cols):
    return [(r, c) for r in rows for c in cols]


FINE_COLS = list(range(COLS))
EDGE = RADIUS * COLS
GROUP = 8
WEST_COLS, EAST_COLS = list(range(GROUP)), list(range(COLS - GROUP, COLS))
ALL_ROWS = list(range(ROWS))
TOP_ROWS, BOTTOM_ROWS = list(range(RADIUS)), list(range(ROWS - RADIUS, ROWS))
TOP_FINE = cells_of(range(-RADIUS, 0), range(COLS))
BOTTOM_FINE = cells_of(range(ROWS, ROWS + RADIUS), range(COLS))
OWN_FINE = cells_of(ALL_ROWS, FINE_COLS)


def tables_of(queries, keys):
    rows = sorted({q[0] for q in queries})
    cols = sorted({q[1] for q in queries})
    return chosen_lanes(queries, rows, cols), mask_lanes(keys, rows, cols)


def stacked(pairs):
    made = [tables_of(*pair) for pair in pairs]
    return [np.concatenate(tables) for tables in zip(*made)]


OWN_CHOSEN, OWN_MASK = stacked(
    [
        (cells_of(range(*q), FINE_COLS), cells_of(range(*k), FINE_COLS))
        for q, k in OWN_BLOCKS
    ]
)
LON_CHOSEN, LON_MASK = stacked(
    [
        (cells_of(ALL_ROWS, WEST_COLS), LEFT_FINE),
        (cells_of(ALL_ROWS, EAST_COLS), RIGHT_FINE),
    ]
)
LAT_CHOSEN, LAT_MASK = stacked(
    [
        (cells_of(TOP_ROWS, FINE_COLS), TOP_FINE),
        (cells_of(BOTTOM_ROWS, FINE_COLS), BOTTOM_FINE),
    ]
)
OUTER_COLS = (WEST_COLS, EAST_COLS)
CORNER_CHOSEN, CORNER_MASK = tables_of(
    [cell for rows in (TOP_ROWS, BOTTOM_ROWS) for cols in OUTER_COLS for cell in cells_of(rows, cols)],
    corner_keys(True) + corner_keys(False),
)
EXACT_KEYS = (
    OWN_FINE + LEFT_FINE + RIGHT_FINE + TOP_FINE + corner_keys(True) + BOTTOM_FINE + corner_keys(False)
)
EXACT_CHOSEN, EXACT_MASK = stacked(
    [
        (cells_of(range(b * BLOCK_ROWS, (b + 1) * BLOCK_ROWS), FINE_COLS), EXACT_KEYS)
        for b in range(BLOCKS)
    ]
)

CQ_COLS = list(range(-1, CCOLS + 1))
OWN_COARSE = [(r, c) for r in range(CROWS) for c in range(CCOLS)]
LEFT_COARSE = [(r, c - 7) for r in range(CROWS) for c in range(7)] + [None] * CROWS
RIGHT_COARSE = [(r, c + CCOLS) for r in range(CROWS) for c in range(7)] + [None] * CROWS
BAND = OWN_COARSE + LEFT_COARSE + RIGHT_COARSE


def moved(keys, rows):
    return [None if key is None else (key[0] + rows, key[1]) for key in keys]


COARSE_KEYS = BAND + moved(BAND, -CROWS) + moved(BAND, CROWS)
COARSE_COUNT = 512
COARSE_KEYS = COARSE_KEYS + [None] * (COARSE_COUNT - len(COARSE_KEYS))
COARSE_QUERIES = (
    OWN_COARSE
    + [None] * 10
    + [(r, -1) for r in range(CROWS)]
    + [None] * 10
    + [(r, CCOLS) for r in range(CROWS)]
)
COARSE_CHOSEN = chosen_lanes(COARSE_QUERIES, list(range(CROWS)), CQ_COLS)
COARSE_MASK = mask_lanes(COARSE_KEYS, list(range(CROWS)), CQ_COLS)
LATE_CELLS_OF_ROW = [(0, c) for c in range(CCOLS)] + [(0, -1), (0, CCOLS)]


def late_cells(part):
    cells = LATE_CELLS_OF_ROW[part::2]
    before = 2 * CORNERS - ATT_ROWS
    return [None] * before + cells + [None] * (LATE_ROWS - ATT_ROWS - before - len(cells))


LATE_ATT = late_cells(0) + late_cells(1)
ATT_CELLS = COARSE_QUERIES + moved(LATE_ATT, -1) + moved(LATE_ATT, CROWS)


def coefficient(fine):
    coarse, offset = fine // FACTOR, (fine % FACTOR - 1.5) / FACTOR
    taps = {coarse: 1.0 - abs(offset)}
    taps[coarse + (1 if offset > 0 else -1)] = abs(offset)
    return taps


def up_table(fine_cells, coarse_cells, pole):
    where = {cell: n for n, cell in reversed(list(enumerate(coarse_cells))) if cell is not None}
    table = np.zeros((len(fine_cells), len(coarse_cells)), np.float32)
    for n, (row, col) in enumerate(fine_cells):
        for r, a in coefficient(row).items():
            if pole == "top":
                r = max(r, 0)
            if pole == "bottom":
                r = min(r, CROWS - 1)
            for c, b in coefficient(col).items():
                table[n, where[(r, c)]] += a * b
    return table


def poles(fine_cells, coarse_cells):
    return np.stack([up_table(fine_cells, coarse_cells, p) for p in ("none", "top", "bottom")])


FINE_CELLS = [(r, c) for r in range(ROWS) for c in range(COLS)]
INNER = [(r, c) for r in range(2, ROWS - 2) for c in range(2, COLS - 2)]
EARLY_COUNT = 512
EARLY_CELLS = INNER[:EARLY_COUNT]
LATE_CELLS = [cell for cell in FINE_CELLS if cell not in set(EARLY_CELLS)]
UP_EARLY = up_table(EARLY_CELLS, OWN_COARSE, "none")
UP_LATE = poles(LATE_CELLS, COARSE_KEYS)
INNER_CELLS = FINE_CELLS[EDGE:-EDGE]
UP_INNER = up_table(INNER_CELLS, COARSE_QUERIES, "none")
UP_OUTER = poles(FINE_CELLS[:EDGE] + FINE_CELLS[-EDGE:], ATT_CELLS)


def picked(indices, count):
    table = np.zeros((len(indices), count), np.float32)
    for n, index in enumerate(indices):
        if index is not None:
            table[n, index] = 1.0
    return table


FINE_EAST = [r * COLS // 2 + COLS // 2 - RADIUS + c for r in ROW_ORDER for c in range(RADIUS)]
FINE_WEST = [r * COLS // 2 + c for r in ROW_ORDER for c in range(RADIUS)]
PICK_FINE = picked(FINE_EAST + FINE_WEST, ROWS * COLS // 2)
SIDE = len(ROW_ORDER) * RADIUS


def late_picks(corner, row):
    rest = LATE_ROWS - 2 * CORNERS
    left = picked(list(corner) + [None] * (CORNERS + rest), SIDE)
    right = picked([None] * CORNERS + list(corner) + [None] * rest, SIDE)
    tables = [left, right]
    for part in range(2):
        cells = moved(late_cells(part), row)
        att = [None if cell is None else COARSE_QUERIES.index(cell) for cell in cells]
        tables.append(picked([None] * ATT_ROWS + att, len(COARSE_QUERIES)))
    return tables


LATE_PICKS = [
    np.concatenate(tables)
    for tables in zip(late_picks(CORNER_BOTTOM, CROWS - 1), late_picks(CORNER_TOP, 0))
]


PAIRS = HEADS // 2
LEAST, MOST = 2.0**-80, 2.0**100


def halves():
    return lax.broadcasted_iota(jnp.int32, (1, LANES), 1) < LANES // 2


def head_of(pair, head):
    return jnp.where(halves() == (head == 0), pair, jnp.zeros((), pair.dtype))


def packed(first, second):
    return jnp.where(halves(), first, second)


def dot(a, b):
    return jnp.dot(a, b, preferred_element_type=F32)


def scores(queries, keys):
    return lax.dot_general(queries, keys, (((1,), (1,)), ((), ())), preferred_element_type=F32)


def mix(weights, values):
    mixed = dot(weights.astype(BF16), values)
    return mixed[:, :LANES], mixed[:, LANES:]


def with_ones(values):
    return jnp.concatenate([values, jnp.ones_like(values)], 1)


def even(axis):
    return lax.axis_index(axis) % 2 == 0


def pole_flags():
    lat = lax.axis_index("lat")
    return lat == 0, lat == lax.axis_size("lat") - 1


def pole_table():
    is_top, is_bottom = pole_flags()
    return jnp.where(is_top, 1, jnp.where(is_bottom, 2, 0))


def lanes_of(group):
    if isinstance(group, int):
        return slice(group * LANES, (group + 1) * LANES)
    return pl.ds(pl.multiple_of(group * LANES, LANES), LANES)


def low(pair):
    return lanes_of(pair)


def high(pair):
    return lanes_of(pair + PAIRS)


def close_edge(mask, closed):
    lane = lax.broadcasted_iota(jnp.int32, (1, LANES), 1)
    return jnp.where((lane == LANES - 1) & closed, MASKED, mask.astype(F32)).astype(BF16)


def before_after(axis, first, second, *index):
    a, b = first[index], second[index]
    if axis == "lat":
        return a, b
    return jnp.where(even(axis), b, a), jnp.where(even(axis), a, b)


def both_heads(queries, chosen):
    rows = jnp.concatenate([head_of(queries, 0), head_of(queries, 1)], 0)
    if chosen is None:
        return rows
    return jnp.concatenate([rows, jnp.concatenate([chosen, chosen], 0)], 1)


def plain_softmax(queries, chosen, keys, values):
    count = queries.shape[0]
    mixed, total = mix(jnp.exp2(scores(both_heads(queries, chosen), keys) * EXPONENT), values)
    return packed(mixed[:count], mixed[count:]), packed(total[:count], total[count:])


def exact_softmax(queries, chosen, keys, values):
    count = queries.shape[0]
    score = scores(both_heads(queries, chosen), keys)
    score = score - jnp.max(score, 1, keepdims=True)
    mixed, total = mix(jnp.exp2(score * EXPONENT), values)
    result = mixed / total
    return packed(result[:count], result[count:])


def settled(mixed, total):
    fits = (total > LEAST) & (total < MOST)
    return jnp.where(fits, mixed / total, jnp.nan)


def fetch(moves, sems):
    copies = [pltpu.make_async_copy(a, b, sems.at[n]) for n, (a, b) in enumerate(moves)]
    for copy in copies:
        copy.start()
    for copy in copies:
        copy.wait()


def send_coarse_kernel(both_ref, c0_ref, c1_ref):
    channels = both_ref.shape[1] // 3
    n = lax.broadcasted_iota(jnp.int32, (48, CROWS * CCOLS), 0)
    cell = lax.broadcasted_iota(jnp.int32, (48, CROWS * CCOLS), 1)
    row = (n * 37) >> 8
    sides = []
    for first, col in ((1, CCOLS - 1), (0, 0)):
        keyval = (n < 42) & (cell == row * CCOLS + first + n - row * 7)
        query = (n >= 42) & (cell == (n - 42) * CCOLS + col)
        both = dot(keyval.astype(F32).astype(BF16), both_ref[:, : 2 * channels])
        query = dot(query.astype(F32).astype(BF16), both_ref[:, 2 * channels :])
        sides.append(jnp.concatenate([both[:, :channels] + query, both[:, channels:]], 1).astype(BF16))
    eastward = even("lon")
    c0_ref[...] = jnp.where(eastward, sides[0], sides[1])
    c1_ref[...] = jnp.where(eastward, sides[1], sides[0])


def send_fine_kernel(fkv_ref, pick_ref, f0_ref, f1_ref, r0_ref, r1_ref):
    cells = fkv_ref.shape[0]
    halves_of_rows = fkv_ref[...].reshape(ROWS, COLS, -1)
    east = halves_of_rows[:, COLS // 2 :].reshape(ROWS * COLS // 2, -1)
    west = halves_of_rows[:, : COLS // 2].reshape(ROWS * COLS // 2, -1)
    fine = [dot(pick_ref[:SIDE], east).astype(BF16), dot(pick_ref[SIDE:], west).astype(BF16)]
    eastward = even("lon")
    f0_ref[...] = jnp.where(eastward, fine[0], fine[1])
    f1_ref[...] = jnp.where(eastward, fine[1], fine[0])
    r0_ref[...] = fkv_ref[cells - EDGE :, :]
    r1_ref[...] = fkv_ref[:EDGE, :]


def send_band_kernel(ckv_ref, c0_ref, c1_ref, band_ref):
    left, right = before_after("lon", c0_ref, c1_ref, slice(None), slice(None))
    band_ref[0:48, :] = ckv_ref[...]
    band_ref[48:96, :] = left
    band_ref[96:144, :] = right


def send_late_kernel(f0_ref, f1_ref, att_ref, pl_ref, pr_ref, pa_ref, pb_ref, l0_ref, l1_ref):
    left, right = before_after("lon", f0_ref, f1_ref, slice(None), slice(None))
    sides = dot(pl_ref[...], left) + dot(pr_ref[...], right)
    att = jnp.concatenate([dot(pa_ref[...], att_ref[...]), dot(pb_ref[...], att_ref[...])], 1)
    late = (sides + att).astype(BF16)
    l0_ref[...], l1_ref[...] = late[:LATE_ROWS], late[LATE_ROWS:]


def own_kernel(blocks, q_ref, kv_ref, chosen_ref, mask_ref, *refs):
    mixed_ref, total_ref = refs[-2:]
    for pair in range(PAIRS):
        lo, hi = low(pair), high(pair)
        for block in blocks:
            (q0, q1), (k0, k1) = OWN_BLOCKS[block]
            rows = slice(q0 * COLS, q1 * COLS)
            near = slice(k0 * COLS, k1 * COLS)
            size = (k1 - k0) * COLS
            mask = mask_ref[block * size : (block + 1) * size, :]
            keys = jnp.concatenate([kv_ref[near, lo], mask], 1)
            mixed_ref[rows, lo], total_ref[rows, lo] = plain_softmax(
                q_ref[rows, lo], chosen_ref[rows, :], keys, with_ones(kv_ref[near, hi])
            )


CROSS_ROWS = 768


def raise_pair(table, keys, values):
    both = dot(table, jnp.concatenate([keys, values], 1)).astype(BF16)
    return both[:, :LANES], with_ones(both[:, LANES:])


def early_cross_kernel(q_ref, ckv_ref, up_ref, mixed_ref, total_ref):
    up = up_ref[...]
    raised = [raise_pair(up, ckv_ref[:, low(pair)], ckv_ref[:, high(pair)]) for pair in range(PAIRS)]
    for pair in range(PAIRS):
        lo = low(pair)
        up_keys, up_values = raised[pair]
        for first in range(0, q_ref.shape[0], CROSS_ROWS):
            rows = slice(first, first + CROSS_ROWS)
            mixed_ref[rows, lo], total_ref[rows, lo] = plain_softmax(
                q_ref[rows, lo], None, up_keys, up_values
            )


def columns(queries, first):
    rows = queries.shape[0] // COLS
    split = queries.astype(F32).reshape(rows, COLS, LANES)[:, first : first + GROUP]
    return split.reshape(rows * GROUP, LANES).astype(BF16)


def lon_kernel(q_ref, f0_ref, f1_ref, chosen_ref, mask_ref, om_ref, ot_ref, mixed_ref, total_ref):
    strip = ROWS * GROUP
    for pair in range(PAIRS):
        lo, hi = low(pair), high(pair)
        keys = before_after("lon", f0_ref, f1_ref, slice(None), lo)
        values = before_after("lon", f0_ref, f1_ref, slice(None), hi)
        queries = q_ref[:, lo]
        for n, first in enumerate((0, COLS - GROUP)):
            mixed, total = plain_softmax(
                columns(queries, first),
                chosen_ref[n * strip : (n + 1) * strip, :],
                jnp.concatenate([keys[n], mask_ref[n * SIDE : (n + 1) * SIDE, :]], 1),
                with_ones(values[n]),
            )
            for row in range(ROWS):
                at = slice(row * COLS + first, row * COLS + first + GROUP)
                piece = slice(row * GROUP, (row + 1) * GROUP)
                mixed_ref[at, lo] = om_ref[at, lo] + mixed[piece]
                total_ref[at, lo] = ot_ref[at, lo] + total[piece]


def lat_kernel(q_ref, r0_ref, r1_ref, chosen_ref, mask_ref, om_ref, ot_ref, mixed_ref, total_ref):
    cells = q_ref.shape[0]
    closed = pole_flags()
    masks = [close_edge(mask_ref[n * EDGE : (n + 1) * EDGE, :], closed[n]) for n in range(2)]
    for pair in range(PAIRS):
        lo, hi = low(pair), high(pair)
        keys = before_after("lat", r0_ref, r1_ref, slice(None), lo)
        values = before_after("lat", r0_ref, r1_ref, slice(None), hi)
        for n, first in enumerate((0, cells - EDGE)):
            rows = slice(first, first + EDGE)
            mixed, total = plain_softmax(
                q_ref[rows, lo],
                chosen_ref[n * EDGE : (n + 1) * EDGE, :],
                jnp.concatenate([keys[n], masks[n]], 1),
                with_ones(values[n]),
            )
            mixed_ref[rows, lo] = om_ref[rows, lo] + mixed
            total_ref[rows, lo] = ot_ref[rows, lo] + total


def gathered(own, coarse, band, lanes):
    left, right = before_after("lon", *coarse, slice(None), lanes)
    top, bottom = before_after("lat", *band, slice(None), lanes)
    pad = jnp.zeros((COARSE_COUNT - 3 * len(BAND), LANES), BF16)
    return jnp.concatenate([own[:, lanes], left, right, top, bottom, pad], 0)


def coarse_kernel(q_ref, own_ref, c0_ref, c1_ref, b0_ref, b1_ref, chosen_ref, mask_ref, out_ref):
    is_top, is_bottom = pole_flags()
    band = len(BAND)
    mask = [
        mask_ref[:band, :],
        close_edge(mask_ref[band : 2 * band, :], is_top),
        close_edge(mask_ref[2 * band :, :], is_bottom),
    ]
    mask = jnp.concatenate(mask, 0)
    chosen = chosen_ref[...]
    for pair in range(PAIRS):
        lo = slice(pair * LANES, (pair + 1) * LANES)
        hi = slice((pair + PAIRS) * LANES, (pair + PAIRS + 1) * LANES)
        keys = jnp.concatenate([gathered(own_ref, (c0_ref, c1_ref), (b0_ref, b1_ref), lo), mask], 1)
        values = with_ones(gathered(own_ref, (c0_ref, c1_ref), (b0_ref, b1_ref), hi))
        left, right = before_after("lon", c0_ref, c1_ref, slice(32, 48), lo)
        queries = jnp.concatenate([q_ref[:, lo], left, right], 0)
        out_ref[:, lo] = exact_softmax(queries, chosen, keys, values).astype(BF16)


def late_cross_kernel(q_ref, oc_ref, lc_ref, ckv_ref, c0_ref, c1_ref, b0_ref, b1_ref, late_ref, cross_ref):
    late = late_ref[pole_table()]
    coarse = (ckv_ref, (c0_ref, c1_ref), (b0_ref, b1_ref))
    raised = [
        raise_pair(late, gathered(*coarse, low(pair)), gathered(*coarse, high(pair))) for pair in range(PAIRS)
    ]
    for pair in range(PAIRS):
        lo = low(pair)
        up_keys, up_values = raised[pair]
        for first in range(0, q_ref.shape[0], CROSS_ROWS):
            rows = slice(first, first + CROSS_ROWS)
            mixed, total = plain_softmax(q_ref[rows, lo], None, up_keys, up_values)
            cross_ref[rows, lo] = settled(oc_ref[rows, lo] + mixed, lc_ref[rows, lo] + total)


def join(mixed, total, cross, raised):
    fine = settled(mixed, total).astype(BF16).astype(F32)
    joined = fine + cross + raised
    return joined.astype(BF16), jnp.sum(joined.reshape(-1, 8, LANES) * 0.0, 0)


def inner_kernel(mixed_ref, total_ref, cross_ref, att_ref, up_ref, weight_ref, out_ref, bad_ref):
    rows = slice(EDGE, mixed_ref.shape[0] - EDGE)
    raised = dot(up_ref[...], att_ref[...])
    parts = [
        join(mixed_ref[rows, low(n)], total_ref[rows, low(n)], cross_ref[rows, low(n)], raised[:, low(n)])
        for n in range(PAIRS)
    ]
    bad_ref[...] = sum(bad for _, bad in parts)
    joined = jnp.concatenate([piece for piece, _ in parts], 1)
    out_ref[...] = dot(joined, weight_ref[...]).astype(BF16)


def lon_inner_kernel(
    q_ref, f0_ref, f1_ref, chosen_ref, mask_ref, om_ref, ot_ref, cross_ref, att_ref, up_ref, weight_ref,
    mixed_ref, total_ref, out_ref, bad_ref,
):
    lon_kernel(q_ref, f0_ref, f1_ref, chosen_ref, mask_ref, om_ref, ot_ref, mixed_ref, total_ref)
    inner_kernel(mixed_ref, total_ref, cross_ref, att_ref, up_ref, weight_ref, out_ref, bad_ref)


def late_kernel(
    q_ref, mixed_ref, total_ref, cross_ref, l0_ref, l1_ref, att_ref,
    chosen_ref, mask_ref, up_ref, weight_ref, inner_ref, inner_bad_ref,
    kv_hbm, f0_ref, f1_ref, r0_ref, r1_ref, ckv_ref, c0_ref, c1_ref, b0_ref, b1_ref,
    exact_chosen_hbm, exact_mask_hbm, early_hbm, late_hbm, up_inner_hbm,
    out_ref, joined_ref, bad_ref,
    kv_ref, exact_chosen_ref, exact_mask_ref, early_ref, late_ref, up_inner_ref, sems,
):
    cells = q_ref.shape[0]
    closed = pole_flags()
    pole = pole_table()
    up = up_ref[pole]
    mask = [close_edge(mask_ref[n * LATE_ROWS : (n + 1) * LATE_ROWS, :], closed[n]) for n in range(2)]
    mask = jnp.concatenate(mask, 0)
    corner = RADIUS * GROUP
    bad = inner_bad_ref[...]

    def raised_att(group, count):
        lanes = [slice((n + group) * LANES, (n + group + count) * LANES) for n in (0, PAIRS)]
        if count == 1:
            lanes = [low(group), high(group)]
        tops, bottoms = zip(*[before_after("lat", l0_ref, l1_ref, slice(ATT_ROWS, None), at) for at in lanes])
        return dot(up, jnp.concatenate([att_ref[:, lanes[0]], *tops, *bottoms], 0))

    def cornered(sums, part):
        west, east = part[:corner].reshape(-1, GROUP, LANES), part[corner:].reshape(-1, GROUP, LANES)
        rows = sums.reshape(-1, COLS, LANES)
        rows = jnp.concatenate(
            [rows[:, :GROUP] + west, rows[:, GROUP : COLS - GROUP], rows[:, COLS - GROUP :] + east], 1
        )
        return rows.reshape(-1, LANES)

    raised = [raised_att(pair, 2) for pair in range(0, PAIRS, 2)]
    parts = []
    for pair in range(PAIRS):
        lo, hi = low(pair), high(pair)
        corner_keys = before_after("lat", l0_ref, l1_ref, slice(None), lo)
        corner_values = before_after("lat", l0_ref, l1_ref, slice(None), hi)
        lift = raised[pair // 2][:, pair % 2 * LANES : (pair % 2 + 1) * LANES]
        outer = [slice(0, EDGE), slice(cells - EDGE, cells)]
        queries = [columns(q_ref[rows, lo], first) for rows in outer for first in (0, COLS - GROUP)]
        keys = jnp.concatenate([jnp.concatenate(corner_keys, 0), mask], 1)
        values = with_ones(jnp.concatenate(corner_values, 0))
        mixed, total = plain_softmax(jnp.concatenate(queries, 0), chosen_ref[...], keys, values)
        pieces = []
        for n, rows in enumerate(outer):
            at = slice(2 * n * corner, 2 * (n + 1) * corner)
            piece, wrong = join(
                cornered(mixed_ref[rows, lo], mixed[at]),
                cornered(total_ref[rows, lo], total[at]),
                cross_ref[rows, lo],
                lift[n * EDGE : (n + 1) * EDGE],
            )
            pieces.append(piece)
            bad += wrong
        parts.append(jnp.concatenate(pieces, 0))
    bad_ref[...] = bad
    outer = dot(jnp.concatenate(parts, 1), weight_ref[...]).astype(BF16)
    out_ref[:EDGE, :] = outer[:EDGE]
    out_ref[EDGE : cells - EDGE, :] = inner_ref[...]
    out_ref[cells - EDGE :, :] = outer[EDGE:]

    @pl.when(jnp.logical_not(jnp.sum(bad_ref[...]) == 0.0))
    def _():
        fetch(
            [(kv_hbm, kv_ref), (exact_chosen_hbm, exact_chosen_ref), (exact_mask_hbm, exact_mask_ref),
             (early_hbm, early_ref), (late_hbm, late_ref), (up_inner_hbm, up_inner_ref)],
            sems,
        )
        coarse = (ckv_ref, (c0_ref, c1_ref), (b0_ref, b1_ref))
        early, late = early_ref[...], late_ref[pole]
        count = len(EXACT_KEYS)
        edges = [cells + 2 * SIDE, cells + 2 * SIDE + EDGE + LATE_ROWS, count]

        @pl.loop(0, PAIRS)
        def _(pair):
            def all_of(lanes):
                left, right = before_after("lon", f0_ref, f1_ref, slice(None), lanes)
                top, bottom = before_after("lat", r0_ref, r1_ref, slice(None), lanes)
                late_top, late_bottom = before_after("lat", l0_ref, l1_ref, slice(None), lanes)
                return jnp.concatenate(
                    [kv_ref[:, lanes], left, right, top, late_top, bottom, late_bottom], 0
                )

            def up_of(lanes):
                first = dot(early, ckv_ref[:, lanes]).astype(BF16)
                return jnp.concatenate([first, dot(late, gathered(*coarse, lanes)).astype(BF16)], 0)

            lo, hi = low(pair), high(pair)
            keys, values = all_of(lo), with_ones(all_of(hi))
            up_keys, up_values = up_of(lo), with_ones(up_of(hi))
            outer, inner = raised_att(pair, 1), dot(up_inner_ref[...], att_ref[:, lo])
            raised = jnp.concatenate([outer[:EDGE], inner, outer[EDGE:]], 0)
            for block in range(BLOCKS):
                mask = exact_mask_ref[block * count : (block + 1) * count, :]
                mask = [mask[: edges[0]]] + [
                    close_edge(mask[edges[n] : edges[n + 1]], closed[n]) for n in range(2)
                ]
                rows = slice(block * BLOCK, (block + 1) * BLOCK)
                queries = q_ref[rows, lo]
                fine = exact_softmax(
                    queries,
                    exact_chosen_ref[rows, :],
                    jnp.concatenate([keys, jnp.concatenate(mask, 0)], 1),
                    values,
                )
                cross = exact_softmax(queries, None, up_keys, up_values)
                joined = fine.astype(BF16).astype(F32) + cross + raised[rows, :]
                joined_ref[pair, rows, :] = joined.astype(BF16)

        joined = jnp.concatenate([joined_ref[n] for n in range(PAIRS)], 1)
        out_ref[...] = dot(joined, weight_ref[...]).astype(BF16)


def constant(table):
    return jnp.asarray(table, BF16)


def call(kernel, name, outs, operands, flops, hbm=(), scratch=(), vmem=28, aliases={}):
    near = pl.BlockSpec(memory_space=pltpu.VMEM)
    far = pl.BlockSpec(memory_space=pltpu.HBM)
    moved_bytes = sum(x.size * x.dtype.itemsize for x in list(operands) + list(outs))
    return pl.pallas_call(
        kernel,
        in_specs=[far if n in hbm else near for n in range(len(operands))],
        out_specs=[near] * len(outs),
        out_shape=list(outs),
        scratch_shapes=list(scratch),
        input_output_aliases=dict(aliases),
        compiler_params=pltpu.CompilerParams(vmem_limit_bytes=vmem << 20),
        cost_estimate=pl.CostEstimate(
            flops=int(flops), bytes_accessed=int(moved_bytes if flops > 1e9 else moved_bytes // 16), transcendentals=int(flops / 1000)
        ),
        name=name,
    )(*operands)


def swap(array, above):
    size = lax.axis_size("lon")
    pairs = [(i, (i + 1) % size) for i in range(0 if above else 1, size, 2)]
    return lax.ppermute(array, "lon", pairs + [(b, a) for a, b in pairs])


def shift(array, step):
    size = lax.axis_size("lat")
    return lax.ppermute(array, "lat", [(i, (i + step) % size) for i in range(size)])


def ring(southward, northward):
    return shift(southward, 1), shift(northward, -1)


def shards(fine_query, fine_keyval, coarse_query, coarse_keyval, out_weight):
    channels = fine_query.shape[-1]
    cells = ROWS * COLS
    fq = fine_query.reshape(cells, channels)
    fkv = fine_keyval.reshape(cells, 2 * channels)
    cq = coarse_query.reshape(-1, channels)
    ckv = coarse_keyval.reshape(-1, 2 * channels)
    half = lambda rows: jax.ShapeDtypeStruct((rows, channels), BF16)
    full = lambda rows: jax.ShapeDtypeStruct((rows, 2 * channels), BF16)
    state = lambda rows: jax.ShapeDtypeStruct((rows, channels), F32)
    after = lax.optimization_barrier

    c0, c1 = call(
        send_coarse_kernel, "send_coarse", [full(48)] * 2, [jnp.concatenate([ckv, cq], 1)], 1e10, vmem=8
    )
    coarse0, coarse1 = swap(c0, True), swap(c1, False)
    near_kv, _ = after((fkv, c0))
    f0, f1, r0, r1 = call(
        send_fine_kernel, "send_fine", [full(SIDE)] * 2 + [full(EDGE)] * 2, [near_kv, constant(PICK_FINE)], 5e9
    )
    edge0 = shift(r0, 1)
    side0 = swap(f0, True)
    own_tables = [constant(OWN_CHOSEN), constant(OWN_MASK)]
    fq, near_kv, _ = after((fq, near_kv, f0))
    own = call(
        functools.partial(own_kernel, (0,)), "own_first", [state(cells)] * 2, [fq, near_kv, *own_tables], 2e9
    )
    f1, coarse0, coarse1, r0, own = after((f1, coarse0, coarse1, r0, own))
    coarse = (coarse0, coarse1)
    sides = (side0, swap(f1, False))
    ckv, _ = after((ckv, f1))
    (band,) = call(send_band_kernel, "send_band", [full(len(BAND))], [ckv, *coarse], 1e6)
    bands = ring(band, band)
    fq, near_kv, _ = after((fq, near_kv, band))
    own = call(
        functools.partial(own_kernel, (1, 2)), "own", [state(cells)] * 2, [fq, near_kv, *own_tables, *own], 3e9,
        aliases={4: 0, 5: 1},
    )
    fq, own = after((fq, own))
    early = call(early_cross_kernel, "early_cross", [state(cells)] * 2, [fq, ckv, constant(UP_EARLY)], 5e9)
    bands, early, r1 = after((bands, early, r1))
    edges = (edge0, shift(r1, -1))
    (coarse_att,) = call(
        coarse_kernel, "coarse", [half(len(COARSE_QUERIES))],
        [cq, ckv, *coarse, *bands, constant(COARSE_CHOSEN), constant(COARSE_MASK)], 2e9,
    )
    late0, late1 = call(
        send_late_kernel, "send_late", [full(LATE_ROWS)] * 2,
        [*sides, coarse_att] + [constant(table) for table in LATE_PICKS], 2e8,
    )
    lates = ring(late0, late1)
    fq, _ = after((fq, late0))
    (cross,) = call(
        late_cross_kernel, "late_cross", [state(cells)], [fq, *early, ckv, *coarse, *bands, constant(UP_LATE)], 1e8
    )
    fq, cross = after((fq, cross))
    *sums, inner, inner_bad = call(
        lon_inner_kernel, "lon_inner",
        [state(cells)] * 2 + [half(cells - 2 * EDGE), jax.ShapeDtypeStruct((8, LANES), F32)],
        [fq, *sides, constant(LON_CHOSEN), constant(LON_MASK), *own, cross, coarse_att, constant(UP_INNER), out_weight],
        1e8, aliases={5: 0, 6: 1},
    )
    fq, sums, _ = after((fq, sums, inner))
    sums = call(
        lat_kernel, "lat_strips", [state(cells)] * 2,
        [fq, *edges, constant(LAT_CHOSEN), constant(LAT_MASK), *sums], 1e8, aliases={5: 0, 6: 1},
    )
    exact = [constant(table) for table in (EXACT_CHOSEN, EXACT_MASK, UP_EARLY, UP_LATE, UP_INNER)]
    (out,) = call(
        late_kernel, "late", [half(cells)],
        [fq, *sums, cross, *lates, coarse_att, constant(CORNER_CHOSEN),
         constant(CORNER_MASK), constant(UP_OUTER), out_weight, inner, inner_bad,
         near_kv, *sides, *edges, ckv, *coarse, *bands, *exact],
        3e9,
        hbm=(13, 23, 24, 25, 26, 27),
        scratch=[
            pltpu.VMEM((PAIRS, cells, LANES), BF16), pltpu.VMEM((8, LANES), F32),
            pltpu.VMEM((cells, 2 * channels), BF16),
            *[pltpu.VMEM(x.shape, BF16) for x in exact], pltpu.SemaphoreType.DMA((6,)),
        ],
    )
    return out.reshape(ROWS, COLS, channels)


def solution(mesh):
    tiled = P("lat", "lon", None)
    return jax.shard_map(
        shards, mesh=mesh, in_specs=(tiled,) * 4 + (P(),), out_specs=tiled, check_vma=False
    )
```

```python
import functools
import math

import jax
import jax.numpy as jnp
import numpy as np
from jax import lax
from jax.experimental import pallas as pl
from jax.experimental.pallas import tpu as pltpu
from jax.sharding import PartitionSpec as P

HEADS = 8
RADIUS = 6
FACTOR = 4
ROWS, COLS = 24, 32
CROWS, CCOLS = 6, 8
LANES = 128
BLOCK_ROWS = 8
BLOCKS = ROWS // BLOCK_ROWS
BLOCK = BLOCK_ROWS * COLS
MASKED = -16384.0
EXPONENT = 0.125 * math.log2(math.e)
F32 = jnp.float32
BF16 = jnp.bfloat16


ROW_ORDER = list(range(2, 22)) + [0, 1, 22, 23]
LEFT_FINE = [(r, c - RADIUS) for r in ROW_ORDER for c in range(RADIUS)]
RIGHT_FINE = [(r, COLS + c) for r in ROW_ORDER for c in range(RADIUS)]
CORNER_TOP = list(range(0, 24)) + list(range(120, 132))
CORNER_BOTTOM = list(range(96, 120)) + list(range(132, 144))
CORNERS = 36
LATE_ROWS = 80
ATT_ROWS = 64


OWN_BLOCKS = [((0, 10), (0, 16)), ((10, 14), (4, 20)), ((14, 24), (8, 24))]


def corner_keys(top):
    picks = CORNER_BOTTOM if top else CORNER_TOP
    shift = -ROWS if top else ROWS
    keys = [(LEFT_FINE[i][0] + shift, LEFT_FINE[i][1]) for i in picks]
    keys += [(RIGHT_FINE[i][0] + shift, RIGHT_FINE[i][1]) for i in picks]
    return keys + [None] * (LATE_ROWS - len(keys))


def mask_lanes(keys, rows, cols):
    table = np.zeros((len(keys), LANES), np.float32)
    for n, key in enumerate(keys):
        if key is None:
            table[n, : len(rows) + len(cols)] = MASKED
            continue
        for i, row in enumerate(rows):
            if abs(key[0] - row) > RADIUS:
                table[n, i] = MASKED
        for j, col in enumerate(cols):
            if abs(key[1] - col) > RADIUS:
                table[n, len(rows) + j] = MASKED
    return table


def chosen_lanes(queries, rows, cols):
    table = np.zeros((len(queries), LANES), np.float32)
    for n, query in enumerate(queries):
        if query is None:
            continue
        table[n, rows.index(query[0])] = 1.0
        table[n, len(rows) + cols.index(query[1])] = 1.0
        table[n, LANES - 1] = 1.0
    return table


def cells_of(rows, cols):
    return [(r, c) for r in rows for c in cols]


FINE_COLS = list(range(COLS))
EDGE = RADIUS * COLS
GROUP = 8
WEST_COLS, EAST_COLS = list(range(GROUP)), list(range(COLS - GROUP, COLS))
ALL_ROWS = list(range(ROWS))
TOP_ROWS, BOTTOM_ROWS = list(range(RADIUS)), list(range(ROWS - RADIUS, ROWS))
TOP_FINE = cells_of(range(-RADIUS, 0), range(COLS))
BOTTOM_FINE = cells_of(range(ROWS, ROWS + RADIUS), range(COLS))
OWN_FINE = cells_of(ALL_ROWS, FINE_COLS)


def tables_of(queries, keys):
    rows = sorted({q[0] for q in queries})
    cols = sorted({q[1] for q in queries})
    return chosen_lanes(queries, rows, cols), mask_lanes(keys, rows, cols)


def stacked(pairs):
    made = [tables_of(*pair) for pair in pairs]
    return [np.concatenate(tables) for tables in zip(*made)]


OWN_CHOSEN, OWN_MASK = stacked(
    [
        (cells_of(range(*q), FINE_COLS), cells_of(range(*k), FINE_COLS))
        for q, k in OWN_BLOCKS
    ]
)
LON_CHOSEN, LON_MASK = stacked(
    [
        (cells_of(ALL_ROWS, WEST_COLS), LEFT_FINE),
        (cells_of(ALL_ROWS, EAST_COLS), RIGHT_FINE),
    ]
)
LAT_CHOSEN, LAT_MASK = stacked(
    [
        (cells_of(TOP_ROWS, FINE_COLS), TOP_FINE),
        (cells_of(BOTTOM_ROWS, FINE_COLS), BOTTOM_FINE),
    ]
)
OUTER_COLS = (WEST_COLS, EAST_COLS)
CORNER_CHOSEN, CORNER_MASK = tables_of(
    [cell for rows in (TOP_ROWS, BOTTOM_ROWS) for cols in OUTER_COLS for cell in cells_of(rows, cols)],
    corner_keys(True) + corner_keys(False),
)
EXACT_KEYS = (
    OWN_FINE + LEFT_FINE + RIGHT_FINE + TOP_FINE + corner_keys(True) + BOTTOM_FINE + corner_keys(False)
)
EXACT_CHOSEN, EXACT_MASK = stacked(
    [
        (cells_of(range(b * BLOCK_ROWS, (b + 1) * BLOCK_ROWS), FINE_COLS), EXACT_KEYS)
        for b in range(BLOCKS)
    ]
)

CQ_COLS = list(range(-1, CCOLS + 1))
OWN_COARSE = [(r, c) for r in range(CROWS) for c in range(CCOLS)]
LEFT_COARSE = [(r, c - 7) for r in range(CROWS) for c in range(7)] + [None] * CROWS
RIGHT_COARSE = [(r, c + CCOLS) for r in range(CROWS) for c in range(7)] + [None] * CROWS
BAND = OWN_COARSE + LEFT_COARSE + RIGHT_COARSE


def moved(keys, rows):
    return [None if key is None else (key[0] + rows, key[1]) for key in keys]


COARSE_KEYS = BAND + moved(BAND, -CROWS) + moved(BAND, CROWS)
COARSE_COUNT = 512
COARSE_KEYS = COARSE_KEYS + [None] * (COARSE_COUNT - len(COARSE_KEYS))
COARSE_QUERIES = (
    OWN_COARSE
    + [None] * 10
    + [(r, -1) for r in range(CROWS)]
    + [None] * 10
    + [(r, CCOLS) for r in range(CROWS)]
)
COARSE_CHOSEN = chosen_lanes(COARSE_QUERIES, list(range(CROWS)), CQ_COLS)
COARSE_MASK = mask_lanes(COARSE_KEYS, list(range(CROWS)), CQ_COLS)
LATE_CELLS_OF_ROW = [(0, c) for c in range(CCOLS)] + [(0, -1), (0, CCOLS)]


def late_cells(part):
    cells = LATE_CELLS_OF_ROW[part::2]
    before = 2 * CORNERS - ATT_ROWS
    return [None] * before + cells + [None] * (LATE_ROWS - ATT_ROWS - before - len(cells))


LATE_ATT = late_cells(0) + late_cells(1)
ATT_CELLS = COARSE_QUERIES + moved(LATE_ATT, -1) + moved(LATE_ATT, CROWS)


def coefficient(fine):
    coarse, offset = fine // FACTOR, (fine % FACTOR - 1.5) / FACTOR
    taps = {coarse: 1.0 - abs(offset)}
    taps[coarse + (1 if offset > 0 else -1)] = abs(offset)
    return taps


def up_table(fine_cells, coarse_cells, pole):
    where = {cell: n for n, cell in reversed(list(enumerate(coarse_cells))) if cell is not None}
    table = np.zeros((len(fine_cells), len(coarse_cells)), np.float32)
    for n, (row, col) in enumerate(fine_cells):
        for r, a in coefficient(row).items():
            if pole == "top":
                r = max(r, 0)
            if pole == "bottom":
                r = min(r, CROWS - 1)
            for c, b in coefficient(col).items():
                table[n, where[(r, c)]] += a * b
    return table


def poles(fine_cells, coarse_cells):
    return np.stack([up_table(fine_cells, coarse_cells, p) for p in ("none", "top", "bottom")])


FINE_CELLS = [(r, c) for r in range(ROWS) for c in range(COLS)]
INNER = [(r, c) for r in range(2, ROWS - 2) for c in range(2, COLS - 2)]
EARLY_COUNT = 512
EARLY_CELLS = INNER[:EARLY_COUNT]
LATE_CELLS = [cell for cell in FINE_CELLS if cell not in set(EARLY_CELLS)]
UP_EARLY = up_table(EARLY_CELLS, OWN_COARSE, "none")
UP_LATE = poles(LATE_CELLS, COARSE_KEYS)
INNER_CELLS = FINE_CELLS[EDGE:-EDGE]
UP_INNER = up_table(INNER_CELLS, COARSE_QUERIES, "none")
UP_OUTER = poles(FINE_CELLS[:EDGE] + FINE_CELLS[-EDGE:], ATT_CELLS)


def picked(indices, count):
    table = np.zeros((len(indices), count), np.float32)
    for n, index in enumerate(indices):
        if index is not None:
            table[n, index] = 1.0
    return table


FINE_EAST = [r * COLS // 2 + COLS // 2 - RADIUS + c for r in ROW_ORDER for c in range(RADIUS)]
FINE_WEST = [r * COLS // 2 + c for r in ROW_ORDER for c in range(RADIUS)]
PICK_FINE = picked(FINE_EAST + FINE_WEST, ROWS * COLS // 2)
SIDE = len(ROW_ORDER) * RADIUS


def late_picks(corner, row):
    rest = LATE_ROWS - 2 * CORNERS
    left = picked(list(corner) + [None] * (CORNERS + rest), SIDE)
    right = picked([None] * CORNERS + list(corner) + [None] * rest, SIDE)
    tables = [left, right]
    for part in range(2):
        cells = moved(late_cells(part), row)
        att = [None if cell is None else COARSE_QUERIES.index(cell) for cell in cells]
        tables.append(picked([None] * ATT_ROWS + att, len(COARSE_QUERIES)))
    return tables


LATE_PICKS = [
    np.concatenate(tables)
    for tables in zip(late_picks(CORNER_BOTTOM, CROWS - 1), late_picks(CORNER_TOP, 0))
]


PAIRS = HEADS // 2
LEAST, MOST = 2.0**-80, 2.0**100


def halves():
    return lax.broadcasted_iota(jnp.int32, (1, LANES), 1) < LANES // 2


def head_of(pair, head):
    return jnp.where(halves() == (head == 0), pair, jnp.zeros((), pair.dtype))


def packed(first, second):
    return jnp.where(halves(), first, second)


def dot(a, b):
    return jnp.dot(a, b, preferred_element_type=F32)


def scores(queries, keys):
    return lax.dot_general(queries, keys, (((1,), (1,)), ((), ())), preferred_element_type=F32)


def mix(weights, values):
    mixed = dot(weights.astype(BF16), values)
    return mixed[:, :LANES], mixed[:, LANES:]


def with_ones(values):
    return jnp.concatenate([values, jnp.ones_like(values)], 1)


def even(axis):
    return lax.axis_index(axis) % 2 == 0


def pole_flags():
    lat = lax.axis_index("lat")
    return lat == 0, lat == lax.axis_size("lat") - 1


def pole_table():
    is_top, is_bottom = pole_flags()
    return jnp.where(is_top, 1, jnp.where(is_bottom, 2, 0))


def lanes_of(group):
    if isinstance(group, int):
        return slice(group * LANES, (group + 1) * LANES)
    return pl.ds(pl.multiple_of(group * LANES, LANES), LANES)


def low(pair):
    return lanes_of(pair)


def high(pair):
    return lanes_of(pair + PAIRS)


def close_edge(mask, closed):
    lane = lax.broadcasted_iota(jnp.int32, (1, LANES), 1)
    return jnp.where((lane == LANES - 1) & closed, MASKED, mask.astype(F32)).astype(BF16)


def before_after(axis, first, second, *index):
    a, b = first[index], second[index]
    if axis == "lat":
        return a, b
    return jnp.where(even(axis), b, a), jnp.where(even(axis), a, b)


def both_heads(queries, chosen):
    rows = jnp.concatenate([head_of(queries, 0), head_of(queries, 1)], 0)
    if chosen is None:
        return rows
    return jnp.concatenate([rows, jnp.concatenate([chosen, chosen], 0)], 1)


def plain_softmax(queries, chosen, keys, values):
    count = queries.shape[0]
    mixed, total = mix(jnp.exp2(scores(both_heads(queries, chosen), keys) * EXPONENT), values)
    return packed(mixed[:count], mixed[count:]), packed(total[:count], total[count:])


def exact_softmax(queries, chosen, keys, values):
    count = queries.shape[0]
    score = scores(both_heads(queries, chosen), keys)
    score = score - jnp.max(score, 1, keepdims=True)
    mixed, total = mix(jnp.exp2(score * EXPONENT), values)
    result = mixed / total
    return packed(result[:count], result[count:])


def settled(mixed, total):
    fits = (total > LEAST) & (total < MOST)
    return jnp.where(fits, mixed / total, jnp.nan)


def fetch(moves, sems):
    copies = [pltpu.make_async_copy(a, b, sems.at[n]) for n, (a, b) in enumerate(moves)]
    for copy in copies:
        copy.start()
    for copy in copies:
        copy.wait()


def send_coarse_kernel(both_ref, c0_ref, c1_ref):
    channels = both_ref.shape[1] // 3
    n = lax.broadcasted_iota(jnp.int32, (48, CROWS * CCOLS), 0)
    cell = lax.broadcasted_iota(jnp.int32, (48, CROWS * CCOLS), 1)
    row = (n * 37) >> 8
    sides = []
    for first, col in ((1, CCOLS - 1), (0, 0)):
        keyval = (n < 42) & (cell == row * CCOLS + first + n - row * 7)
        query = (n >= 42) & (cell == (n - 42) * CCOLS + col)
        both = dot(keyval.astype(F32).astype(BF16), both_ref[:, : 2 * channels])
        query = dot(query.astype(F32).astype(BF16), both_ref[:, 2 * channels :])
        sides.append(jnp.concatenate([both[:, :channels] + query, both[:, channels:]], 1).astype(BF16))
    eastward = even("lon")
    c0_ref[...] = jnp.where(eastward, sides[0], sides[1])
    c1_ref[...] = jnp.where(eastward, sides[1], sides[0])


def send_fine_kernel(fkv_ref, pick_ref, f0_ref, f1_ref, r0_ref, r1_ref):
    cells = fkv_ref.shape[0]
    halves_of_rows = fkv_ref[...].reshape(ROWS, COLS, -1)
    east = halves_of_rows[:, COLS // 2 :].reshape(ROWS * COLS // 2, -1)
    west = halves_of_rows[:, : COLS // 2].reshape(ROWS * COLS // 2, -1)
    fine = [dot(pick_ref[:SIDE], east).astype(BF16), dot(pick_ref[SIDE:], west).astype(BF16)]
    eastward = even("lon")
    f0_ref[...] = jnp.where(eastward, fine[0], fine[1])
    f1_ref[...] = jnp.where(eastward, fine[1], fine[0])
    r0_ref[...] = fkv_ref[cells - EDGE :, :]
    r1_ref[...] = fkv_ref[:EDGE, :]


def send_band_kernel(ckv_ref, c0_ref, c1_ref, band_ref):
    left, right = before_after("lon", c0_ref, c1_ref, slice(None), slice(None))
    band_ref[0:48, :] = ckv_ref[...]
    band_ref[48:96, :] = left
    band_ref[96:144, :] = right


def send_late_kernel(f0_ref, f1_ref, att_ref, pl_ref, pr_ref, pa_ref, pb_ref, l0_ref, l1_ref):
    left, right = before_after("lon", f0_ref, f1_ref, slice(None), slice(None))
    sides = dot(pl_ref[...], left) + dot(pr_ref[...], right)
    att = jnp.concatenate([dot(pa_ref[...], att_ref[...]), dot(pb_ref[...], att_ref[...])], 1)
    late = (sides + att).astype(BF16)
    l0_ref[...], l1_ref[...] = late[:LATE_ROWS], late[LATE_ROWS:]


def own_kernel(blocks, q_ref, kv_ref, chosen_ref, mask_ref, *refs):
    mixed_ref, total_ref = refs[-2:]
    for pair in range(PAIRS):
        lo, hi = low(pair), high(pair)
        for block in blocks:
            (q0, q1), (k0, k1) = OWN_BLOCKS[block]
            rows = slice(q0 * COLS, q1 * COLS)
            near = slice(k0 * COLS, k1 * COLS)
            size = (k1 - k0) * COLS
            mask = mask_ref[block * size : (block + 1) * size, :]
            keys = jnp.concatenate([kv_ref[near, lo], mask], 1)
            mixed_ref[rows, lo], total_ref[rows, lo] = plain_softmax(
                q_ref[rows, lo], chosen_ref[rows, :], keys, with_ones(kv_ref[near, hi])
            )


CROSS_ROWS = 768


def raise_pair(table, keys, values):
    both = dot(table, jnp.concatenate([keys, values], 1)).astype(BF16)
    return both[:, :LANES], with_ones(both[:, LANES:])


def early_cross_kernel(q_ref, ckv_ref, up_ref, mixed_ref, total_ref):
    up = up_ref[...]
    raised = [raise_pair(up, ckv_ref[:, low(pair)], ckv_ref[:, high(pair)]) for pair in range(PAIRS)]
    for pair in range(PAIRS):
        lo = low(pair)
        up_keys, up_values = raised[pair]
        for first in range(0, q_ref.shape[0], CROSS_ROWS):
            rows = slice(first, first + CROSS_ROWS)
            mixed_ref[rows, lo], total_ref[rows, lo] = plain_softmax(
                q_ref[rows, lo], None, up_keys, up_values
            )


def columns(queries, first):
    rows = queries.shape[0] // COLS
    split = queries.astype(F32).reshape(rows, COLS, LANES)[:, first : first + GROUP]
    return split.reshape(rows * GROUP, LANES).astype(BF16)


def lon_kernel(q_ref, f0_ref, f1_ref, chosen_ref, mask_ref, om_ref, ot_ref, mixed_ref, total_ref):
    strip = ROWS * GROUP
    for pair in range(PAIRS):
        lo, hi = low(pair), high(pair)
        keys = before_after("lon", f0_ref, f1_ref, slice(None), lo)
        values = before_after("lon", f0_ref, f1_ref, slice(None), hi)
        queries = q_ref[:, lo]
        for n, first in enumerate((0, COLS - GROUP)):
            mixed, total = plain_softmax(
                columns(queries, first),
                chosen_ref[n * strip : (n + 1) * strip, :],
                jnp.concatenate([keys[n], mask_ref[n * SIDE : (n + 1) * SIDE, :]], 1),
                with_ones(values[n]),
            )
            for row in range(ROWS):
                at = slice(row * COLS + first, row * COLS + first + GROUP)
                piece = slice(row * GROUP, (row + 1) * GROUP)
                mixed_ref[at, lo] = om_ref[at, lo] + mixed[piece]
                total_ref[at, lo] = ot_ref[at, lo] + total[piece]


def lat_kernel(q_ref, r0_ref, r1_ref, chosen_ref, mask_ref, om_ref, ot_ref, mixed_ref, total_ref):
    cells = q_ref.shape[0]
    closed = pole_flags()
    masks = [close_edge(mask_ref[n * EDGE : (n + 1) * EDGE, :], closed[n]) for n in range(2)]
    for pair in range(PAIRS):
        lo, hi = low(pair), high(pair)
        keys = before_after("lat", r0_ref, r1_ref, slice(None), lo)
        values = before_after("lat", r0_ref, r1_ref, slice(None), hi)
        for n, first in enumerate((0, cells - EDGE)):
            rows = slice(first, first + EDGE)
            mixed, total = plain_softmax(
                q_ref[rows, lo],
                chosen_ref[n * EDGE : (n + 1) * EDGE, :],
                jnp.concatenate([keys[n], masks[n]], 1),
                with_ones(values[n]),
            )
            mixed_ref[rows, lo] = om_ref[rows, lo] + mixed
            total_ref[rows, lo] = ot_ref[rows, lo] + total


def gathered(own, coarse, band, lanes):
    left, right = before_after("lon", *coarse, slice(None), lanes)
    top, bottom = before_after("lat", *band, slice(None), lanes)
    pad = jnp.zeros((COARSE_COUNT - 3 * len(BAND), LANES), BF16)
    return jnp.concatenate([own[:, lanes], left, right, top, bottom, pad], 0)


def coarse_kernel(q_ref, own_ref, c0_ref, c1_ref, b0_ref, b1_ref, chosen_ref, mask_ref, out_ref):
    is_top, is_bottom = pole_flags()
    band = len(BAND)
    mask = [
        mask_ref[:band, :],
        close_edge(mask_ref[band : 2 * band, :], is_top),
        close_edge(mask_ref[2 * band :, :], is_bottom),
    ]
    mask = jnp.concatenate(mask, 0)
    chosen = chosen_ref[...]
    for pair in range(PAIRS):
        lo = slice(pair * LANES, (pair + 1) * LANES)
        hi = slice((pair + PAIRS) * LANES, (pair + PAIRS + 1) * LANES)
        keys = jnp.concatenate([gathered(own_ref, (c0_ref, c1_ref), (b0_ref, b1_ref), lo), mask], 1)
        values = with_ones(gathered(own_ref, (c0_ref, c1_ref), (b0_ref, b1_ref), hi))
        left, right = before_after("lon", c0_ref, c1_ref, slice(32, 48), lo)
        queries = jnp.concatenate([q_ref[:, lo], left, right], 0)
        out_ref[:, lo] = exact_softmax(queries, chosen, keys, values).astype(BF16)


def late_cross_kernel(q_ref, oc_ref, lc_ref, ckv_ref, c0_ref, c1_ref, b0_ref, b1_ref, late_ref, cross_ref):
    late = late_ref[pole_table()]
    coarse = (ckv_ref, (c0_ref, c1_ref), (b0_ref, b1_ref))
    raised = [
        raise_pair(late, gathered(*coarse, low(pair)), gathered(*coarse, high(pair))) for pair in range(PAIRS)
    ]
    for pair in range(PAIRS):
        lo = low(pair)
        up_keys, up_values = raised[pair]
        for first in range(0, q_ref.shape[0], CROSS_ROWS):
            rows = slice(first, first + CROSS_ROWS)
            mixed, total = plain_softmax(q_ref[rows, lo], None, up_keys, up_values)
            cross_ref[rows, lo] = settled(oc_ref[rows, lo] + mixed, lc_ref[rows, lo] + total)


def join(mixed, total, cross, raised):
    fine = settled(mixed, total).astype(BF16).astype(F32)
    joined = fine + cross + raised
    return joined.astype(BF16), jnp.sum(joined.reshape(-1, 8, LANES) * 0.0, 0)


def inner_kernel(mixed_ref, total_ref, cross_ref, att_ref, up_ref, weight_ref, out_ref, bad_ref):
    rows = slice(EDGE, mixed_ref.shape[0] - EDGE)
    raised = dot(up_ref[...], att_ref[...])
    parts = [
        join(mixed_ref[rows, low(n)], total_ref[rows, low(n)], cross_ref[rows, low(n)], raised[:, low(n)])
        for n in range(PAIRS)
    ]
    bad_ref[...] = sum(bad for _, bad in parts)
    joined = jnp.concatenate([piece for piece, _ in parts], 1)
    out_ref[...] = dot(joined, weight_ref[...]).astype(BF16)


def lon_inner_kernel(
    q_ref, f0_ref, f1_ref, chosen_ref, mask_ref, om_ref, ot_ref, cross_ref, att_ref, up_ref, weight_ref,
    mixed_ref, total_ref, out_ref, bad_ref,
):
    lon_kernel(q_ref, f0_ref, f1_ref, chosen_ref, mask_ref, om_ref, ot_ref, mixed_ref, total_ref)
    inner_kernel(mixed_ref, total_ref, cross_ref, att_ref, up_ref, weight_ref, out_ref, bad_ref)


def late_kernel(
    q_ref, mixed_ref, total_ref, cross_ref, l0_ref, l1_ref, att_ref,
    chosen_ref, mask_ref, up_ref, weight_ref, inner_ref, inner_bad_ref,
    kv_hbm, f0_ref, f1_ref, r0_ref, r1_ref, ckv_ref, c0_ref, c1_ref, b0_ref, b1_ref,
    exact_chosen_hbm, exact_mask_hbm, early_hbm, late_hbm, up_inner_hbm,
    out_ref, joined_ref, bad_ref,
    kv_ref, exact_chosen_ref, exact_mask_ref, early_ref, late_ref, up_inner_ref, sems,
):
    cells = q_ref.shape[0]
    closed = pole_flags()
    pole = pole_table()
    up = up_ref[pole]
    mask = [close_edge(mask_ref[n * LATE_ROWS : (n + 1) * LATE_ROWS, :], closed[n]) for n in range(2)]
    mask = jnp.concatenate(mask, 0)
    corner = RADIUS * GROUP
    bad = inner_bad_ref[...]

    def raised_att(group, count):
        lanes = [slice((n + group) * LANES, (n + group + count) * LANES) for n in (0, PAIRS)]
        if count == 1:
            lanes = [low(group), high(group)]
        tops, bottoms = zip(*[before_after("lat", l0_ref, l1_ref, slice(ATT_ROWS, None), at) for at in lanes])
        return dot(up, jnp.concatenate([att_ref[:, lanes[0]], *tops, *bottoms], 0))

    def cornered(sums, part):
        west, east = part[:corner].reshape(-1, GROUP, LANES), part[corner:].reshape(-1, GROUP, LANES)
        rows = sums.reshape(-1, COLS, LANES)
        rows = jnp.concatenate(
            [rows[:, :GROUP] + west, rows[:, GROUP : COLS - GROUP], rows[:, COLS - GROUP :] + east], 1
        )
        return rows.reshape(-1, LANES)

    raised = [raised_att(pair, 2) for pair in range(0, PAIRS, 2)]
    parts = []
    for pair in range(PAIRS):
        lo, hi = low(pair), high(pair)
        corner_keys = before_after("lat", l0_ref, l1_ref, slice(None), lo)
        corner_values = before_after("lat", l0_ref, l1_ref, slice(None), hi)
        lift = raised[pair // 2][:, pair % 2 * LANES : (pair % 2 + 1) * LANES]
        outer = [slice(0, EDGE), slice(cells - EDGE, cells)]
        queries = [columns(q_ref[rows, lo], first) for rows in outer for first in (0, COLS - GROUP)]
        keys = jnp.concatenate([jnp.concatenate(corner_keys, 0), mask], 1)
        values = with_ones(jnp.concatenate(corner_values, 0))
        mixed, total = plain_softmax(jnp.concatenate(queries, 0), chosen_ref[...], keys, values)
        pieces = []
        for n, rows in enumerate(outer):
            at = slice(2 * n * corner, 2 * (n + 1) * corner)
            piece, wrong = join(
                cornered(mixed_ref[rows, lo], mixed[at]),
                cornered(total_ref[rows, lo], total[at]),
                cross_ref[rows, lo],
                lift[n * EDGE : (n + 1) * EDGE],
            )
            pieces.append(piece)
            bad += wrong
        parts.append(jnp.concatenate(pieces, 0))
    bad_ref[...] = bad
    outer = dot(jnp.concatenate(parts, 1), weight_ref[...]).astype(BF16)
    out_ref[:EDGE, :] = outer[:EDGE]
    out_ref[EDGE : cells - EDGE, :] = inner_ref[...]
    out_ref[cells - EDGE :, :] = outer[EDGE:]

    @pl.when(jnp.logical_not(jnp.sum(bad_ref[...]) == 0.0))
    def _():
        fetch(
            [(kv_hbm, kv_ref), (exact_chosen_hbm, exact_chosen_ref), (exact_mask_hbm, exact_mask_ref),
             (early_hbm, early_ref), (late_hbm, late_ref), (up_inner_hbm, up_inner_ref)],
            sems,
        )
        coarse = (ckv_ref, (c0_ref, c1_ref), (b0_ref, b1_ref))
        early, late = early_ref[...], late_ref[pole]
        count = len(EXACT_KEYS)
        edges = [cells + 2 * SIDE, cells + 2 * SIDE + EDGE + LATE_ROWS, count]

        @pl.loop(0, PAIRS)
        def _(pair):
            def all_of(lanes):
                left, right = before_after("lon", f0_ref, f1_ref, slice(None), lanes)
                top, bottom = before_after("lat", r0_ref, r1_ref, slice(None), lanes)
                late_top, late_bottom = before_after("lat", l0_ref, l1_ref, slice(None), lanes)
                return jnp.concatenate(
                    [kv_ref[:, lanes], left, right, top, late_top, bottom, late_bottom], 0
                )

            def up_of(lanes):
                first = dot(early, ckv_ref[:, lanes]).astype(BF16)
                return jnp.concatenate([first, dot(late, gathered(*coarse, lanes)).astype(BF16)], 0)

            lo, hi = low(pair), high(pair)
            keys, values = all_of(lo), with_ones(all_of(hi))
            up_keys, up_values = up_of(lo), with_ones(up_of(hi))
            outer, inner = raised_att(pair, 1), dot(up_inner_ref[...], att_ref[:, lo])
            raised = jnp.concatenate([outer[:EDGE], inner, outer[EDGE:]], 0)
            for block in range(BLOCKS):
                mask = exact_mask_ref[block * count : (block + 1) * count, :]
                mask = [mask[: edges[0]]] + [
                    close_edge(mask[edges[n] : edges[n + 1]], closed[n]) for n in range(2)
                ]
                rows = slice(block * BLOCK, (block + 1) * BLOCK)
                queries = q_ref[rows, lo]
                fine = exact_softmax(
                    queries,
                    exact_chosen_ref[rows, :],
                    jnp.concatenate([keys, jnp.concatenate(mask, 0)], 1),
                    values,
                )
                cross = exact_softmax(queries, None, up_keys, up_values)
                joined = fine.astype(BF16).astype(F32) + cross + raised[rows, :]
                joined_ref[pair, rows, :] = joined.astype(BF16)

        joined = jnp.concatenate([joined_ref[n] for n in range(PAIRS)], 1)
        out_ref[...] = dot(joined, weight_ref[...]).astype(BF16)


def constant(table):
    return jnp.asarray(table, BF16)


def call(kernel, name, outs, operands, flops, hbm=(), scratch=(), vmem=28, aliases={}):
    near = pl.BlockSpec(memory_space=pltpu.VMEM)
    far = pl.BlockSpec(memory_space=pltpu.HBM)
    moved_bytes = sum(x.size * x.dtype.itemsize for x in list(operands) + list(outs))
    return pl.pallas_call(
        kernel,
        in_specs=[far if n in hbm else near for n in range(len(operands))],
        out_specs=[near] * len(outs),
        out_shape=list(outs),
        scratch_shapes=list(scratch),
        input_output_aliases=dict(aliases),
        compiler_params=pltpu.CompilerParams(vmem_limit_bytes=vmem << 20),
        cost_estimate=pl.CostEstimate(
            flops=int(flops), bytes_accessed=int(moved_bytes if flops > 1e9 else moved_bytes // 16), transcendentals=int(flops / 1000)
        ),
        name=name,
    )(*operands)


def swap(array, above):
    size = lax.axis_size("lon")
    pairs = [(i, (i + 1) % size) for i in range(0 if above else 1, size, 2)]
    return lax.ppermute(array, "lon", pairs + [(b, a) for a, b in pairs])


def shift(array, step):
    size = lax.axis_size("lat")
    return lax.ppermute(array, "lat", [(i, (i + step) % size) for i in range(size)])


def ring(southward, northward):
    return shift(southward, 1), shift(northward, -1)


def shards(fine_query, fine_keyval, coarse_query, coarse_keyval, out_weight):
    channels = fine_query.shape[-1]
    cells = ROWS * COLS
    fq = fine_query.reshape(cells, channels)
    fkv = fine_keyval.reshape(cells, 2 * channels)
    cq = coarse_query.reshape(-1, channels)
    ckv = coarse_keyval.reshape(-1, 2 * channels)
    half = lambda rows: jax.ShapeDtypeStruct((rows, channels), BF16)
    full = lambda rows: jax.ShapeDtypeStruct((rows, 2 * channels), BF16)
    state = lambda rows: jax.ShapeDtypeStruct((rows, channels), F32)
    after = lax.optimization_barrier

    c0, c1 = call(
        send_coarse_kernel, "send_coarse", [full(48)] * 2, [jnp.concatenate([ckv, cq], 1)], 1e10, vmem=8
    )
    coarse0, coarse1 = swap(c0, True), swap(c1, False)
    near_kv, _ = after((fkv, c0))
    f0, f1, r0, r1 = call(
        send_fine_kernel, "send_fine", [full(SIDE)] * 2 + [full(EDGE)] * 2, [near_kv, constant(PICK_FINE)], 5e9
    )
    edge1 = shift(r1, -1)
    side0 = swap(f0, True)
    own_tables = [constant(OWN_CHOSEN), constant(OWN_MASK)]
    fq, near_kv, _ = after((fq, near_kv, f0))
    own = call(
        functools.partial(own_kernel, (0,)), "own_first", [state(cells)] * 2, [fq, near_kv, *own_tables], 2e9
    )
    f1, coarse0, coarse1, r1, own = after((f1, coarse0, coarse1, r1, own))
    coarse = (coarse0, coarse1)
    sides = (side0, swap(f1, False))
    ckv, _ = after((ckv, f1))
    (band,) = call(send_band_kernel, "send_band", [full(len(BAND))], [ckv, *coarse], 1e6)
    bands = ring(band, band)
    fq, near_kv, _ = after((fq, near_kv, band))
    own = call(
        functools.partial(own_kernel, (1, 2)), "own", [state(cells)] * 2, [fq, near_kv, *own_tables, *own], 3e9,
        aliases={4: 0, 5: 1},
    )
    fq, own = after((fq, own))
    early = call(early_cross_kernel, "early_cross", [state(cells)] * 2, [fq, ckv, constant(UP_EARLY)], 5e9)
    bands, early, r0 = after((bands, early, r0))
    edges = (shift(r0, 1), edge1)
    (coarse_att,) = call(
        coarse_kernel, "coarse", [half(len(COARSE_QUERIES))],
        [cq, ckv, *coarse, *bands, constant(COARSE_CHOSEN), constant(COARSE_MASK)], 2e9,
    )
    late0, late1 = call(
        send_late_kernel, "send_late", [full(LATE_ROWS)] * 2,
        [*sides, coarse_att] + [constant(table) for table in LATE_PICKS], 2e8,
    )
    lates = ring(late0, late1)
    fq, _ = after((fq, late0))
    (cross,) = call(
        late_cross_kernel, "late_cross", [state(cells)], [fq, *early, ckv, *coarse, *bands, constant(UP_LATE)], 1e8
    )
    fq, cross = after((fq, cross))
    *sums, inner, inner_bad = call(
        lon_inner_kernel, "lon_inner",
        [state(cells)] * 2 + [half(cells - 2 * EDGE), jax.ShapeDtypeStruct((8, LANES), F32)],
        [fq, *sides, constant(LON_CHOSEN), constant(LON_MASK), *own, cross, coarse_att, constant(UP_INNER), out_weight],
        1e8, aliases={5: 0, 6: 1},
    )
    fq, sums, _ = after((fq, sums, inner))
    sums = call(
        lat_kernel, "lat_strips", [state(cells)] * 2,
        [fq, *edges, constant(LAT_CHOSEN), constant(LAT_MASK), *sums], 1e8, aliases={5: 0, 6: 1},
    )
    exact = [constant(table) for table in (EXACT_CHOSEN, EXACT_MASK, UP_EARLY, UP_LATE, UP_INNER)]
    (out,) = call(
        late_kernel, "late", [half(cells)],
        [fq, *sums, cross, *lates, coarse_att, constant(CORNER_CHOSEN),
         constant(CORNER_MASK), constant(UP_OUTER), out_weight, inner, inner_bad,
         near_kv, *sides, *edges, ckv, *coarse, *bands, *exact],
        3e9,
        hbm=(13, 23, 24, 25, 26, 27),
        scratch=[
            pltpu.VMEM((PAIRS, cells, LANES), BF16), pltpu.VMEM((8, LANES), F32),
            pltpu.VMEM((cells, 2 * channels), BF16),
            *[pltpu.VMEM(x.shape, BF16) for x in exact], pltpu.SemaphoreType.DMA((6,)),
        ],
    )
    return out.reshape(ROWS, COLS, channels)


def solution(mesh):
    tiled = P("lat", "lon", None)
    return jax.shard_map(
        shards, mesh=mesh, in_specs=(tiled,) * 4 + (P(),), out_specs=tiled, check_vma=False
    )
```
